128 devices in a mesh: seq: 8 (over x_lo, y), dp: 16 (over z, x_hi, core).
Axes of the slice: x: 4 (x_hi: 2, x_lo: 2; x = x_hi * 2 + x_lo), y: 4, z: 4, core: 2. Of those that a mesh axis runs over, the one named last changes fastest.
Arguments:
- tokens: bfloat16 [16, 1024, 2048], P('dp', 'seq'), may hold values from -6 to 6
- valid_counts: int32 [16, 8], P('dp', 'seq'), may hold values from 32 to 128, as said below
- block_owner: int32 [16, 8], P('dp'), may hold values from 0 to 7, each once within a row
- norm1_gain: bfloat16 [2048], P(('seq', 'dp')), may hold values from 0.099609375 to 1.8984375
- attn_weight: bfloat16 [2048, 4, 2048], P(('seq', 'dp'))
- norm2_gain: bfloat16 [2048], P(('seq', 'dp')), may hold values from 0.099609375 to 1.8984375
- mlp_weight: bfloat16 [2048, 3, 5504], P(('seq', 'dp')), may hold values from -0.125 to 0.125
- cotangent: bfloat16 [16, 1024, 2048], P('dp', 'seq'), may hold values from -6 to 6
Outputs:
- layer_out: bfloat16 [16, 1024, 2048], P('dp', 'seq')
- input_grad: float32 [16, 1024, 2048], P('dp', 'seq')
- norm1_grad: float32 [2048], P(('seq', 'dp'))
- attn_grad: float32 [2048, 4, 2048], P(('seq', 'dp'))
- norm2_grad: float32 [2048], P(('seq', 'dp'))
- mlp_grad: float32 [2048, 3, 5504], P(('seq', 'dp'))
The draws below stay inside these ranges and needn't reach their ends.
Inputs may be any that keep to these rules, and one draw needn't show every extreme that they name: Device i of sequence s holds 128 tokens, of which the first valid_counts[s, i] are real and the rest padding; in every sequence some device holds no padding. block_owner[s, i] is the place, in blocks of 128 tokens, of the block held by device i of sequence s; each row names every block once.
All inputs are finite; a program needn't handle non-finite values.
Results may differ from the reference program's by a relative error of at most 0.02.
Values may be sent and summed in bfloat16 or wider, within the bound.
A program may use at most 704 MiB of HBM per device.

```python
import math
import jax
import jax.numpy as jnp
from jax import lax

D = 2048
HEADS = 16
HEAD_DIM = 128
FF = 5504
SEQ_LEN = 1024
ROWS = 128
SEQS = 16
N_SEQ = 8


def draw_valid_counts(key, part):
    key = jax.random.fold_in(key, 3)
    first, second = jax.random.split(key)
    base = jax.random.randint(first, (SEQS, N_SEQ), ROWS // 4, ROWS + 1, dtype=jnp.int32)
    full = jax.random.randint(second, (SEQS, 1), 0, N_SEQ, dtype=jnp.int32)
    slots = jnp.arange(N_SEQ, dtype=jnp.int32)[None, :]
    return jnp.where(slots == full, ROWS, base).astype(jnp.int32)


def draw_attn_weight(key, part):
    key = jax.random.fold_in(key, 7)
    slot = jnp.arange(4)[None, :, None]
    spread = jnp.where(slot == 3, float(max(1, 4 * D // SEQ_LEN)) ** (-0.5), float(D) ** (-0.5))
    base = jax.random.truncated_normal(key, -4.0, 4.0, (D, 4, D), jnp.float32)
    return (base * spread).astype(jnp.bfloat16)


def block_levels(own_key, dims, shards, least, largest):
    loudness, own = 1.0, jax.random.fold_in(own_key, 6)
    for dim, parts in shards:
        heights = jnp.exp(jax.random.uniform(jax.random.fold_in(own, dim), (parts,), jnp.float32, least / len(shards), largest / len(shards)))
        loudness = loudness * jnp.repeat(heights, dims[dim] // parts).reshape([-1 if axis == dim else 1 for axis in range(len(dims))])
    return loudness


def noise(stream_key, extent, scale, limit, cuts=(), kind=jnp.bfloat16):
    entries = jax.random.normal(stream_key, extent, jnp.float32) * scale
    if len(cuts) > 0:
        entries = block_levels(stream_key, extent, cuts, -0.22, 0.18) * entries
    return jnp.clip(entries, min=-limit, max=limit).astype(kind)


def setup_inputs(seed: int = 0) -> dict:
    keys = jax.random.split(jax.random.key(seed), 9)
    return {
        "tokens": noise(keys[0], (SEQS, SEQ_LEN, D), 1.0, 6.0, ((0, 16), (1, 8))),
        "valid_counts": draw_valid_counts(jax.random.fold_in(keys[8], 71), 0),
        "block_owner": jax.vmap(lambda own: jax.random.permutation(own, N_SEQ))(jax.random.split(keys[2], SEQS)).reshape((SEQS, N_SEQ)).astype(jnp.int32),
        "norm1_gain": jnp.clip(1.0 + 0.18 * jax.random.normal(keys[3], (D,), jnp.float32), 0.099609375, 1.8984375).astype(jnp.bfloat16),
        "attn_weight": draw_attn_weight(jax.random.fold_in(keys[8], 71), 0),
        "norm2_gain": jnp.clip(1.0 + 0.18 * jax.random.normal(keys[5], (D,), jnp.float32), 0.099609375, 1.8984375).astype(jnp.bfloat16),
        "mlp_weight": noise(keys[6], (D, 3, FF), D ** -0.5, 0.125, ((0, 128),)),
        "cotangent": noise(keys[7], (SEQS, SEQ_LEN, D), 1.0, 6.0, ((0, 16), (1, 8))),
    }


@jax.custom_vjp
def low(v):
    return lax.optimization_barrier(v.astype(jnp.bfloat16)).astype(jnp.float32)

@jax.custom_vjp
def low_back(v):
    return v

def low_keep(v):
    return (low(v), None)

def low_pass(kept, grad):
    return (grad,)

def back_keep(v):
    return (v, None)

def back_low(kept, grad):
    return (low(grad),)
low.defvjp(low_keep, low_pass)
low_back.defvjp(back_keep, back_low)
EPS = 1e-05
HIGH = lax.Precision.HIGHEST

def norm_rows(values, gain):
    scale = lax.rsqrt(lax.optimization_barrier(jnp.mean(values * values, axis=-1, keepdims=True)) + EPS)
    return values * scale * gain[None, :]

def one_sequence(gain_one, attn_w, gain_two, mlp_w, inputs, counts, owners):
    index = jnp.arange(SEQ_LEN, dtype=jnp.int32)
    shard = index // ROWS
    within = index % ROWS
    positions = owners[shard] * ROWS + within
    live_rows = within < counts[shard]
    normed_one = low(norm_rows(inputs, gain_one))
    projected = jnp.einsum('tc,cjd->tjd', normed_one, attn_w[:, :3, :], precision=HIGH)
    projected = low(low_back(projected))
    queries = projected[:, 0].reshape(SEQ_LEN, HEADS, HEAD_DIM)
    key_heads = projected[:, 1].reshape(SEQ_LEN, HEADS, HEAD_DIM)
    value_heads = projected[:, 2].reshape(SEQ_LEN, HEADS, HEAD_DIM)
    scores = jnp.einsum('qhd,khd->hqk', queries, key_heads, precision=HIGH)
    scores = low_back(scores * (1.0 / math.sqrt(HEAD_DIM)) - math.log(SEQ_LEN))
    allowed = (positions[None, :] <= positions[:, None]) & live_rows[None, :]
    weights = low(jnp.where(allowed[None], jax.nn.sigmoid(scores), 0.0))
    attended = jnp.einsum('hqk,khd->qhd', weights, value_heads, precision=HIGH).reshape(SEQ_LEN, D)
    attended = low(low_back(attended))
    branch = low_back(jnp.dot(attended, attn_w[:, 3, :], precision=HIGH))
    resid = inputs + branch
    normed_two = low(norm_rows(resid, gain_two))
    gate_up = low_back(jnp.einsum('tc,cjf->tjf', normed_two, mlp_w[:, :2, :], precision=HIGH))
    hidden = low(jax.nn.silu(gate_up[:, 0]) * gate_up[:, 1])
    branch_two = low_back(jnp.einsum('tf,cf->tc', hidden, mlp_w[:, 2, :], precision=HIGH))
    return live_rows.astype(jnp.float32)[:, None] * (resid + branch_two)

def reference(tokens, valid_counts, block_owner, norm1_gain, attn_weight, norm2_gain, mlp_weight, cotangent):

    def forward(inputs, gain_one, attn_w, gain_two, mlp_w):

        def step(pieces):
            return one_sequence(gain_one, attn_w, gain_two, mlp_w, pieces[0], pieces[1], pieces[2])
        return lax.map(jax.checkpoint(step), (inputs, valid_counts, block_owner))
    primals = (tokens.astype(jnp.float32), norm1_gain.astype(jnp.float32), attn_weight.astype(jnp.float32), norm2_gain.astype(jnp.float32), mlp_weight.astype(jnp.float32))
    output, pullback = jax.vjp(forward, *primals)
    grads = pullback(cotangent.astype(jnp.float32))
    return (output.astype(jnp.bfloat16), grads[0], grads[1], grads[2], grads[3], grads[4])
```

```python
import math

import jax
import jax.numpy as jnp
from jax import lax
from jax.sharding import PartitionSpec as P

HEAD_DIM = 128
EPS = 1e-05
LOW = jnp.bfloat16
WIDE = jnp.float32


def dot(a, b, dims):
    return lax.dot_general(a, b, (dims, ((), ())), preferred_element_type=WIDE)


def norm_scale(values):
    return lax.rsqrt(jnp.mean(values * values, axis=-1, keepdims=True) + EPS)


def norm_back(grad_hat, normed, scale):
    inner = jnp.mean(grad_hat * normed, axis=-1, keepdims=True)
    return scale * (grad_hat - normed * inner)


def gather_tokens(rows):
    return lax.all_gather(rows, "seq", axis=0, tiled=True)


def scatter_tokens(partial):
    return lax.psum_scatter(partial.astype(LOW), "seq", scatter_dimension=0, tiled=True).astype(WIDE)


def columns_in(rows):
    count, slots, width = rows.shape
    seq, dp = lax.axis_size("seq"), lax.axis_size("dp")
    cut = rows.reshape(count, slots, seq, width // seq)
    mine = lax.all_to_all(cut, "seq", split_axis=2, concat_axis=0, tiled=True)[:, :, 0]
    mine = mine.reshape(seq, count, slots, width // seq)
    whole = lax.all_gather(mine, "dp", axis=0)
    return whole.transpose(1, 0, 2, 3, 4).reshape(seq * dp * count, slots, width // seq)


def columns_out(grads):
    rows, slots, part = grads.shape
    seq, dp = lax.axis_size("seq"), lax.axis_size("dp")
    count = rows // (seq * dp)
    cut = grads.astype(LOW).reshape(seq, dp, count, slots, part).transpose(1, 0, 2, 3, 4)
    mine = lax.psum_scatter(cut, "dp", scatter_dimension=0)
    mine = lax.all_to_all(mine, "seq", split_axis=0, concat_axis=0, tiled=True)
    return mine.transpose(1, 2, 0, 3).reshape(count, slots, seq * part).astype(WIDE)


def local(
    tokens, valid_counts, block_owner, norm1_gain, attn_weight, norm2_gain, mlp_weight, cotangent
):
    rows, model = tokens.shape[1], tokens.shape[2]
    seq = lax.axis_size("seq")
    length = rows * seq
    score_bias = -math.log(length)
    head_scale = 1.0 / math.sqrt(HEAD_DIM)
    heads = model // HEAD_DIM // seq
    live = (jnp.arange(rows, dtype=jnp.int32) < valid_counts[0, 0]).astype(WIDE)[:, None]
    inputs = tokens[0].astype(WIDE)
    grad_out = cotangent[0].astype(WIDE) * live
    gain_one = norm1_gain.astype(WIDE)[:, None, None]
    gain_two = norm2_gain.astype(WIDE)[:, None, None]

    w_in = columns_in((attn_weight[:, :3].astype(WIDE) * gain_one).astype(LOW))
    w_out = lax.all_gather(attn_weight[:, 3], "dp", axis=0, tiled=True)
    m_in = columns_in(
        jnp.concatenate(
            [(mlp_weight[:, :2].astype(WIDE) * gain_two).astype(LOW), mlp_weight[:, 2:]], axis=1
        )
    )
    m_pair, m_down = m_in[:, :2], m_in[:, 2]
    units = m_down.shape[1]

    scale_one = norm_scale(inputs)
    hat_one = inputs * scale_one
    all_one = gather_tokens((hat_one * live).astype(LOW))
    all_grad = gather_tokens(grad_out.astype(LOW))

    w_flat = w_in.reshape(model, -1)
    proj = dot(all_one, w_flat, ((1,), (0,))).astype(LOW).reshape(length, 3, heads, HEAD_DIM)
    q, k, v = proj[:, 0], proj[:, 1], proj[:, 2]
    pos = (block_owner[0][:, None] * rows + jnp.arange(rows, dtype=jnp.int32)[None]).reshape(-1)
    allowed = (pos[None, :] <= pos[:, None])[None]

    def probabilities():
        scores = jnp.einsum("qhd,khd->hqk", q, k, preferred_element_type=WIDE)
        return jnp.where(allowed, jax.nn.sigmoid(scores * head_scale + score_bias), 0.0)

    probs = probabilities()
    weights = probs.astype(LOW)
    attended = jnp.einsum("hqk,khd->qhd", weights, v, preferred_element_type=WIDE)
    attended = attended.astype(LOW).reshape(length, heads * HEAD_DIM)
    resid = inputs + scatter_tokens(dot(attended, w_out, ((1,), (0,))))

    scale_two = norm_scale(resid)
    hat_two = resid * scale_two
    all_two = gather_tokens((hat_two * live).astype(LOW))
    m_flat = m_pair.reshape(model, 2 * units)
    gate_up = dot(all_two, m_flat, ((1,), (0,)))
    gate_act, up_act = gate_up[:, :units], gate_up[:, units:]
    squashed = jax.nn.sigmoid(gate_act)
    activated = gate_act * squashed
    hidden = (activated * up_act).astype(LOW)
    grad_hidden = dot(all_grad, m_down, ((1,), (0,)))
    slope = squashed * (1.0 + gate_act * (1.0 - squashed))
    grad_pair = jnp.concatenate(
        [(grad_hidden * up_act * slope).astype(LOW), (grad_hidden * activated).astype(LOW)], axis=1
    )
    e_two = scatter_tokens(dot(grad_pair, m_flat, ((1,), (1,))))
    grad_resid = grad_out + norm_back(e_two, hat_two, scale_two)
    all_branch = gather_tokens(grad_resid.astype(LOW))

    branch_two = scatter_tokens(dot(hidden, m_down, ((1,), (1,))))
    layer_out = (live * (resid + branch_two)).astype(LOW)
    mlp_terms = jnp.concatenate(
        [
            dot(all_two, grad_pair, ((0,), (0,))).reshape(model, 2, units),
            dot(all_grad, hidden, ((0,), (0,)))[:, None],
        ],
        axis=1,
    )
    mlp_sum = columns_out(mlp_terms)

    g_att = dot(all_branch, w_out, ((1,), (1,))).astype(LOW).reshape(length, heads, HEAD_DIM)
    grad_v = jnp.einsum("hqk,qhd->khd", weights, g_att, preferred_element_type=WIDE)
    grad_w = jnp.einsum("qhd,khd->hqk", g_att, v, preferred_element_type=WIDE)
    grad_s = (grad_w * probs * (1.0 - probs)).astype(LOW)
    grad_k = jnp.einsum("hqk,qhd->khd", grad_s, q, preferred_element_type=WIDE) * head_scale
    grad_q = jnp.einsum("hqk,khd->qhd", grad_s, k, preferred_element_type=WIDE) * head_scale
    grad_proj = jnp.stack([grad_q, grad_k, grad_v], axis=1).astype(LOW)
    grad_proj = grad_proj.reshape(length, 3 * heads * HEAD_DIM)
    e_one = scatter_tokens(dot(grad_proj, w_flat, ((1,), (1,))))
    input_grad = grad_resid + live * norm_back(e_one, hat_one, scale_one)

    in_terms = dot(all_one, grad_proj, ((0,), (0,))).reshape(model, 3, heads * HEAD_DIM)
    in_sum = columns_out(in_terms)
    out_terms = dot(attended, all_branch, ((0,), (0,))).astype(LOW)
    out_sum = lax.psum_scatter(out_terms, "dp", scatter_dimension=0, tiled=True).astype(WIDE)
    attn_grad = jnp.concatenate([in_sum * gain_one, out_sum[:, None]], axis=1)
    mlp_grad = jnp.concatenate([mlp_sum[:, :2] * gain_two, mlp_sum[:, 2:]], axis=1)
    gain_one_grad = jnp.sum(in_sum * attn_weight[:, :3].astype(WIDE), axis=(1, 2))
    gain_two_grad = jnp.sum(mlp_sum[:, :2] * mlp_weight[:, :2].astype(WIDE), axis=(1, 2))
    return (layer_out[None], input_grad[None], gain_one_grad, attn_grad, gain_two_grad, mlp_grad)


def solution(mesh):
    token_spec = P("dp", "seq", None)
    row_spec = P(("seq", "dp"), None, None)
    gain_spec = P(("seq", "dp"))
    in_specs = (
        token_spec, P("dp", "seq"), P("dp", None), gain_spec, row_spec, gain_spec, row_spec, token_spec
    )
    out_specs = (token_spec, token_spec, gain_spec, row_spec, gain_spec, row_spec)
    return jax.shard_map(local, mesh=mesh, in_specs=in_specs, out_specs=out_specs, check_vma=False)
```

```python
import functools, math
import jax
import jax.numpy as jnp
from jax import lax
from jax.experimental import pallas as pl
from jax.experimental.pallas import tpu as pltpu
from jax.sharding import PartitionSpec as P

LOW = jnp.bfloat16
WIDE = jnp.float32
MESH = pl.DeviceIdType.MESH
EPS = 1e-05
HEAD_DIM = 128
ROWS = 128
MODEL = 2048
PART = 256
PROJ = 3 * PART
UNITS = 1408
SLAB = 3 * UNITS
PAIR = 2 * UNITS
FIRST = 80
MID = MODEL // 2


class Place:
    def __init__(self):
        self.seq, self.dp = lax.axis_index("seq"), lax.axis_index("dp")
        self.a, self.y = self.seq // 4, self.seq % 4
        self.b = 1 - self.a
        self.up, self.down, self.far = (self.y + 1) % 4, (self.y + 3) % 4, (self.y + 2) % 4
        self.z, self.h, self.core = self.dp // 4, self.dp // 2 % 2, self.dp % 2
        self.z_up, self.z_down, self.z_far = (self.z + 1) % 4, (self.z + 3) % 4, (self.z + 2) % 4
        self.x_dev = {"seq": self.b * 4 + self.y}
        self.up_dev = {"seq": self.a * 4 + self.up}
        self.down_dev = {"seq": self.a * 4 + self.down}
        self.h_dev = {"dp": self.member(self.z, 1 - self.h)}
        self.z_up_dev = {"dp": self.member(self.z_up, self.h)}
        self.z_down_dev = {"dp": self.member(self.z_down, self.h)}
        self.twin_dev = {"dp": self.dp + 1 - 2 * self.core}
        self.x = self.h * 2 + self.a
        self.x_up, self.x_down, self.x_far = (self.x + 1) % 4, (self.x + 3) % 4, (self.x + 2) % 4
        self.x_up_dev, self.x_down_dev = self.at_x(self.x_up), self.at_x(self.x_down)

    def member(self, z, h, twin=False):
        core = 1 - self.core if twin else self.core
        return z * 4 + h * 2 + core

    def at_x(self, x):
        return {"seq": x % 2 * 4 + self.y, "dp": self.member(self.z, x // 2)}

    def column(self, twin=False):
        return self.z * 4 + (1 - self.core if twin else self.core)

    def peers(self):
        return [{"seq": (self.seq + k) % 8} for k in range(1, 8)]


def enter(devices):
    barrier = pltpu.get_barrier_semaphore()
    for device in devices:
        pl.semaphore_signal(barrier, inc=1, device_id=device, device_id_type=MESH)
    pl.semaphore_wait(barrier, len(devices))


class Mail:
    def __init__(self, send, recv):
        self.send, self.recv = send, recv
        self.count, self.started = 0, {}

    def slots(self, n):
        first = self.count
        self.count += n
        return first

    def copy(self, slot, src, dst, device):
        return pltpu.make_async_remote_copy(
            src_ref=src, dst_ref=dst, send_sem=self.send.at[slot], recv_sem=self.recv.at[slot],
            device_id=device, device_id_type=MESH,
        )

    def go(self, slot, src, dst, device):
        copy = self.copy(slot, src, dst, device)
        copy.start()
        self.started[slot] = copy

    def arrived(self, slot, dst, device):
        self.copy(slot, dst, dst, device).wait_recv()

    def sent(self, slot):
        self.started.pop(slot).wait_send()

    def finish(self):
        for copy in self.started.values():
            copy.wait_send()


def gather_seq(me, mail, x_ref, out_ref):
    a, b, y, up, down, far = me.a, me.b, me.y, me.up, me.down, me.far
    XP, U, D = me.x_dev, me.up_dev, me.down_dev
    n = mail.slots(18)

    def cut(ref, rows, half):
        lo, hi = ((0, FIRST), (FIRST, ROWS))[rows]
        return ref.at[lo:hi] if half is None else ref.at[lo:hi, half * MID : half * MID + MID]

    def at(col, row, rows, half=None):
        return cut(out_ref.at[col * 4 + row], rows, half)

    def send(i, rows, dev):
        mail.go(n + i, cut(x_ref, rows, None), at(a, y, rows), dev)

    def fwd(i, ref, dev):
        mail.go(n + i, ref, ref, dev)

    def got(i, dst):
        mail.arrived(n + i, dst, XP)

    send(0, 0, XP)
    send(1, 0, U)
    send(2, 0, D)
    send(3, 1, U)
    send(4, 1, D)
    send(5, 1, XP)
    yield
    got(0, at(b, y, 0))
    fwd(6, at(b, y, 0), U)
    fwd(7, at(b, y, 0), D)
    yield
    got(1, at(a, down, 0))
    fwd(8, at(a, down, 0, 0), U)
    got(2, at(a, up, 0))
    fwd(9, at(a, up, 0, 1), D)
    yield
    got(3, at(a, down, 1))
    fwd(10, at(a, down, 1, 0), U)
    fwd(11, at(a, down, 1), XP)
    got(4, at(a, up, 1))
    fwd(12, at(a, up, 1, 1), D)
    fwd(13, at(a, up, 1), XP)
    yield
    got(5, at(b, y, 1))
    got(6, at(b, down, 0))
    fwd(14, at(b, down, 0, 0), U)
    got(7, at(b, up, 0))
    fwd(15, at(b, up, 0, 1), D)
    yield
    got(10, at(a, far, 1, 0))
    fwd(16, at(a, far, 1, 0), XP)
    got(12, at(a, far, 1, 1))
    fwd(17, at(a, far, 1, 1), XP)
    yield
    got(8, at(a, far, 0, 0))
    got(9, at(a, far, 0, 1))
    got(11, at(b, down, 1))
    got(13, at(b, up, 1))
    yield
    got(14, at(b, far, 0, 0))
    got(15, at(b, far, 0, 1))
    got(16, at(b, far, 1, 0))
    got(17, at(b, far, 1, 1))


def gather_y(me, mail, x_ref, out_ref):
    y, up, down, far = me.y, me.up, me.down, me.far
    U, D = me.up_dev, me.down_dev
    n = mail.slots(4)
    H = ROWS // 2
    mail.go(n, x_ref, out_ref.at[y], U)
    mail.go(n + 1, x_ref, out_ref.at[y], D)
    yield
    mail.arrived(n, out_ref.at[down], D)
    mail.go(n + 2, out_ref.at[down, 0:H], out_ref.at[down, 0:H], U)
    mail.arrived(n + 1, out_ref.at[up], U)
    mail.go(n + 3, out_ref.at[up, H:ROWS], out_ref.at[up, H:ROWS], D)
    yield
    mail.arrived(n + 2, out_ref.at[far, 0:H], D)
    mail.arrived(n + 3, out_ref.at[far, H:ROWS], U)


def scatter_y(me, mail, part, p2, p1, out):
    y, up, down, far = me.y, me.up, me.down, me.far
    U, D = me.up_dev, me.down_dev
    n = mail.slots(6)
    H = ROWS // 2
    mail.go(n + 2, part.at[up, H:ROWS], p1.at[0, H:ROWS], U)
    mail.go(n + 3, part.at[down, 0:H], p1.at[1, 0:H], D)
    yield
    mail.go(n, part.at[far, 0:H], p2.at[0], U)
    mail.go(n + 1, part.at[far, H:ROWS], p2.at[1], D)
    yield
    mail.arrived(n, p2.at[0], D)
    add(part.at[up, 0:H], p2.at[0])
    mail.go(n + 4, part.at[up, 0:H], p1.at[0, 0:H], U)
    mail.arrived(n + 1, p2.at[1], U)
    add(part.at[down, H:ROWS], p2.at[1])
    mail.go(n + 5, part.at[down, H:ROWS], p1.at[1, H:ROWS], D)
    yield
    mail.arrived(n + 2, p1.at[0, H:ROWS], D)
    mail.arrived(n + 5, p1.at[1, H:ROWS], U)
    out(H, ROWS, val(part.at[y, H:ROWS]) + val(p1.at[0, H:ROWS]) + val(p1.at[1, H:ROWS]))
    mail.arrived(n + 3, p1.at[1, 0:H], U)
    mail.arrived(n + 4, p1.at[0, 0:H], D)
    out(0, H, val(part.at[y, 0:H]) + val(p1.at[0, 0:H]) + val(p1.at[1, 0:H]))


def val(ref):
    return ref[...].astype(WIDE)


def add(dst, src):
    dst[...] = (val(dst) + val(src)).astype(LOW)


def swap_seq(me, mail, own_ref, all_ref, lo, hi):
    n = mail.slots(7)
    for k in range(1, 8):
        to = (me.seq + k) % 8
        mail.go(n + k - 1, own_ref.at[to, :, lo:hi], all_ref.at[me.seq, me.dp, :, lo:hi], {"seq": to})
    yield
    for k in range(1, 8):
        came = (me.seq + 8 - k) % 8
        mail.arrived(n + k - 1, all_ref.at[came, me.dp, :, lo:hi], me.x_dev)


def gather_dp(me, mail, ref):
    z, h = me.z, me.h
    n = mail.slots(19)
    HD, ZU, ZD, TW = me.h_dev, me.z_up_dev, me.z_down_dev, me.twin_dev

    def at(zz, hh, half=None, twin=False):
        d = me.member(zz, hh, twin)
        return ref.at[:, d] if half is None else ref.at[4 * half : 4 * half + 4, d]

    def fwd(i, r, dev):
        mail.go(n + i, r, r, dev)

    def got(i, r):
        mail.arrived(n + i, r, TW)

    hs = (h, 1 - h)
    fwd(0, at(z, h), HD)
    fwd(1, at(z, h), ZU)
    fwd(2, at(z, h), ZD)
    fwd(9, at(z, h), TW)
    yield
    got(0, at(z, 1 - h))
    fwd(3, at(z, 1 - h), ZU)
    fwd(4, at(z, 1 - h), ZD)
    fwd(10, at(z, 1 - h), TW)
    yield
    for k in range(2):
        got(1 + 2 * k, at(me.z_down, hs[k]))
        fwd(5 + 2 * k, at(me.z_down, hs[k], 0), ZU)
        fwd(11 + 2 * k, at(me.z_down, hs[k]), TW)
        yield
        got(2 + 2 * k, at(me.z_up, hs[k]))
        fwd(6 + 2 * k, at(me.z_up, hs[k], 1), ZD)
        fwd(12 + 2 * k, at(me.z_up, hs[k]), TW)
        yield
    for k in range(2):
        got(5 + 2 * k, at(me.z_far, hs[k], 0))
        fwd(15 + 2 * k, at(me.z_far, hs[k], 0), TW)
        got(6 + 2 * k, at(me.z_far, hs[k], 1))
        fwd(16 + 2 * k, at(me.z_far, hs[k], 1), TW)
        yield
    got(9, at(z, h, twin=True))
    got(10, at(z, 1 - h, twin=True))
    for k in range(2):
        got(11 + 2 * k, at(me.z_down, hs[k], twin=True))
        got(12 + 2 * k, at(me.z_up, hs[k], twin=True))
        got(15 + 2 * k, at(me.z_far, hs[k], 0, twin=True))
        got(16 + 2 * k, at(me.z_far, hs[k], 1, twin=True))


def swap_y(me, mail, own_ref, all_ref):
    n = mail.slots(3)
    for k in (2, 1, 3):
        to = (me.y + k) % 4
        mail.go(n + k - 1, own_ref.at[to], all_ref.at[me.seq, me.dp], {"seq": me.a * 4 + to})
    yield
    for k in (1, 3, 2):
        came = me.a * 4 + (me.y + 4 - k) % 4
        mail.arrived(n + k - 1, all_ref.at[came, me.dp], me.up_dev)


def slab(me, ref, x, z, half=None, twin=False):
    d = me.member(z, x // 2, twin)
    first = x % 2 * 4
    return ref.at[pl.ds(first, 4), d] if half is None else ref.at[pl.ds(first + 2 * half, 2), d]


def gather_xz(me, mail, ref):
    n = mail.slots(36)
    XU, XD, ZU, ZD, TW = me.x_up_dev, me.x_down_dev, me.z_up_dev, me.z_down_dev, me.twin_dev
    z, zu, zd, zf = me.z, me.z_up, me.z_down, me.z_far
    xs = (me.x, me.x_down, me.x_up, me.x_far)

    def at(x, zz, half=None, twin=False):
        return slab(me, ref, x, zz, half, twin)

    def fwd(i, r, dev):
        mail.go(n + i, r, r, dev)

    def got(i, r):
        mail.arrived(n + i, r, TW)

    def z_first(k):
        fwd(4 + 4 * k, at(xs[k], z), ZU)
        fwd(5 + 4 * k, at(xs[k], z), ZD)
        fwd(20 + 4 * k, at(xs[k], z), TW)

    def z_second(k):
        got(4 + 4 * k, at(xs[k], zd))
        fwd(6 + 4 * k, at(xs[k], zd, 0), ZU)
        fwd(21 + 4 * k, at(xs[k], zd), TW)
        got(5 + 4 * k, at(xs[k], zu))
        fwd(7 + 4 * k, at(xs[k], zu, 1), ZD)
        fwd(22 + 4 * k, at(xs[k], zu), TW)

    def z_third(k):
        got(6 + 4 * k, at(xs[k], zf, 0))
        got(7 + 4 * k, at(xs[k], zf, 1))
        fwd(23 + 4 * k, at(xs[k], zf), TW)

    fwd(0, at(me.x, z), XU)
    fwd(1, at(me.x, z), XD)
    z_first(0)
    yield
    got(0, at(me.x_down, z))
    fwd(2, at(me.x_down, z, 0), XU)
    got(1, at(me.x_up, z))
    fwd(3, at(me.x_up, z, 1), XD)
    z_first(1)
    z_first(2)
    yield
    z_second(0)
    yield
    got(2, at(me.x_far, z, 0))
    got(3, at(me.x_far, z, 1))
    z_first(3)
    yield
    z_second(1)
    yield
    z_third(0)
    z_second(2)
    yield
    z_third(1)
    yield
    z_second(3)
    z_third(2)
    yield
    z_third(3)
    yield
    for k in range(4):
        for i, zz in enumerate((z, zd, zu, zf)):
            got(20 + 4 * k + i, at(xs[k], zz, twin=True))


def add_slabs(dst, *sources):
    def one(i, carry):
        total = val(dst.at[i])
        for source in sources:
            total = total + val(source.at[i])
        dst[i] = total.astype(LOW)
        return carry

    lax.fori_loop(0, dst.shape[0], one, 0)


def halved(ref, half):
    k = ref.shape[0] // 2
    return ref.at[half * k : half * k + k]


class RingSum:
    def __init__(self, mail, at, places, devices, over, near):
        self.mail, self.at, self.places, self.devices = mail, at, places, devices
        self.over, self.near = over, near
        self.n = mail.slots(6)

    def first(self):
        own, up, down, far = self.places
        U, D = self.devices
        go, n = self.mail.go, self.n
        go(n, halved(self.at(far), 0), self.over.at[0], U)
        go(n + 1, halved(self.at(far), 1), self.over.at[1], D)
        go(n + 2, halved(self.at(up), 1), halved(self.near.at[0], 1), U)
        go(n + 3, halved(self.at(down), 0), halved(self.near.at[1], 0), D)

    def second(self):
        own, up, down, far = self.places
        U, D = self.devices
        go, got, n = self.mail.go, self.mail.arrived, self.n
        got(n, self.over.at[0], D)
        add_slabs(halved(self.at(up), 0), self.over.at[0])
        go(n + 4, halved(self.at(up), 0), halved(self.near.at[0], 0), U)
        got(n + 1, self.over.at[1], U)
        add_slabs(halved(self.at(down), 1), self.over.at[1])
        go(n + 5, halved(self.at(down), 1), halved(self.near.at[1], 1), D)

    def third(self):
        own = self.places[0]
        U, D = self.devices
        got, n = self.mail.arrived, self.n
        got(n + 2, halved(self.near.at[0], 1), D)
        got(n + 3, halved(self.near.at[1], 0), U)
        got(n + 4, halved(self.near.at[0], 0), D)
        got(n + 5, halved(self.near.at[1], 1), U)
        add_slabs(self.at(own), self.near.at[0], self.near.at[1])


def twin_sum(me, mail, stage, acc, order, product):
    slots = stage.shape[0]
    n = mail.slots(len(order))

    def settle(i):
        mail.arrived(n + i, acc.at[order[i]], me.twin_dev)
        add_slabs(acc.at[order[i]], stage.at[i % slots, :, me.core])

    for i, s in enumerate(order):
        if i >= slots:
            mail.sent(n + i - slots)
        product(s, stage.at[i % slots])
        mail.go(n + i, stage.at[i % slots, :, 1 - me.core], acc.at[s], me.twin_dev)
        if i > 0:
            settle(i - 1)
        yield
    settle(len(order) - 1)
    for i in range(max(0, len(order) - slots), len(order)):
        mail.sent(n + i)


def scatter_xz(me, mail, acc, z_over, z_near, x_over, x_near):
    xs = (me.x_far, me.x, me.x_up, me.x_down)
    zs = (me.z, me.z_up, me.z_down, me.z_far)
    XU, XD, ZU, ZD = me.x_up_dev, me.x_down_dev, me.z_up_dev, me.z_down_dev

    def at(x):
        return lambda z: acc.at[pl.ds(x % 2 * 4, 4), z * 2 + x // 2]

    rings = [RingSum(mail, at(x), zs, (ZU, ZD), z_over.at[k], z_near.at[k]) for k, x in enumerate(xs)]
    ring = RingSum(mail, lambda x: at(x)(me.z), (me.x, me.x_up, me.x_down, me.x_far), (XU, XD), x_over, x_near)
    rings[0].first()
    yield
    rings[2].first()
    rings[3].first()
    rings[1].first()
    yield
    for k in (0, 2, 3, 1):
        rings[k].second()
        yield
    for k in (0, 2, 3):
        rings[k].third()
        yield
    ring.first()
    yield
    rings[1].third()
    yield
    ring.second()
    yield
    ring.third()


def scatter_hz(me, mail, acc, z_over, z_near, h_near):
    hs = (1 - me.h, me.h)
    zs = (me.z, me.z_up, me.z_down, me.z_far)

    def at(h):
        return lambda z: acc.at[:, z * 2 + h]

    rings = [RingSum(mail, at(h), zs, (me.z_up_dev, me.z_down_dev), z_over.at[k], z_near.at[k]) for k, h in enumerate(hs)]
    n = mail.slots(1)
    rings[0].first()
    rings[1].first()
    yield
    for k in range(2):
        rings[k].second()
        yield
    rings[0].third()
    mail.go(n, at(1 - me.h)(me.z), h_near, me.h_dev)
    yield
    rings[1].third()
    yield
    mail.arrived(n, h_near, me.h_dev)
    add_slabs(at(me.h)(me.z), h_near)


def send_y(me, mail, slab, result):
    n = mail.slots(3)
    for k in (2, 1, 3):
        to = (me.y + k) % 4
        mail.go(n + k - 1, slab.at[to], result.at[me.y], {"seq": me.a * 4 + to})
    result[me.y] = slab[me.y]
    yield
    for k in (1, 3, 2):
        mail.arrived(n + k - 1, result.at[(me.y + 4 - k) % 4], me.up_dev)


def send_seq(me, mail, slab, result, lo, hi):
    n = mail.slots(7)
    for k in range(1, 8):
        to = (me.seq + k) % 8
        mail.go(n + k - 1, slab.at[to, :, lo:hi], result.at[me.seq], {"seq": to})
    result[me.seq] = slab[me.seq, :, lo:hi]
    yield
    for k in range(1, 8):
        mail.arrived(n + k - 1, result.at[(me.seq + 8 - k) % 8], me.x_dev)


def scatter_bufs():
    late = ROWS - FIRST
    shapes = ((4, late, MODEL), (2, late, MID), (2, late, MODEL), (4, FIRST, MID), (4, FIRST, MODEL), (1, FIRST, MODEL))
    return [pltpu.VMEM(shape, LOW) for shape in shapes]


def scatter_seq(me, mail, part, bufs, out):
    a, b, y, up, down, far = me.a, me.b, me.y, me.up, me.down, me.far
    XP, U, D = me.x_dev, me.up_dev, me.down_dev
    qx, q2, q1, p2, p1, px = bufs
    n = mail.slots(23)
    halves = (pl.ds(0, MID), pl.ds(MID, MID))

    def go(i, src, dst, dev):
        mail.go(n + i, src, dst, dev)

    def got(i, dst):
        mail.arrived(n + i, dst, XP)

    def at(col, row, rows, half=None):
        lo, hi = ((0, FIRST), (FIRST, ROWS))[rows]
        ref = part.at[col * 4 + row]
        return ref.at[lo:hi] if half is None else ref.at[lo:hi, halves[half]]

    def lane(ref, k, half):
        return ref.at[k, :, halves[half]]

    for k, row in enumerate((far, down, up, y)):
        go(k, at(b, row, 1), qx.at[row], XP)
    cols = (b, a)

    def p_first(k):
        c, s = cols[k], 10 + 6 * k
        go(s, at(c, far, 0, 0), p2.at[2 * k], U)
        go(s + 1, at(c, far, 0, 1), p2.at[2 * k + 1], D)
        go(s + 2, at(c, up, 0, 1), lane(p1, 2 * k, 1), U)
        go(s + 3, at(c, down, 0, 0), lane(p1, 2 * k + 1, 0), D)

    def p_second(k):
        c, s = cols[k], 10 + 6 * k
        got(s, p2.at[2 * k])
        add(at(c, up, 0, 0), p2.at[2 * k])
        go(s + 4, at(c, up, 0, 0), lane(p1, 2 * k, 0), U)
        got(s + 1, p2.at[2 * k + 1])
        add(at(c, down, 0, 1), p2.at[2 * k + 1])
        go(s + 5, at(c, down, 0, 1), lane(p1, 2 * k + 1, 1), D)

    def p_third(k):
        s = 10 + 6 * k
        got(s + 2, lane(p1, 2 * k, 1))
        got(s + 3, lane(p1, 2 * k + 1, 0))
        got(s + 4, lane(p1, 2 * k, 0))
        got(s + 5, lane(p1, 2 * k + 1, 1))
        return val(at(cols[k], y, 0)) + val(p1.at[2 * k]) + val(p1.at[2 * k + 1])

    p_first(0)
    yield
    p_first(1)
    yield
    got(0, qx.at[far])
    add(at(a, far, 1), qx.at[far])
    go(4, at(a, far, 1, 0), q2.at[0], U)
    go(5, at(a, far, 1, 1), q2.at[1], D)
    yield
    p_second(0)
    yield
    got(1, qx.at[down])
    add(at(a, down, 1), qx.at[down])
    go(6, at(a, down, 1, 0), lane(q1, 1, 0), D)
    got(2, qx.at[up])
    add(at(a, up, 1), qx.at[up])
    go(7, at(a, up, 1, 1), lane(q1, 0, 1), U)
    yield
    p_second(1)
    yield
    rows = p_third(0)
    own = at(b, y, 0)
    own[...] = rows.astype(LOW)
    go(22, own, px.at[0], XP)
    yield
    got(4, q2.at[0])
    add(at(a, up, 1, 0), q2.at[0])
    go(8, at(a, up, 1, 0), lane(q1, 0, 0), U)
    got(5, q2.at[1])
    add(at(a, down, 1, 1), q2.at[1])
    go(9, at(a, down, 1, 1), lane(q1, 1, 1), D)
    yield
    rows = p_third(1)
    got(22, px.at[0])
    out(0, FIRST, rows + val(px.at[0]))
    yield
    got(3, qx.at[y])
    got(6, lane(q1, 1, 0))
    got(7, lane(q1, 0, 1))
    got(8, lane(q1, 0, 0))
    got(9, lane(q1, 1, 1))
    out(FIRST, ROWS, val(at(a, y, 1)) + val(qx.at[y]) + val(q1.at[0]) + val(q1.at[1]))


def run(*tasks):
    tasks = list(tasks)
    while tasks:
        for task in list(tasks):
            if next(task, tasks) is tasks:
                tasks.remove(task)


def step(task):
    return next(task, None)
def dot(a, b, dims=((1,), (0,))):
    return lax.dot_general(a, b, (dims, ((), ())), preferred_element_type=WIDE)


def row_scale(values):
    return lax.rsqrt(jnp.mean(values * values, axis=-1, keepdims=True) + EPS)


def front_kernel(
    x_ref, live_ref, cot_ref, wa_own, wm_own, pos_q, pos_k,
    one_out, wa_out, grad_all, wm, qkv_out, probs_out, att_out, resid, two,
    one_all, wa, grad_own, qkv, probs, att, part, qx, q2, q1, p2, p1, px, send, recv, local_sem,
):
    me = Place()
    mail = Mail(send, recv)
    saves = []

    def save(src, dst):
        copy = pltpu.make_async_copy(src, dst, local_sem.at[len(saves)])
        copy.start()
        saves.append(copy)
        return copy

    enter(me.peers() + [me.h_dev, me.z_up_dev, me.z_down_dev, me.twin_dev, me.x_up_dev, me.x_down_dev])
    swap_a = swap_seq(me, mail, wa_own, wa, 0, PROJ)
    step(swap_a)
    x = x_ref[...].astype(WIDE)
    one_all[me.seq] = (x * row_scale(x) * live_ref[...]).astype(LOW)
    gather_one = gather_seq(me, mail, one_all.at[me.seq], one_all)
    step(gather_one)
    wa[pl.ds(me.seq, 1), pl.ds(me.dp, 1), :, 0:PROJ] = wa_own[pl.ds(me.seq, 1), :, 0:PROJ][None]
    for k in range(8):
        wa[k, pl.ds(me.dp, 1), :, PROJ:] = wa_own[k, :, PROJ:][None]
    step(swap_a)
    gather_wa = gather_dp(me, mail, wa)
    step(gather_wa)
    swap_m = swap_y(me, mail, wm_own, wm)
    step(swap_m)
    keep_m = save(wm_own.at[me.y], wm.at[me.seq, me.dp])
    grad_own[...] = (cot_ref[...].astype(WIDE) * live_ref[...]).astype(LOW)
    save(grad_own, grad_all.at[me.y])
    for i in range(3):
        step(gather_one)
        step(gather_wa)
    step(swap_m)
    keep_m.wait()
    gather_wm = gather_xz(me, mail, wm)
    step(gather_wm)
    run(gather_one, gather_wa)
    gather_g = gather_y(me, mail, grad_own, grad_all)
    step(gather_g)
    save(one_all, one_out)
    save(wa, wa_out)

    def project(i, carry):
        rows = one_all[pl.ds(i * 2, 2)].reshape(2 * ROWS, MODEL)
        weight = wa[:, :, :, 0:PROJ].reshape(MODEL, PROJ)
        qkv[pl.ds(pl.multiple_of(i * 256, 256), 256), :] = dot(rows, weight).astype(LOW)
        return carry

    def attend(i, carry):
        first = pl.multiple_of(i * ROWS, ROWS)
        rows = pl.ds(first, ROWS)
        allowed = pos_k[...] <= pos_q[rows, :]
        for head in range(2):
            lo, hi = head * HEAD_DIM, (head + 1) * HEAD_DIM
            q = qkv[rows, lo:hi]
            k = qkv[:, PART + lo : PART + hi]
            v = qkv[:, 2 * PART + lo : 2 * PART + hi]
            scores = dot(q, k, ((1,), (1,))) * (1.0 / math.sqrt(HEAD_DIM)) - math.log(8 * ROWS)
            p = jnp.where(allowed, 1.0 / (1.0 + jnp.exp(-scores)), 0.0).astype(LOW)
            probs[head, rows, :] = p
            att[rows, lo:hi] = dot(p, v).astype(LOW)
        return carry

    def out_project(col):
        rows = att[pl.ds(pl.multiple_of(col * 512, 512), 512), :]

        def piece(k, carry):
            weight = wa[k, :, :, PROJ:].reshape(PART, PART)
            columns = pl.ds(pl.multiple_of(k * PART, PART), PART)
            part[pl.ds(col * 4, 4), :, columns] = dot(rows, weight).reshape(4, ROWS, PART).astype(LOW)
            return carry

        lax.fori_loop(0, 8, piece, 0)

    for i in range(2):
        lax.fori_loop(2 * i, 2 * i + 2, project, 0)
        step(gather_g)
        step(gather_wm)
    save(qkv, qkv_out)

    def write(lo, hi, rows):
        total = x_ref[lo:hi].astype(WIDE) + rows
        resid[lo:hi] = total
        two[lo:hi] = (total * row_scale(total) * live_ref[lo:hi]).astype(LOW)

    scatter = scatter_seq(me, mail, part, (qx, q2, q1, p2, p1, px), write)
    for col in (me.b, me.a):
        for i in range(2):
            lax.fori_loop(col * 4 + 2 * i, col * 4 + 2 * i + 2, attend, 0)
            step(gather_wm)
            step(gather_g)
        out_project(col)
        step(scatter)
    save(probs, probs_out)
    save(att, att_out)
    run(scatter, gather_wm, gather_g)
    for copy in saves:
        if copy is not keep_m:
            copy.wait()
    mail.finish()


def front(x, live, cot, wa_own, wm_own, pos):
    vmem, anywhere = pl.BlockSpec(memory_space=pltpu.VMEM), pl.BlockSpec(memory_space=pl.ANY)
    shape = jax.ShapeDtypeStruct
    count = 7 + 18 + 19 + 3 + 36 + 4 + 23
    return pl.pallas_call(
        front_kernel,
        out_shape=(
            shape((8, ROWS, MODEL), LOW), shape((8, 16, 16, 1024), LOW), shape((4, ROWS, MODEL), LOW),
            shape((8, 16, 16, SLAB), LOW), shape((1024, PROJ), LOW), shape((2, 1024, 1024), LOW),
            shape((1024, PART), LOW), shape((ROWS, MODEL), WIDE), shape((ROWS, MODEL), LOW),
        ),
        in_specs=[vmem] * 4 + [anywhere] + [vmem] * 2,
        out_specs=(anywhere,) * 7 + (vmem, vmem),
        scratch_shapes=[
            pltpu.VMEM((8, ROWS, MODEL), LOW), pltpu.VMEM((8, 16, 16, 1024), LOW), pltpu.VMEM((ROWS, MODEL), LOW),
            pltpu.VMEM((1024, PROJ), LOW), pltpu.VMEM((2, 1024, 1024), LOW), pltpu.VMEM((1024, PART), LOW),
            pltpu.VMEM((8, ROWS, MODEL), LOW),
        ]
        + scatter_bufs()
        + [pltpu.SemaphoreType.DMA((count,)), pltpu.SemaphoreType.DMA((count,)), pltpu.SemaphoreType.DMA((8,))],
        compiler_params=pltpu.CompilerParams(collective_id=1, has_side_effects=True, vmem_limit_bytes=56 * 2**20),
        name="front",
    )(x, live, cot, wa_own, wm_own, pos[:, None], pos[None, :])
def mlp_kernel(
    two_ref, resid, cot_ref, live_ref, grad_all, wm_all,
    two_out, hidden_out, pair_out, branch_out, grad_resid, grad_branch,
    down_own,
    wm, grads, twos, hidden, pair, part, branch, p2, p1,
    stage, acc, z_over, z_near, x_over, x_near, send, recv, local_sem,
):
    me = Place()
    mail = Mail(send, recv)
    saves = []

    def save(src, dst):
        copy = pltpu.make_async_copy(src, dst, local_sem.at[len(saves)])
        copy.start()
        saves.append(copy)
        return copy

    load_w = save(wm_all, wm)
    load_g = save(grad_all, grads)
    others = [{"seq": me.a * 4 + (me.y + k) % 4} for k in (1, 2, 3)]
    enter(others + [me.x_up_dev, me.x_down_dev, me.z_up_dev, me.z_down_dev, me.twin_dev])
    twos[me.y] = two_ref[...]
    gather = gather_y(me, mail, twos.at[me.y], twos)
    step(gather)
    load_w.wait()
    load_g.wait()

    def rows_of(ref, blocks):
        return jnp.concatenate([ref[k] for k in blocks], axis=0)

    def put(ref, blocks, columns, values):
        for i, k in enumerate(blocks):
            ref[k, :, columns] = values[i * ROWS : (i + 1) * ROWS].astype(LOW)

    def hidden_tile(blocks, j, wide):
        start = j * 128
        if not isinstance(j, int):
            start = pl.multiple_of(start, 128)
        width = wide * 128
        weight = wm[:, :, :, pl.ds(2 * start, 2 * width)].reshape(MODEL, 2 * width)
        gate_up = dot(rows_of(twos, blocks), weight)
        down = wm[:, :, :, pl.ds(PAIR + start, width)].reshape(MODEL, width)
        grad_hidden = dot(rows_of(grads, blocks), down)
        low, pairs = [], []
        for i in range(wide):
            gate = gate_up[:, i * 256 : i * 256 + 128]
            up = gate_up[:, i * 256 + 128 : i * 256 + 256]
            back = grad_hidden[:, i * 128 : i * 128 + 128]
            squashed = 1.0 / (1.0 + jnp.exp(-gate))
            active = gate * squashed
            low.append(active * up)
            pairs.append(back * up * (squashed * (1.0 + gate * (1.0 - squashed))))
            pairs.append(back * active)
        put(hidden, blocks, pl.ds(start, width), jnp.concatenate(low, axis=1))
        put(pair, blocks, pl.ds(2 * start, 2 * width), jnp.concatenate(pairs, axis=1))

    def ahead(blocks):
        def tile(j, carry):
            hidden_tile(blocks, 2 * j, 2)
            return carry

        lax.fori_loop(0, 5, tile, 0)
        hidden_tile(blocks, 10, 1)

    def back(blocks):
        def tile(s, carry):
            columns = pl.ds(pl.multiple_of(s * 256, 256), 256)
            weight = wm[s, :, :, 0:PAIR].reshape(256, PAIR)
            put(part, blocks, columns, dot(rows_of(pair, blocks), weight, ((1,), (1,))))
            return carry

        lax.fori_loop(0, 8, tile, 0)

    def down_back(blocks):
        def tile(s, carry):
            columns = pl.ds(pl.multiple_of(s * 256, 256), 256)
            weight = wm[s, :, :, PAIR:].reshape(256, UNITS)
            put(branch, blocks, columns, dot(rows_of(hidden, blocks), weight, ((1,), (1,))))
            return carry

        lax.fori_loop(0, 8, tile, 0)

    def write(lo, hi, rows):
        x = resid[lo:hi]
        scale = row_scale(x)
        hat = x * scale
        inner = jnp.mean(rows * hat, axis=-1, keepdims=True)
        total = cot_ref[lo:hi].astype(WIDE) * live_ref[lo:hi] + scale * (rows - hat * inner)
        grad_resid[lo:hi] = total
        grad_branch[lo:hi] = total.astype(LOW)

    scatter = scatter_y(me, mail, part, p2, p1, write)
    ahead([me.y])
    step(gather)
    ahead([me.up, me.down])
    back([me.up, me.down])
    step(scatter)
    step(gather)
    ahead([me.far])
    back([me.far])
    step(scatter)
    save(twos, two_out)
    save(hidden, hidden_out)
    save(pair, pair_out)
    back([me.y])
    step(scatter)
    order = [me.a * 4 + i for i in range(4)] + [me.b * 4 + i for i in range(4)]

    def down_product(s, out):
        rows = grads[:, :, pl.ds(pl.multiple_of(s * 256, 256), 256)].reshape(4 * ROWS, 256)

        def tile(j, carry):
            columns = pl.ds(pl.multiple_of(j * 128, 128), 128)
            terms = dot(rows, hidden[:, :, columns].reshape(4 * ROWS, 128), ((0,), (0,)))
            out[:, :, :, columns] = terms.reshape(8, 2, 16, 128).astype(LOW)
            return carry

        lax.fori_loop(0, UNITS // 128, tile, 0)

    twin = twin_sum(me, mail, stage, acc, order, down_product)
    for i in range(4):
        step(twin)
    step(scatter)
    step(twin)
    sums = scatter_xz(me, mail, acc, z_over, z_near, x_over, x_near)
    step(sums)
    run(twin)
    step(sums)
    step(scatter)
    every = [me.y, me.up, me.down, me.far]
    down_back(every)
    save(branch, branch_out)
    run(scatter, gather, sums)
    run(send_y(me, mail, acc.at[pl.ds(me.a * 4, 4), me.z * 2 + me.h], down_own))
    for copy in saves[2:]:
        copy.wait()
    mail.finish()


def mlp(two, resid, cot, live, grad_all, wm):
    vmem, anywhere = pl.BlockSpec(memory_space=pltpu.VMEM), pl.BlockSpec(memory_space=pl.ANY)
    shape = jax.ShapeDtypeStruct
    blocks = (4, ROWS, MODEL)
    return pl.pallas_call(
        mlp_kernel,
        out_shape=(
            shape(blocks, LOW), shape((4, ROWS, UNITS), LOW), shape((4, ROWS, PAIR), LOW), shape(blocks, LOW),
            shape((ROWS, MODEL), WIDE), shape((ROWS, MODEL), LOW), shape((4, 16, UNITS), LOW),
        ),
        in_specs=[vmem] * 4 + [anywhere] * 2,
        out_specs=(anywhere,) * 4 + (vmem,) * 3,
        scratch_shapes=[
            pltpu.VMEM((8, 16, 16, SLAB), LOW), pltpu.VMEM(blocks, LOW), pltpu.VMEM(blocks, LOW),
            pltpu.VMEM((4, ROWS, UNITS), LOW), pltpu.VMEM((4, ROWS, PAIR), LOW), pltpu.VMEM(blocks, LOW),
            pltpu.VMEM(blocks, LOW), pltpu.VMEM((2, ROWS // 2, MODEL), LOW), pltpu.VMEM((2, ROWS, MODEL), LOW),
            pltpu.VMEM((3, 8, 2, 16, UNITS), LOW), pltpu.VMEM((8, 8, 16, UNITS), LOW),
            pltpu.VMEM((4, 2, 2, 16, UNITS), LOW), pltpu.VMEM((4, 2, 4, 16, UNITS), LOW),
            pltpu.VMEM((2, 2, 16, UNITS), LOW), pltpu.VMEM((2, 4, 16, UNITS), LOW),
            pltpu.SemaphoreType.DMA((51,)), pltpu.SemaphoreType.DMA((51,)), pltpu.SemaphoreType.DMA((6,)),
        ],
        compiler_params=pltpu.CompilerParams(collective_id=2, has_side_effects=True, vmem_limit_bytes=56 * 2**20),
        name="mlp",
    )(two, resid, cot, live, grad_all, wm)
def back_kernel(
    branch_grad, grad_resid, x_ref, live_ref, resid, branch_all, two_all, pair_all, one_all, wa_all, qkv_all, probs_all, att_all,
    layer_out, input_grad, pair_own, in_own, out_own,
    acc, z_over, z_near, x_over, x_near, grads, part, qx, q2, q1, p2, p1, px,
    wa, acc_a, az_over, az_near, h_near, twos, pair, stage, ones, qkv, probs, att, grad_att, grad_proj, grad_k, grad_v, stage_a,
    send, recv, local_sem,
):
    me = Place()
    mail = Mail(send, recv)
    loads = []

    def load(src, dst):
        copy = pltpu.make_async_copy(src, dst, local_sem.at[len(loads)])
        copy.start()
        loads.append(copy)
        return copy

    load_wa = load(wa_all, wa)
    load_branch = load(branch_all, part.at[0:4])
    enter(me.peers() + [me.h_dev, me.z_up_dev, me.z_down_dev, me.x_up_dev, me.x_down_dev, me.twin_dev])
    grads[me.seq] = branch_grad[...]
    gather = gather_seq(me, mail, grads.at[me.seq], grads)
    step(gather)
    order = [me.a * 4 + i for i in range(4)] + [me.b * 4 + i for i in range(4)]

    def columns_of(s, width=256):
        return pl.ds(pl.multiple_of(s * width, width), width)

    def pair_sums():
        yield from scatter_xz(me, mail, acc, z_over, z_near, x_over, x_near)
        yield from send_y(me, mail, acc.at[pl.ds(me.a * 4, 4), me.z * 2 + me.h], pair_own)

    sums = pair_sums()

    first, second = load(two_all, twos), load(pair_all, pair)
    waits = [load(*both) for both in ((qkv_all, qkv), (att_all, att), (one_all.at[4:8], ones))]
    first.wait()
    second.wait()

    def pair_product(s, out):
        rows = twos[:, :, columns_of(s)].reshape(4 * ROWS, 256)

        def tile(j, carry):
            columns = columns_of(j)
            terms = dot(rows, pair[:, :, columns].reshape(4 * ROWS, 256), ((0,), (0,)))
            out[:, :, :, columns] = terms.reshape(8, 2, 16, 256).astype(LOW)
            return carry

        lax.fori_loop(0, PAIR // 256, tile, 0)

    twin = twin_sum(me, mail, stage, acc, order, pair_product)
    for i in range(5):
        step(twin)
        step(gather)
    step(sums)
    for i in range(4):
        step(twin)
        step(gather)
    step(sums)

    def write_out(lo, hi, rows):
        layer_out[lo:hi] = (live_ref[lo:hi] * (resid[lo:hi] + rows)).astype(LOW)

    def write_grad(lo, hi, rows):
        x = x_ref[lo:hi].astype(WIDE)
        scale = row_scale(x)
        hat = x * scale
        inner = jnp.mean(rows * hat, axis=-1, keepdims=True)
        input_grad[lo:hi] = grad_resid[lo:hi] + live_ref[lo:hi] * scale * (rows - hat * inner)

    class Lower:
        at = {0: part.at[6, 0 : ROWS // 2], 1: part.at[6, ROWS // 2 : ROWS]}

    out_sum = scatter_y(me, mail, part.at[0:4], Lower, part.at[4:6], write_out)
    grad_sum = scatter_seq(me, mail, part, (qx, q2, q1, p2, p1, px), write_grad)

    run(gather)
    waits.append(load(one_all.at[0:4], twos))
    fetch = [load(probs_all.at[:, 256 * i : 256 * i + 256], probs.at[i]) for i in range(2)]
    load_branch.wait()
    out_slots = range(mail.count, mail.count + 6)
    step(out_sum)
    load_wa.wait()
    for wait in waits:
        wait.wait()
    head_scale = 1.0 / math.sqrt(HEAD_DIM)

    def attended_grad(i, carry):
        total = jnp.zeros((256, PART), WIDE)
        for k in range(8):
            rows = grads[pl.ds(i * 2, 2), :, k * PART : k * PART + PART].reshape(256, PART)
            total = total + dot(rows, wa[k, :, :, PROJ:].reshape(PART, PART), ((1,), (1,)))
        grad_att[columns_of(i), :] = total.astype(LOW)
        return carry

    lax.fori_loop(0, 4, attended_grad, 0)
    step(out_sum)
    step(sums)
    grad_k[...] = jnp.zeros_like(grad_k)
    grad_v[...] = jnp.zeros_like(grad_v)

    def attend_back(i):
        rows = pl.ds(256 * i, 256)
        for head in range(2):
            lo, hi = head * HEAD_DIM, (head + 1) * HEAD_DIM
            low = probs[i % 2, head]
            p = low.astype(WIDE)
            g = grad_att[rows, lo:hi]
            back = dot(g, qkv[:, 2 * PART + lo : 2 * PART + hi], ((1,), (1,)))
            grad_s = (back * (p * (1.0 - p))).astype(LOW)
            grad_q = dot(grad_s, qkv[:, PART + lo : PART + hi]) * head_scale
            grad_proj[rows, lo:hi] = grad_q.astype(LOW)
            grad_v[:, lo:hi] += dot(low, g, ((0,), (0,)))
            grad_k[:, lo:hi] += dot(grad_s, qkv[rows, lo:hi], ((0,), (0,)))

    for i in range(4):
        fetch[i].wait()
        attend_back(i)
        if i < 2:
            fetch.append(load(probs_all.at[:, 256 * i + 512 : 256 * i + 768], probs.at[i]))
        step(sums)
        step(out_sum)
    run(out_sum)
    for slot in out_slots:
        mail.sent(slot)
    grad_proj[:, PART : 2 * PART] = (grad_k[...] * head_scale).astype(LOW)
    grad_proj[:, 2 * PART :] = grad_v[...].astype(LOW)

    def norm_terms(col):
        rows = grad_proj[columns_of(col, 512), :]

        def piece(s, carry):
            weight = wa[s, :, :, 0:PROJ].reshape(256, PROJ)
            terms = dot(rows, weight, ((1,), (1,)))
            part[pl.ds(col * 4, 4), :, columns_of(s)] = terms.reshape(4, ROWS, 256).astype(LOW)
            return carry

        lax.fori_loop(0, 8, piece, 0)

    norm_terms(me.b)
    step(grad_sum)
    norm_terms(me.a)
    step(grad_sum)
    step(sums)

    def product(s, out):
        terms = jnp.zeros((256, PROJ), WIDE)
        for half, tokens in enumerate((twos, ones)):
            rows = tokens[:, :, columns_of(s)].reshape(4 * ROWS, 256)
            terms = terms + dot(rows, grad_proj[512 * half : 512 * half + 512, :], ((0,), (0,)))
        out[:, :, :, 0:PROJ] = terms.reshape(8, 2, 16, PROJ).astype(LOW)
        rows = grads[:, :, columns_of(s)].reshape(8 * ROWS, 256)
        terms = dot(att[...], rows, ((0,), (0,)))
        out[:, :, :, PROJ:] = terms.reshape(8, 2, 16, PART).astype(LOW)

    twin = twin_sum(me, mail, stage_a, acc_a, order, product)
    for i in range(9):
        step(twin)
        step(grad_sum)
        if i % 2 == 0:
            step(sums)

    def proj_sums():
        yield from scatter_hz(me, mail, acc_a, az_over, az_near, h_near)
        own = acc_a.at[:, me.z * 2 + me.h]
        out_own[...] = own[:, :, PROJ:]
        yield from send_seq(me, mail, own, in_own, 0, PROJ)

    run(proj_sums(), grad_sum, sums)

    mail.finish()


def back(branch_grad, grad_resid, x, live, resid, branch, twos, pair, ones, wa, qkv, probs, att):
    vmem, anywhere = pl.BlockSpec(memory_space=pltpu.VMEM), pl.BlockSpec(memory_space=pl.ANY)
    shape = jax.ShapeDtypeStruct
    blocks = (4, ROWS, MODEL)
    count = 18 + 8 + 30 + 3 + 6 + 23 + 8 + 13 + 7
    return pl.pallas_call(
        back_kernel,
        out_shape=(
            shape((ROWS, MODEL), LOW), shape((ROWS, MODEL), WIDE), shape((4, 16, PAIR), LOW),
            shape((8, 16, PROJ), LOW), shape((8, 16, PART), LOW),
        ),
        in_specs=[vmem] * 5 + [anywhere] * 8,
        out_specs=(vmem,) * 5,
        scratch_shapes=[
            pltpu.VMEM((8, 8, 16, PAIR), LOW), pltpu.VMEM((4, 2, 2, 16, PAIR), LOW), pltpu.VMEM((4, 2, 4, 16, PAIR), LOW),
            pltpu.VMEM((2, 2, 16, PAIR), LOW), pltpu.VMEM((2, 4, 16, PAIR), LOW), pltpu.VMEM((8, ROWS, MODEL), LOW),
            pltpu.VMEM((8, ROWS, MODEL), LOW),
        ]
        + scatter_bufs()
        + [
            pltpu.VMEM((8, 16, 16, 1024), LOW), pltpu.VMEM((8, 8, 16, 1024), LOW), pltpu.VMEM((2, 2, 4, 16, 1024), LOW),
            pltpu.VMEM((2, 2, 8, 16, 1024), LOW), pltpu.VMEM((8, 16, 1024), LOW),
            pltpu.VMEM(blocks, LOW), pltpu.VMEM((4, ROWS, PAIR), LOW), pltpu.VMEM((2, 8, 2, 16, PAIR), LOW), pltpu.VMEM(blocks, LOW),
            pltpu.VMEM((1024, PROJ), LOW), pltpu.VMEM((2, 2, 256, 1024), LOW), pltpu.VMEM((1024, PART), LOW),
            pltpu.VMEM((1024, PART), LOW), pltpu.VMEM((1024, PROJ), LOW),
            pltpu.VMEM((1024, PART), WIDE), pltpu.VMEM((1024, PART), WIDE), pltpu.VMEM((2, 8, 2, 16, 1024), LOW),
            pltpu.SemaphoreType.DMA((count,)), pltpu.SemaphoreType.DMA((count,)), pltpu.SemaphoreType.DMA((12,)),
        ],
        compiler_params=pltpu.CompilerParams(collective_id=3, has_side_effects=True, vmem_limit_bytes=62 * 2**20),
        name="back",
    )(branch_grad, grad_resid, x, live, resid, branch, twos, pair, ones, wa, qkv, probs, att)
def weights_out(attn_weight, mlp_weight, gain_one, gain_two):
    proj = (attn_weight[:, :3].astype(WIDE) * gain_one).astype(LOW).reshape(16, 3, 8, PART)
    proj = proj.transpose(2, 0, 1, 3).reshape(8, 16, PROJ)
    out = attn_weight[:, 3].reshape(16, 8, PART).transpose(1, 0, 2)
    units = mlp_weight.shape[2] // 4
    spare = UNITS - units
    pair = (mlp_weight[:, :2].astype(WIDE) * gain_two).astype(LOW).reshape(16, 2, 4, units)
    pair = jnp.pad(pair, ((0, 0), (0, 0), (0, 0), (0, spare))).reshape(16, 2, 4, UNITS // 128, 128)
    pair = pair.transpose(2, 0, 3, 1, 4).reshape(4, 16, PAIR)
    down = jnp.pad(mlp_weight[:, 2].reshape(16, 4, units), ((0, 0), (0, 0), (0, spare))).transpose(1, 0, 2)
    return jnp.concatenate([proj, out], axis=2), jnp.concatenate([pair, down], axis=2)


def weights_back(pair, down, proj, out, units):
    proj = proj.reshape(8, 16, 3, PART).transpose(1, 2, 0, 3).reshape(16, 3, MODEL).astype(WIDE)
    out = out.transpose(1, 0, 2).reshape(16, MODEL).astype(WIDE)
    pair = pair.reshape(4, 16, UNITS // 128, 2, 128).transpose(1, 3, 0, 2, 4).reshape(16, 2, 4, UNITS)
    pair = pair[..., : units // 4].reshape(16, 2, units).astype(WIDE)
    down = down[..., : units // 4].transpose(1, 0, 2).reshape(16, units).astype(WIDE)
    return proj, out, pair, down


def local(
    tokens, valid_counts, block_owner, norm1_gain, attn_weight, norm2_gain, mlp_weight, cotangent
):
    row_index = jnp.arange(ROWS, dtype=jnp.int32)
    live = (row_index < valid_counts[0, 0]).astype(WIDE)[:, None]
    pos = (block_owner[0][:, None] * ROWS + row_index[None]).reshape(-1)
    x, cot = tokens[0], cotangent[0]
    gain_one = norm1_gain.astype(WIDE)[:, None, None]
    gain_two = norm2_gain.astype(WIDE)[:, None, None]
    wa_own, wm_own = weights_out(attn_weight, mlp_weight, gain_one, gain_two)
    ones, wa, grads, wm, qkv, probs, att, resid, two = front(x, live, cot, wa_own, wm_own, pos)
    twos, hidden, pair, branch, grad_resid, branch_grad, down_own = mlp(two, resid, cot, live, grads, wm)
    layer_out, input_grad, pair_own, in_own, out_own = back(
        branch_grad, grad_resid, x, live, resid, branch, twos, pair, ones, wa, qkv, probs, att
    )
    in_sum, out_sum, pair_sum, down_sum = weights_back(pair_own, down_own, in_own, out_own, mlp_weight.shape[2])
    attn_grad = jnp.concatenate([in_sum * gain_one, out_sum[:, None]], axis=1)
    mlp_grad = jnp.concatenate([pair_sum * gain_two, down_sum[:, None]], axis=1)
    gain_one_grad = jnp.sum(in_sum * attn_weight[:, :3].astype(WIDE), axis=(1, 2))
    gain_two_grad = jnp.sum(pair_sum * mlp_weight[:, :2].astype(WIDE), axis=(1, 2))
    return (layer_out[None], input_grad[None], gain_one_grad, attn_grad, gain_two_grad, mlp_grad)


def solution(mesh):
    token_spec = P("dp", "seq", None)
    row_spec = P(("seq", "dp"), None, None)
    gain_spec = P(("seq", "dp"))
    in_specs = (
        token_spec, P("dp", "seq"), P("dp", None), gain_spec, row_spec, gain_spec, row_spec, token_spec
    )
    out_specs = (token_spec, token_spec, gain_spec, row_spec, gain_spec, row_spec)
    return jax.shard_map(local, mesh=mesh, in_specs=in_specs, out_specs=out_specs, check_vma=False)
```

```python
import functools, math
import jax
import jax.numpy as jnp
from jax import lax
from jax.experimental import pallas as pl
from jax.experimental.pallas import tpu as pltpu
from jax.sharding import PartitionSpec as P

LOW = jnp.bfloat16
WIDE = jnp.float32
MESH = pl.DeviceIdType.MESH
EPS = 1e-05
HEAD_DIM = 128
ROWS = 128
MODEL = 2048
PART = 256
PROJ = 3 * PART
UNITS = 1408
SLAB = 3 * UNITS
PAIR = 2 * UNITS
FIRST = 80
MID = MODEL // 2


class Place:
    def __init__(self):
        self.seq, self.dp = lax.axis_index("seq"), lax.axis_index("dp")
        self.a, self.y = self.seq // 4, self.seq % 4
        self.b = 1 - self.a
        self.up, self.down, self.far = (self.y + 1) % 4, (self.y + 3) % 4, (self.y + 2) % 4
        self.z, self.h, self.core = self.dp // 4, self.dp // 2 % 2, self.dp % 2
        self.z_up, self.z_down, self.z_far = (self.z + 1) % 4, (self.z + 3) % 4, (self.z + 2) % 4
        self.x_dev = {"seq": self.b * 4 + self.y}
        self.up_dev = {"seq": self.a * 4 + self.up}
        self.down_dev = {"seq": self.a * 4 + self.down}
        self.h_dev = {"dp": self.member(self.z, 1 - self.h)}
        self.z_up_dev = {"dp": self.member(self.z_up, self.h)}
        self.z_down_dev = {"dp": self.member(self.z_down, self.h)}
        self.twin_dev = {"dp": self.dp + 1 - 2 * self.core}
        self.x = self.h * 2 + self.a
        self.x_up, self.x_down, self.x_far = (self.x + 1) % 4, (self.x + 3) % 4, (self.x + 2) % 4
        self.x_up_dev, self.x_down_dev = self.at_x(self.x_up), self.at_x(self.x_down)

    def member(self, z, h, twin=False):
        core = 1 - self.core if twin else self.core
        return z * 4 + h * 2 + core

    def at_x(self, x):
        return {"seq": x % 2 * 4 + self.y, "dp": self.member(self.z, x // 2)}

    def column(self, twin=False):
        return self.z * 4 + (1 - self.core if twin else self.core)

    def peers(self):
        return [{"seq": (self.seq + k) % 8} for k in range(1, 8)]


def enter(devices):
    barrier = pltpu.get_barrier_semaphore()
    for device in devices:
        pl.semaphore_signal(barrier, inc=1, device_id=device, device_id_type=MESH)
    pl.semaphore_wait(barrier, len(devices))


class Mail:
    def __init__(self, send, recv):
        self.send, self.recv = send, recv
        self.count, self.started = 0, {}

    def slots(self, n):
        first = self.count
        self.count += n
        return first

    def copy(self, slot, src, dst, device):
        return pltpu.make_async_remote_copy(
            src_ref=src, dst_ref=dst, send_sem=self.send.at[slot], recv_sem=self.recv.at[slot],
            device_id=device, device_id_type=MESH,
        )

    def go(self, slot, src, dst, device):
        copy = self.copy(slot, src, dst, device)
        copy.start()
        self.started[slot] = copy

    def arrived(self, slot, dst, device):
        self.copy(slot, dst, dst, device).wait_recv()

    def sent(self, slot):
        self.started.pop(slot).wait_send()

    def finish(self):
        for copy in self.started.values():
            copy.wait_send()


def gather_seq(me, mail, x_ref, out_ref):
    a, b, y, up, down, far = me.a, me.b, me.y, me.up, me.down, me.far
    XP, U, D = me.x_dev, me.up_dev, me.down_dev
    n = mail.slots(18)

    def cut(ref, rows, half):
        lo, hi = ((0, FIRST), (FIRST, ROWS))[rows]
        return ref.at[lo:hi] if half is None else ref.at[lo:hi, half * MID : half * MID + MID]

    def at(col, row, rows, half=None):
        return cut(out_ref.at[col * 4 + row], rows, half)

    def send(i, rows, dev):
        mail.go(n + i, cut(x_ref, rows, None), at(a, y, rows), dev)

    def fwd(i, ref, dev):
        mail.go(n + i, ref, ref, dev)

    def got(i, dst):
        mail.arrived(n + i, dst, XP)

    send(0, 0, XP)
    send(1, 0, U)
    send(2, 0, D)
    send(3, 1, U)
    send(4, 1, D)
    send(5, 1, XP)
    yield
    got(0, at(b, y, 0))
    fwd(6, at(b, y, 0), U)
    fwd(7, at(b, y, 0), D)
    yield
    got(1, at(a, down, 0))
    fwd(8, at(a, down, 0, 0), U)
    got(2, at(a, up, 0))
    fwd(9, at(a, up, 0, 1), D)
    yield
    got(3, at(a, down, 1))
    fwd(10, at(a, down, 1, 0), U)
    fwd(11, at(a, down, 1), XP)
    got(4, at(a, up, 1))
    fwd(12, at(a, up, 1, 1), D)
    fwd(13, at(a, up, 1), XP)
    yield
    got(5, at(b, y, 1))
    got(6, at(b, down, 0))
    fwd(14, at(b, down, 0, 0), U)
    got(7, at(b, up, 0))
    fwd(15, at(b, up, 0, 1), D)
    yield
    got(10, at(a, far, 1, 0))
    fwd(16, at(a, far, 1, 0), XP)
    got(12, at(a, far, 1, 1))
    fwd(17, at(a, far, 1, 1), XP)
    yield
    got(8, at(a, far, 0, 0))
    got(9, at(a, far, 0, 1))
    got(11, at(b, down, 1))
    got(13, at(b, up, 1))
    yield
    got(14, at(b, far, 0, 0))
    got(15, at(b, far, 0, 1))
    got(16, at(b, far, 1, 0))
    got(17, at(b, far, 1, 1))


def gather_y(me, mail, x_ref, out_ref):
    y, up, down, far = me.y, me.up, me.down, me.far
    U, D = me.up_dev, me.down_dev
    n = mail.slots(4)
    H = ROWS // 2
    mail.go(n, x_ref, out_ref.at[y], U)
    mail.go(n + 1, x_ref, out_ref.at[y], D)
    yield
    mail.arrived(n, out_ref.at[down], D)
    mail.go(n + 2, out_ref.at[down, 0:H], out_ref.at[down, 0:H], U)
    mail.arrived(n + 1, out_ref.at[up], U)
    mail.go(n + 3, out_ref.at[up, H:ROWS], out_ref.at[up, H:ROWS], D)
    yield
    mail.arrived(n + 2, out_ref.at[far, 0:H], D)
    mail.arrived(n + 3, out_ref.at[far, H:ROWS], U)


def scatter_y(me, mail, part, p2, p1, out):
    y, up, down, far = me.y, me.up, me.down, me.far
    U, D = me.up_dev, me.down_dev
    n = mail.slots(6)
    H = ROWS // 2
    mail.go(n + 2, part.at[up, H:ROWS], p1.at[0, H:ROWS], U)
    mail.go(n + 3, part.at[down, 0:H], p1.at[1, 0:H], D)
    yield
    mail.go(n, part.at[far, 0:H], p2.at[0], U)
    mail.go(n + 1, part.at[far, H:ROWS], p2.at[1], D)
    yield
    mail.arrived(n, p2.at[0], D)
    add(part.at[up, 0:H], p2.at[0])
    mail.go(n + 4, part.at[up, 0:H], p1.at[0, 0:H], U)
    mail.arrived(n + 1, p2.at[1], U)
    add(part.at[down, H:ROWS], p2.at[1])
    mail.go(n + 5, part.at[down, H:ROWS], p1.at[1, H:ROWS], D)
    yield
    mail.arrived(n + 2, p1.at[0, H:ROWS], D)
    mail.arrived(n + 5, p1.at[1, H:ROWS], U)
    out(H, ROWS, val(part.at[y, H:ROWS]) + val(p1.at[0, H:ROWS]) + val(p1.at[1, H:ROWS]))
    mail.arrived(n + 3, p1.at[1, 0:H], U)
    mail.arrived(n + 4, p1.at[0, 0:H], D)
    out(0, H, val(part.at[y, 0:H]) + val(p1.at[0, 0:H]) + val(p1.at[1, 0:H]))


def val(ref):
    return ref[...].astype(WIDE)


def add(dst, src):
    dst[...] = (val(dst) + val(src)).astype(LOW)


def swap_seq(me, mail, own_ref, all_ref, lo, hi):
    n = mail.slots(7)
    for k in range(1, 8):
        to = (me.seq + k) % 8
        mail.go(n + k - 1, own_ref.at[to, :, lo:hi], all_ref.at[me.seq, me.dp, :, lo:hi], {"seq": to})
    yield
    for k in range(1, 8):
        came = (me.seq + 8 - k) % 8
        mail.arrived(n + k - 1, all_ref.at[came, me.dp, :, lo:hi], me.x_dev)


def gather_dp(me, mail, ref):
    z, h = me.z, me.h
    n = mail.slots(19)
    HD, ZU, ZD, TW = me.h_dev, me.z_up_dev, me.z_down_dev, me.twin_dev

    def at(zz, hh, half=None, twin=False):
        d = me.member(zz, hh, twin)
        return ref.at[:, d] if half is None else ref.at[4 * half : 4 * half + 4, d]

    def fwd(i, r, dev):
        mail.go(n + i, r, r, dev)

    def got(i, r):
        mail.arrived(n + i, r, TW)

    hs = (h, 1 - h)
    fwd(0, at(z, h), HD)
    fwd(1, at(z, h), ZU)
    fwd(2, at(z, h), ZD)
    fwd(9, at(z, h), TW)
    yield
    got(0, at(z, 1 - h))
    fwd(3, at(z, 1 - h), ZU)
    fwd(4, at(z, 1 - h), ZD)
    fwd(10, at(z, 1 - h), TW)
    yield
    for k in range(2):
        got(1 + 2 * k, at(me.z_down, hs[k]))
        fwd(5 + 2 * k, at(me.z_down, hs[k], 0), ZU)
        fwd(11 + 2 * k, at(me.z_down, hs[k]), TW)
        yield
        got(2 + 2 * k, at(me.z_up, hs[k]))
        fwd(6 + 2 * k, at(me.z_up, hs[k], 1), ZD)
        fwd(12 + 2 * k, at(me.z_up, hs[k]), TW)
        yield
    for k in range(2):
        got(5 + 2 * k, at(me.z_far, hs[k], 0))
        fwd(15 + 2 * k, at(me.z_far, hs[k], 0), TW)
        got(6 + 2 * k, at(me.z_far, hs[k], 1))
        fwd(16 + 2 * k, at(me.z_far, hs[k], 1), TW)
        yield
    got(9, at(z, h, twin=True))
    got(10, at(z, 1 - h, twin=True))
    for k in range(2):
        got(11 + 2 * k, at(me.z_down, hs[k], twin=True))
        got(12 + 2 * k, at(me.z_up, hs[k], twin=True))
        got(15 + 2 * k, at(me.z_far, hs[k], 0, twin=True))
        got(16 + 2 * k, at(me.z_far, hs[k], 1, twin=True))


def swap_y(me, mail, own_ref, all_ref):
    n = mail.slots(3)
    for k in (2, 1, 3):
        to = (me.y + k) % 4
        mail.go(n + k - 1, own_ref.at[to], all_ref.at[me.seq, me.dp], {"seq": me.a * 4 + to})
    yield
    for k in (1, 3, 2):
        came = me.a * 4 + (me.y + 4 - k) % 4
        mail.arrived(n + k - 1, all_ref.at[came, me.dp], me.up_dev)


def slab(me, ref, x, z, half=None, twin=False):
    d = me.member(z, x // 2, twin)
    first = x % 2 * 4
    return ref.at[pl.ds(first, 4), d] if half is None else ref.at[pl.ds(first + 2 * half, 2), d]


def gather_xz(me, mail, ref):
    n = mail.slots(36)
    XU, XD, ZU, ZD, TW = me.x_up_dev, me.x_down_dev, me.z_up_dev, me.z_down_dev, me.twin_dev
    z, zu, zd, zf = me.z, me.z_up, me.z_down, me.z_far
    xs = (me.x, me.x_down, me.x_up, me.x_far)

    def at(x, zz, half=None, twin=False):
        return slab(me, ref, x, zz, half, twin)

    def fwd(i, r, dev):
        mail.go(n + i, r, r, dev)

    def got(i, r):
        mail.arrived(n + i, r, TW)

    def z_first(k):
        fwd(4 + 4 * k, at(xs[k], z), ZU)
        fwd(5 + 4 * k, at(xs[k], z), ZD)
        fwd(20 + 4 * k, at(xs[k], z), TW)

    def z_second(k):
        got(4 + 4 * k, at(xs[k], zd))
        fwd(6 + 4 * k, at(xs[k], zd, 0), ZU)
        fwd(21 + 4 * k, at(xs[k], zd), TW)
        got(5 + 4 * k, at(xs[k], zu))
        fwd(7 + 4 * k, at(xs[k], zu, 1), ZD)
        fwd(22 + 4 * k, at(xs[k], zu), TW)

    def z_third(k):
        got(6 + 4 * k, at(xs[k], zf, 0))
        got(7 + 4 * k, at(xs[k], zf, 1))
        fwd(23 + 4 * k, at(xs[k], zf), TW)

    fwd(0, at(me.x, z), XU)
    fwd(1, at(me.x, z), XD)
    z_first(0)
    yield
    got(0, at(me.x_down, z))
    fwd(2, at(me.x_down, z, 0), XU)
    got(1, at(me.x_up, z))
    fwd(3, at(me.x_up, z, 1), XD)
    z_first(1)
    z_first(2)
    yield
    z_second(0)
    yield
    got(2, at(me.x_far, z, 0))
    got(3, at(me.x_far, z, 1))
    z_first(3)
    yield
    z_second(1)
    yield
    z_third(0)
    z_second(2)
    yield
    z_third(1)
    yield
    z_second(3)
    z_third(2)
    yield
    z_third(3)
    yield
    for k in range(4):
        for i, zz in enumerate((z, zd, zu, zf)):
            got(20 + 4 * k + i, at(xs[k], zz, twin=True))


def add_slabs(dst, *sources):
    def one(i, carry):
        total = val(dst.at[i])
        for source in sources:
            total = total + val(source.at[i])
        dst[i] = total.astype(LOW)
        return carry

    lax.fori_loop(0, dst.shape[0], one, 0)


def halved(ref, half):
    k = ref.shape[0] // 2
    return ref.at[half * k : half * k + k]


class RingSum:
    def __init__(self, mail, at, places, devices, over, near):
        self.mail, self.at, self.places, self.devices = mail, at, places, devices
        self.over, self.near = over, near
        self.n = mail.slots(6)

    def first(self):
        own, up, down, far = self.places
        U, D = self.devices
        go, n = self.mail.go, self.n
        go(n, halved(self.at(far), 0), self.over.at[0], U)
        go(n + 1, halved(self.at(far), 1), self.over.at[1], D)
        go(n + 2, halved(self.at(up), 1), halved(self.near.at[0], 1), U)
        go(n + 3, halved(self.at(down), 0), halved(self.near.at[1], 0), D)

    def second(self):
        own, up, down, far = self.places
        U, D = self.devices
        go, got, n = self.mail.go, self.mail.arrived, self.n
        got(n, self.over.at[0], D)
        add_slabs(halved(self.at(up), 0), self.over.at[0])
        go(n + 4, halved(self.at(up), 0), halved(self.near.at[0], 0), U)
        got(n + 1, self.over.at[1], U)
        add_slabs(halved(self.at(down), 1), self.over.at[1])
        go(n + 5, halved(self.at(down), 1), halved(self.near.at[1], 1), D)

    def third(self):
        own = self.places[0]
        U, D = self.devices
        got, n = self.mail.arrived, self.n
        got(n + 2, halved(self.near.at[0], 1), D)
        got(n + 3, halved(self.near.at[1], 0), U)
        got(n + 4, halved(self.near.at[0], 0), D)
        got(n + 5, halved(self.near.at[1], 1), U)
        add_slabs(self.at(own), self.near.at[0], self.near.at[1])


def twin_sum(me, mail, stage, acc, order, product, kept=None):
    slots = stage.shape[0]
    n = mail.slots(len(order))

    def settle(i):
        mail.arrived(n + i, acc.at[order[i]], me.twin_dev)
        add_slabs(acc.at[order[i]], stage.at[i % slots, :, me.core])
        if kept is not None:
            kept(i)

    for i, s in enumerate(order):
        if i >= slots:
            mail.sent(n + i - slots)
        product(s, stage.at[i % slots])
        mail.go(n + i, stage.at[i % slots, :, 1 - me.core], acc.at[s], me.twin_dev)
        if i > 0:
            settle(i - 1)
        yield
    settle(len(order) - 1)
    for i in range(max(0, len(order) - slots), len(order)):
        mail.sent(n + i)


def scatter_xz(me, mail, acc, z_over, z_near, x_over, x_near):
    xs = (me.x_far, me.x, me.x_up, me.x_down)
    zs = (me.z, me.z_up, me.z_down, me.z_far)
    XU, XD, ZU, ZD = me.x_up_dev, me.x_down_dev, me.z_up_dev, me.z_down_dev

    def at(x):
        return lambda z: acc.at[pl.ds(x % 2 * 4, 4), z * 2 + x // 2]

    rings = [RingSum(mail, at(x), zs, (ZU, ZD), z_over.at[k], z_near.at[k]) for k, x in enumerate(xs)]
    ring = RingSum(mail, lambda x: at(x)(me.z), (me.x, me.x_up, me.x_down, me.x_far), (XU, XD), x_over, x_near)
    rings[0].first()
    yield
    rings[2].first()
    rings[3].first()
    rings[1].first()
    yield
    for k in (0, 2, 3, 1):
        rings[k].second()
        yield
    for k in (0, 2, 3):
        rings[k].third()
        yield
    ring.first()
    yield
    rings[1].third()
    yield
    ring.second()
    yield
    ring.third()


def scatter_hz(me, mail, acc, z_over, z_near, h_near):
    hs = (1 - me.h, me.h)
    zs = (me.z, me.z_up, me.z_down, me.z_far)

    def at(h):
        return lambda z: acc.at[:, z * 2 + h]

    rings = [RingSum(mail, at(h), zs, (me.z_up_dev, me.z_down_dev), z_over.at[k], z_near.at[k]) for k, h in enumerate(hs)]
    n = mail.slots(1)
    rings[0].first()
    rings[1].first()
    yield
    for k in range(2):
        rings[k].second()
        yield
    rings[0].third()
    mail.go(n, at(1 - me.h)(me.z), h_near, me.h_dev)
    yield
    rings[1].third()
    yield
    mail.arrived(n, h_near, me.h_dev)
    add_slabs(at(me.h)(me.z), h_near)


def send_y(me, mail, slab, result):
    n = mail.slots(3)
    for k in (2, 1, 3):
        to = (me.y + k) % 4
        mail.go(n + k - 1, slab.at[to], result.at[me.y], {"seq": me.a * 4 + to})
    result[me.y] = slab[me.y]
    yield
    for k in (1, 3, 2):
        mail.arrived(n + k - 1, result.at[(me.y + 4 - k) % 4], me.up_dev)


def send_seq(me, mail, slab, result, lo, hi):
    n = mail.slots(7)
    for k in range(1, 8):
        to = (me.seq + k) % 8
        mail.go(n + k - 1, slab.at[to, :, lo:hi], result.at[me.seq], {"seq": to})
    result[me.seq] = slab[me.seq, :, lo:hi]
    yield
    for k in range(1, 8):
        mail.arrived(n + k - 1, result.at[(me.seq + 8 - k) % 8], me.x_dev)


def scatter_bufs():
    late = ROWS - FIRST
    shapes = ((4, late, MODEL), (2, late, MID), (2, late, MODEL), (4, FIRST, MID), (4, FIRST, MODEL), (1, FIRST, MODEL))
    return [pltpu.VMEM(shape, LOW) for shape in shapes]


def scatter_seq(me, mail, part, bufs, out):
    a, b, y, up, down, far = me.a, me.b, me.y, me.up, me.down, me.far
    XP, U, D = me.x_dev, me.up_dev, me.down_dev
    qx, q2, q1, p2, p1, px = bufs
    n = mail.slots(23)
    halves = (pl.ds(0, MID), pl.ds(MID, MID))

    def go(i, src, dst, dev):
        mail.go(n + i, src, dst, dev)

    def got(i, dst):
        mail.arrived(n + i, dst, XP)

    def at(col, row, rows, half=None):
        lo, hi = ((0, FIRST), (FIRST, ROWS))[rows]
        ref = part.at[col * 4 + row]
        return ref.at[lo:hi] if half is None else ref.at[lo:hi, halves[half]]

    def lane(ref, k, half):
        return ref.at[k, :, halves[half]]

    for k, row in enumerate((far, down, up, y)):
        go(k, at(b, row, 1), qx.at[row], XP)
    cols = (b, a)

    def p_first(k):
        c, s = cols[k], 10 + 6 * k
        go(s, at(c, far, 0, 0), p2.at[2 * k], U)
        go(s + 1, at(c, far, 0, 1), p2.at[2 * k + 1], D)
        go(s + 2, at(c, up, 0, 1), lane(p1, 2 * k, 1), U)
        go(s + 3, at(c, down, 0, 0), lane(p1, 2 * k + 1, 0), D)

    def p_second(k):
        c, s = cols[k], 10 + 6 * k
        got(s, p2.at[2 * k])
        add(at(c, up, 0, 0), p2.at[2 * k])
        go(s + 4, at(c, up, 0, 0), lane(p1, 2 * k, 0), U)
        got(s + 1, p2.at[2 * k + 1])
        add(at(c, down, 0, 1), p2.at[2 * k + 1])
        go(s + 5, at(c, down, 0, 1), lane(p1, 2 * k + 1, 1), D)

    def p_third(k):
        s = 10 + 6 * k
        got(s + 2, lane(p1, 2 * k, 1))
        got(s + 3, lane(p1, 2 * k + 1, 0))
        got(s + 4, lane(p1, 2 * k, 0))
        got(s + 5, lane(p1, 2 * k + 1, 1))
        return val(at(cols[k], y, 0)) + val(p1.at[2 * k]) + val(p1.at[2 * k + 1])

    p_first(0)
    yield
    p_first(1)
    yield
    got(0, qx.at[far])
    add(at(a, far, 1), qx.at[far])
    go(4, at(a, far, 1, 0), q2.at[0], U)
    go(5, at(a, far, 1, 1), q2.at[1], D)
    yield
    p_second(0)
    yield
    got(1, qx.at[down])
    add(at(a, down, 1), qx.at[down])
    go(6, at(a, down, 1, 0), lane(q1, 1, 0), D)
    got(2, qx.at[up])
    add(at(a, up, 1), qx.at[up])
    go(7, at(a, up, 1, 1), lane(q1, 0, 1), U)
    yield
    p_second(1)
    yield
    rows = p_third(0)
    own = at(b, y, 0)
    own[...] = rows.astype(LOW)
    go(22, own, px.at[0], XP)
    yield
    got(4, q2.at[0])
    add(at(a, up, 1, 0), q2.at[0])
    go(8, at(a, up, 1, 0), lane(q1, 0, 0), U)
    got(5, q2.at[1])
    add(at(a, down, 1, 1), q2.at[1])
    go(9, at(a, down, 1, 1), lane(q1, 1, 1), D)
    yield
    rows = p_third(1)
    got(22, px.at[0])
    out(0, FIRST, rows + val(px.at[0]))
    yield
    got(3, qx.at[y])
    got(6, lane(q1, 1, 0))
    got(7, lane(q1, 0, 1))
    got(8, lane(q1, 0, 0))
    got(9, lane(q1, 1, 1))
    out(FIRST, ROWS, val(at(a, y, 1)) + val(qx.at[y]) + val(q1.at[0]) + val(q1.at[1]))


def run(*tasks):
    tasks = list(tasks)
    while tasks:
        for task in list(tasks):
            if next(task, tasks) is tasks:
                tasks.remove(task)


def step(task):
    return next(task, None)
def dot(a, b, dims=((1,), (0,))):
    return lax.dot_general(a, b, (dims, ((), ())), preferred_element_type=WIDE)


def row_scale(values):
    return lax.rsqrt(jnp.mean(values * values, axis=-1, keepdims=True) + EPS)


def front_kernel(
    x_ref, live_ref, cot_ref, wa_own, wm_own, pos_q, pos_k,
    one_out, wa_out, grad_all, wm, qkv_out, probs_out, att_out, resid, two,
    one_all, wa, grad_own, qkv, probs, att, part, qx, q2, q1, p2, p1, px, send, recv, local_sem,
):
    me = Place()
    mail = Mail(send, recv)
    saves = []

    def save(src, dst):
        copy = pltpu.make_async_copy(src, dst, local_sem.at[len(saves)])
        copy.start()
        saves.append(copy)
        return copy

    enter(me.peers() + [me.h_dev, me.z_up_dev, me.z_down_dev, me.twin_dev, me.x_up_dev, me.x_down_dev])
    swap_a = swap_seq(me, mail, wa_own, wa, 0, PROJ)
    step(swap_a)
    swap_m = swap_y(me, mail, wm_own, wm)
    step(swap_m)
    keep_m = save(wm_own.at[me.y], wm.at[me.seq, me.dp])
    x = x_ref[...].astype(WIDE)
    one_all[me.seq] = (x * row_scale(x) * live_ref[...]).astype(LOW)
    gather_one = gather_seq(me, mail, one_all.at[me.seq], one_all)
    step(gather_one)
    wa[pl.ds(me.seq, 1), pl.ds(me.dp, 1), :, 0:PROJ] = wa_own[pl.ds(me.seq, 1), :, 0:PROJ][None]
    for k in range(8):
        wa[k, pl.ds(me.dp, 1), :, PROJ:] = wa_own[k, :, PROJ:][None]
    step(swap_a)
    gather_wa = gather_dp(me, mail, wa)
    step(gather_wa)
    step(swap_m)
    keep_m.wait()
    gather_wm = gather_xz(me, mail, wm)
    step(gather_wm)
    grad_own[...] = (cot_ref[...].astype(WIDE) * live_ref[...]).astype(LOW)
    save(grad_own, grad_all.at[me.y])
    for i in range(8):
        step(gather_one)
        step(gather_wa)
        if i in (2, 4, 6):
            step(gather_wm)
    run(gather_one, gather_wa)
    gather_g = gather_y(me, mail, grad_own, grad_all)
    step(gather_g)
    save(one_all, one_out)
    save(wa, wa_out)

    def project(i, carry):
        rows = one_all[pl.ds(i * 2, 2)].reshape(2 * ROWS, MODEL)
        weight = wa[:, :, :, 0:PROJ].reshape(MODEL, PROJ)
        qkv[pl.ds(pl.multiple_of(i * 256, 256), 256), :] = dot(rows, weight).astype(LOW)
        return carry

    def attend(i, carry):
        first = pl.multiple_of(i * ROWS, ROWS)
        rows = pl.ds(first, ROWS)
        allowed = pos_k[...] <= pos_q[rows, :]
        for head in range(2):
            lo, hi = head * HEAD_DIM, (head + 1) * HEAD_DIM
            q = qkv[rows, lo:hi]
            k = qkv[:, PART + lo : PART + hi]
            v = qkv[:, 2 * PART + lo : 2 * PART + hi]
            scores = dot(q, k, ((1,), (1,))) * (1.0 / math.sqrt(HEAD_DIM)) - math.log(8 * ROWS)
            p = jnp.where(allowed, 1.0 / (1.0 + jnp.exp(-scores)), 0.0).astype(LOW)
            probs[head, rows, :] = p
            att[rows, lo:hi] = dot(p, v).astype(LOW)
        return carry

    def out_project(col):
        rows = att[pl.ds(pl.multiple_of(col * 512, 512), 512), :]

        def piece(k, carry):
            weight = wa[k, :, :, PROJ:].reshape(PART, PART)
            columns = pl.ds(pl.multiple_of(k * PART, PART), PART)
            part[pl.ds(col * 4, 4), :, columns] = dot(rows, weight).reshape(4, ROWS, PART).astype(LOW)
            return carry

        lax.fori_loop(0, 8, piece, 0)

    for i in range(2):
        lax.fori_loop(2 * i, 2 * i + 2, project, 0)
        step(gather_g)
        step(gather_wm)
    save(qkv, qkv_out)

    def write(lo, hi, rows):
        total = x_ref[lo:hi].astype(WIDE) + rows
        resid[lo:hi] = total
        two[lo:hi] = (total * row_scale(total) * live_ref[lo:hi]).astype(LOW)

    scatter = scatter_seq(me, mail, part, (qx, q2, q1, p2, p1, px), write)
    for col in (me.b, me.a):
        for i in range(2):
            lax.fori_loop(col * 4 + 2 * i, col * 4 + 2 * i + 2, attend, 0)
            step(gather_wm)
            step(gather_g)
        out_project(col)
        step(scatter)
    save(probs, probs_out)
    save(att, att_out)
    run(scatter, gather_wm, gather_g)
    for copy in saves:
        if copy is not keep_m:
            copy.wait()
    mail.finish()


def front(x, live, cot, wa_own, wm_own, pos):
    vmem, anywhere = pl.BlockSpec(memory_space=pltpu.VMEM), pl.BlockSpec(memory_space=pl.ANY)
    shape = jax.ShapeDtypeStruct
    count = 7 + 18 + 19 + 3 + 36 + 4 + 23
    return pl.pallas_call(
        front_kernel,
        out_shape=(
            shape((8, ROWS, MODEL), LOW), shape((8, 16, 16, 1024), LOW), shape((4, ROWS, MODEL), LOW),
            shape((8, 16, 16, SLAB), LOW), shape((1024, PROJ), LOW), shape((2, 1024, 1024), LOW),
            shape((1024, PART), LOW), shape((ROWS, MODEL), WIDE), shape((ROWS, MODEL), LOW),
        ),
        in_specs=[vmem] * 4 + [anywhere] + [vmem] * 2,
        out_specs=(anywhere,) * 7 + (vmem, vmem),
        scratch_shapes=[
            pltpu.VMEM((8, ROWS, MODEL), LOW), pltpu.VMEM((8, 16, 16, 1024), LOW), pltpu.VMEM((ROWS, MODEL), LOW),
            pltpu.VMEM((1024, PROJ), LOW), pltpu.VMEM((2, 1024, 1024), LOW), pltpu.VMEM((1024, PART), LOW),
            pltpu.VMEM((8, ROWS, MODEL), LOW),
        ]
        + scatter_bufs()
        + [pltpu.SemaphoreType.DMA((count,)), pltpu.SemaphoreType.DMA((count,)), pltpu.SemaphoreType.DMA((8,))],
        compiler_params=pltpu.CompilerParams(collective_id=1, has_side_effects=True, vmem_limit_bytes=56 * 2**20),
        name="front",
    )(x, live, cot, wa_own, wm_own, pos[:, None], pos[None, :])
def mlp_kernel(
    two_ref, resid, cot_ref, live_ref, grad_all, wm_all,
    acc_out, branch_out, grad_resid, grad_branch,
    wm, grads, twos, hidden, pair, part, branch, p2, p1,
    stage, acc, send, recv, local_sem,
):
    me = Place()
    mail = Mail(send, recv)
    saves = []

    def save(src, dst):
        copy = pltpu.make_async_copy(src, dst, local_sem.at[len(saves)])
        copy.start()
        saves.append(copy)
        return copy

    load_w = save(wm_all, wm)
    load_g = save(grad_all, grads)
    enter([me.up_dev, me.down_dev, me.twin_dev])
    twos[me.y] = two_ref[...]
    gather = gather_y(me, mail, twos.at[me.y], twos)
    step(gather)
    load_w.wait()
    load_g.wait()

    def rows_of(ref, blocks):
        return jnp.concatenate([ref[k] for k in blocks], axis=0)

    def put(ref, blocks, columns, values):
        for i, k in enumerate(blocks):
            ref[k, :, columns] = values[i * ROWS : (i + 1) * ROWS].astype(LOW)

    def hidden_tile(blocks, j, wide):
        start = j * 128
        if not isinstance(j, int):
            start = pl.multiple_of(start, 128)
        width = wide * 128
        weight = wm[:, :, :, pl.ds(2 * start, 2 * width)].reshape(MODEL, 2 * width)
        gate_up = dot(rows_of(twos, blocks), weight)
        down = wm[:, :, :, pl.ds(PAIR + start, width)].reshape(MODEL, width)
        grad_hidden = dot(rows_of(grads, blocks), down)
        low, pairs = [], []
        for i in range(wide):
            gate = gate_up[:, i * 256 : i * 256 + 128]
            up = gate_up[:, i * 256 + 128 : i * 256 + 256]
            back = grad_hidden[:, i * 128 : i * 128 + 128]
            squashed = 1.0 / (1.0 + jnp.exp(-gate))
            active = gate * squashed
            low.append(active * up)
            pairs.append(back * up * (squashed * (1.0 + gate * (1.0 - squashed))))
            pairs.append(back * active)
        put(hidden, blocks, pl.ds(start, width), jnp.concatenate(low, axis=1))
        put(pair, blocks, pl.ds(2 * start, 2 * width), jnp.concatenate(pairs, axis=1))

    def ahead(blocks):
        def tile(j, carry):
            hidden_tile(blocks, 2 * j, 2)
            return carry

        lax.fori_loop(0, 5, tile, 0)
        hidden_tile(blocks, 10, 1)

    def back(blocks):
        def tile(s, carry):
            columns = pl.ds(pl.multiple_of(s * 256, 256), 256)
            weight = wm[s, :, :, 0:PAIR].reshape(256, PAIR)
            put(part, blocks, columns, dot(rows_of(pair, blocks), weight, ((1,), (1,))))
            return carry

        lax.fori_loop(0, 8, tile, 0)

    def down_back(blocks):
        def tile(s, carry):
            columns = pl.ds(pl.multiple_of(s * 256, 256), 256)
            weight = wm[s, :, :, PAIR:].reshape(256, UNITS)
            put(branch, blocks, columns, dot(rows_of(hidden, blocks), weight, ((1,), (1,))))
            return carry

        lax.fori_loop(0, 8, tile, 0)

    def write(lo, hi, rows):
        x = resid[lo:hi]
        scale = row_scale(x)
        hat = x * scale
        inner = jnp.mean(rows * hat, axis=-1, keepdims=True)
        total = cot_ref[lo:hi].astype(WIDE) * live_ref[lo:hi] + scale * (rows - hat * inner)
        grad_resid[lo:hi] = total
        grad_branch[lo:hi] = total.astype(LOW)

    scatter = scatter_y(me, mail, part, p2, p1, write)
    ahead([me.y])
    step(gather)
    ahead([me.up, me.down])
    back([me.up, me.down])
    step(scatter)
    step(gather)
    ahead([me.far])
    back([me.far])
    step(scatter)
    back([me.y])
    step(scatter)
    order = [me.a * 4 + i for i in range(4)] + [me.b * 4 + i for i in range(4)]

    def product(s, out):
        columns = pl.ds(pl.multiple_of(s * 256, 256), 256)
        rows = twos[:, :, columns].reshape(4 * ROWS, 256).T
        terms = dot(rows, pair[...].reshape(4 * ROWS, PAIR))
        out[:, :, :, 0:PAIR] = terms.reshape(8, 2, 16, PAIR).astype(LOW)
        rows = grads[:, :, columns].reshape(4 * ROWS, 256).T
        terms = dot(rows, hidden[...].reshape(4 * ROWS, UNITS))
        out[:, :, :, PAIR:] = terms.reshape(8, 2, 16, UNITS).astype(LOW)

    def kept(i):
        save(acc.at[order[i]], acc_out.at[order[i]])

    twin = twin_sum(me, mail, stage, acc, order, product, kept)
    for i in range(3):
        step(twin)
    step(scatter)
    for i in range(3):
        step(twin)
    step(scatter)
    run(twin)
    down_back([me.y, me.up, me.down, me.far])
    save(branch, branch_out)
    run(scatter, gather)
    for copy in saves[2:]:
        copy.wait()
    mail.finish()


def mlp(two, resid, cot, live, grad_all, wm):
    vmem, anywhere = pl.BlockSpec(memory_space=pltpu.VMEM), pl.BlockSpec(memory_space=pl.ANY)
    shape = jax.ShapeDtypeStruct
    blocks = (4, ROWS, MODEL)
    return pl.pallas_call(
        mlp_kernel,
        out_shape=(
            shape((8, 8, 16, SLAB), LOW), shape(blocks, LOW), shape((ROWS, MODEL), WIDE), shape((ROWS, MODEL), LOW),
        ),
        in_specs=[vmem] * 4 + [anywhere] * 2,
        out_specs=(anywhere,) * 2 + (vmem,) * 2,
        scratch_shapes=[
            pltpu.VMEM((8, 16, 16, SLAB), LOW), pltpu.VMEM(blocks, LOW), pltpu.VMEM(blocks, LOW),
            pltpu.VMEM((4, ROWS, UNITS), LOW), pltpu.VMEM((4, ROWS, PAIR), LOW), pltpu.VMEM(blocks, LOW),
            pltpu.VMEM(blocks, LOW), pltpu.VMEM((2, ROWS // 2, MODEL), LOW), pltpu.VMEM((2, ROWS, MODEL), LOW),
            pltpu.VMEM((2, 8, 2, 16, SLAB), LOW), pltpu.VMEM((8, 8, 16, SLAB), LOW),
            pltpu.SemaphoreType.DMA((18,)), pltpu.SemaphoreType.DMA((18,)), pltpu.SemaphoreType.DMA((11,)),
        ],
        compiler_params=pltpu.CompilerParams(collective_id=2, has_side_effects=True, vmem_limit_bytes=62 * 2**20),
        name="mlp",
    )(two, resid, cot, live, grad_all, wm)
def back_kernel(
    branch_grad, grad_resid, x_ref, live_ref, resid, branch_all, acc_all, one_all, wa_all, qkv_all, probs_all, att_all,
    layer_out, input_grad, slab_own, in_own, out_own,
    acc, z_over, z_near, x_over, x_near, grads, part, qx, q2, q1, p2, p1, px,
    wa, acc_a, az_over, az_near, h_near, ones, qkv, probs, att, grad_att, grad_proj, grad_k, grad_v, stage_a,
    send, recv, local_sem,
):
    me = Place()
    mail = Mail(send, recv)
    loads = []

    def load(src, dst):
        copy = pltpu.make_async_copy(src, dst, local_sem.at[len(loads)])
        copy.start()
        loads.append(copy)
        return copy

    load_acc = [load(acc_all.at[pl.ds(col * 4, 4)], acc.at[pl.ds(col * 4, 4)]) for col in (me.a, me.b)]
    enter(me.peers() + [me.h_dev, me.z_up_dev, me.z_down_dev, me.x_up_dev, me.x_down_dev, me.twin_dev])
    grads[me.seq] = branch_grad[...]
    gather = gather_seq(me, mail, grads.at[me.seq], grads)
    step(gather)
    load_wa = load(wa_all, wa)
    load_branch = load(branch_all, part.at[0:4])
    waits = [load(*both) for both in ((qkv_all, qkv), (att_all, att), (one_all, ones))]
    fetch = [load(probs_all.at[:, 256 * i : 256 * i + 256], probs.at[i]) for i in range(2)]
    order = [me.a * 4 + i for i in range(4)] + [me.b * 4 + i for i in range(4)]

    def columns_of(s, width=256):
        return pl.ds(pl.multiple_of(s * width, width), width)

    def slab_sums():
        yield from scatter_xz(me, mail, acc, z_over, z_near, x_over, x_near)
        yield from send_y(me, mail, acc.at[pl.ds(me.a * 4, 4), me.z * 2 + me.h], slab_own)

    sums = slab_sums()

    load_acc[0].wait()
    step(sums)
    load_acc[1].wait()
    step(sums)
    for i in range(3):
        step(gather)
        step(sums)

    def write_out(lo, hi, rows):
        layer_out[lo:hi] = (live_ref[lo:hi] * (resid[lo:hi] + rows)).astype(LOW)

    def write_grad(lo, hi, rows):
        x = x_ref[lo:hi].astype(WIDE)
        scale = row_scale(x)
        hat = x * scale
        inner = jnp.mean(rows * hat, axis=-1, keepdims=True)
        input_grad[lo:hi] = grad_resid[lo:hi] + live_ref[lo:hi] * scale * (rows - hat * inner)

    class Lower:
        at = {0: part.at[6, 0 : ROWS // 2], 1: part.at[6, ROWS // 2 : ROWS]}

    out_sum = scatter_y(me, mail, part.at[0:4], Lower, part.at[4:6], write_out)
    grad_sum = scatter_seq(me, mail, part, (qx, q2, q1, p2, p1, px), write_grad)

    run(gather)
    load_branch.wait()
    out_slots = range(mail.count, mail.count + 6)
    step(out_sum)
    load_wa.wait()
    for wait in waits:
        wait.wait()
    head_scale = 1.0 / math.sqrt(HEAD_DIM)

    def attended_grad(i, carry):
        total = jnp.zeros((256, PART), WIDE)
        for k in range(8):
            rows = grads[pl.ds(i * 2, 2), :, k * PART : k * PART + PART].reshape(256, PART)
            total = total + dot(rows, wa[k, :, :, PROJ:].reshape(PART, PART), ((1,), (1,)))
        grad_att[columns_of(i), :] = total.astype(LOW)
        return carry

    lax.fori_loop(0, 4, attended_grad, 0)
    step(out_sum)
    step(sums)
    grad_k[...] = jnp.zeros_like(grad_k)
    grad_v[...] = jnp.zeros_like(grad_v)

    def attend_back(i):
        rows = pl.ds(256 * i, 256)
        for head in range(2):
            lo, hi = head * HEAD_DIM, (head + 1) * HEAD_DIM
            low = probs[i % 2, head]
            p = low.astype(WIDE)
            g = grad_att[rows, lo:hi]
            back = dot(g, qkv[:, 2 * PART + lo : 2 * PART + hi], ((1,), (1,)))
            grad_s = (back * (p * (1.0 - p))).astype(LOW)
            grad_q = dot(grad_s, qkv[:, PART + lo : PART + hi]) * head_scale
            grad_proj[rows, lo:hi] = grad_q.astype(LOW)
            grad_v[:, lo:hi] += dot(low, g, ((0,), (0,)))
            grad_k[:, lo:hi] += dot(grad_s, qkv[rows, lo:hi], ((0,), (0,)))

    for i in range(4):
        fetch[i].wait()
        attend_back(i)
        if i < 2:
            fetch.append(load(probs_all.at[:, 256 * i + 512 : 256 * i + 768], probs.at[i]))
        step(sums)
        step(out_sum)
    run(out_sum)
    for slot in out_slots:
        mail.sent(slot)
    grad_proj[:, PART : 2 * PART] = (grad_k[...] * head_scale).astype(LOW)
    grad_proj[:, 2 * PART :] = grad_v[...].astype(LOW)

    def norm_terms(col):
        rows = grad_proj[columns_of(col, 512), :]

        def piece(s, carry):
            weight = wa[s, :, :, 0:PROJ].reshape(256, PROJ)
            terms = dot(rows, weight, ((1,), (1,)))
            part[pl.ds(col * 4, 4), :, columns_of(s)] = terms.reshape(4, ROWS, 256).astype(LOW)
            return carry

        lax.fori_loop(0, 8, piece, 0)

    def product(s, out):
        rows = ones[:, :, columns_of(s)].reshape(8 * ROWS, 256).T
        terms = dot(rows, grad_proj[...])
        out[:, :, :, 0:PROJ] = terms.reshape(8, 2, 16, PROJ).astype(LOW)
        rows = grads[:, :, columns_of(s)].reshape(8 * ROWS, 256)
        terms = dot(att[...], rows, ((0,), (0,)))
        out[:, :, :, PROJ:] = terms.reshape(8, 2, 16, PART).astype(LOW)

    twin = twin_sum(me, mail, stage_a, acc_a, order, product)
    norm_terms(me.b)
    step(grad_sum)
    for i in range(9):
        step(twin)
    norm_terms(me.a)
    step(grad_sum)
    step(sums)

    def proj_sums():
        yield from scatter_hz(me, mail, acc_a, az_over, az_near, h_near)
        own = acc_a.at[:, me.z * 2 + me.h]
        out_own[...] = own[:, :, PROJ:]
        yield from send_seq(me, mail, own, in_own, 0, PROJ)

    run(proj_sums(), grad_sum, sums)

    mail.finish()


def back(branch_grad, grad_resid, x, live, resid, branch, acc, ones, wa, qkv, probs, att):
    vmem, anywhere = pl.BlockSpec(memory_space=pltpu.VMEM), pl.BlockSpec(memory_space=pl.ANY)
    shape = jax.ShapeDtypeStruct
    count = 18 + 30 + 3 + 6 + 23 + 8 + 13 + 7
    return pl.pallas_call(
        back_kernel,
        out_shape=(
            shape((ROWS, MODEL), LOW), shape((ROWS, MODEL), WIDE), shape((4, 16, SLAB), LOW),
            shape((8, 16, PROJ), LOW), shape((8, 16, PART), LOW),
        ),
        in_specs=[vmem] * 5 + [anywhere] * 7,
        out_specs=(vmem,) * 5,
        scratch_shapes=[
            pltpu.VMEM((8, 8, 16, SLAB), LOW), pltpu.VMEM((4, 2, 2, 16, SLAB), LOW), pltpu.VMEM((4, 2, 4, 16, SLAB), LOW),
            pltpu.VMEM((2, 2, 16, SLAB), LOW), pltpu.VMEM((2, 4, 16, SLAB), LOW), pltpu.VMEM((8, ROWS, MODEL), LOW),
            pltpu.VMEM((8, ROWS, MODEL), LOW),
        ]
        + scatter_bufs()
        + [
            pltpu.VMEM((8, 16, 16, 1024), LOW), pltpu.VMEM((8, 8, 16, 1024), LOW), pltpu.VMEM((2, 2, 4, 16, 1024), LOW),
            pltpu.VMEM((2, 2, 8, 16, 1024), LOW), pltpu.VMEM((8, 16, 1024), LOW),
            pltpu.VMEM((8, ROWS, MODEL), LOW),
            pltpu.VMEM((1024, PROJ), LOW), pltpu.VMEM((2, 2, 256, 1024), LOW), pltpu.VMEM((1024, PART), LOW),
            pltpu.VMEM((1024, PART), LOW), pltpu.VMEM((1024, PROJ), LOW),
            pltpu.VMEM((1024, PART), WIDE), pltpu.VMEM((1024, PART), WIDE), pltpu.VMEM((2, 8, 2, 16, 1024), LOW),
            pltpu.SemaphoreType.DMA((count,)), pltpu.SemaphoreType.DMA((count,)), pltpu.SemaphoreType.DMA((12,)),
        ],
        compiler_params=pltpu.CompilerParams(collective_id=3, has_side_effects=True, vmem_limit_bytes=62 * 2**20),
        name="back",
    )(branch_grad, grad_resid, x, live, resid, branch, acc, ones, wa, qkv, probs, att)
def weights_out(attn_weight, mlp_weight, gain_one, gain_two):
    proj = (attn_weight[:, :3].astype(WIDE) * gain_one).astype(LOW).reshape(16, 3, 8, PART)
    proj = proj.transpose(2, 0, 1, 3).reshape(8, 16, PROJ)
    out = attn_weight[:, 3].reshape(16, 8, PART).transpose(1, 0, 2)
    units = mlp_weight.shape[2] // 4
    spare = UNITS - units
    pair = (mlp_weight[:, :2].astype(WIDE) * gain_two).astype(LOW).reshape(16, 2, 4, units)
    pair = jnp.pad(pair, ((0, 0), (0, 0), (0, 0), (0, spare))).reshape(16, 2, 4, UNITS // 128, 128)
    pair = pair.transpose(2, 0, 3, 1, 4).reshape(4, 16, PAIR)
    down = jnp.pad(mlp_weight[:, 2].reshape(16, 4, units), ((0, 0), (0, 0), (0, spare))).transpose(1, 0, 2)
    return jnp.concatenate([proj, out], axis=2), jnp.concatenate([pair, down], axis=2)


def weights_back(slab, proj, out, units):
    pair, down = slab[..., :PAIR], slab[..., PAIR:]
    proj = proj.reshape(8, 16, 3, PART).transpose(1, 2, 0, 3).reshape(16, 3, MODEL).astype(WIDE)
    out = out.transpose(1, 0, 2).reshape(16, MODEL).astype(WIDE)
    pair = pair.reshape(4, 16, UNITS // 128, 2, 128).transpose(1, 3, 0, 2, 4).reshape(16, 2, 4, UNITS)
    pair = pair[..., : units // 4].reshape(16, 2, units).astype(WIDE)
    down = down[..., : units // 4].transpose(1, 0, 2).reshape(16, units).astype(WIDE)
    return proj, out, pair, down


def local(
    tokens, valid_counts, block_owner, norm1_gain, attn_weight, norm2_gain, mlp_weight, cotangent
):
    row_index = jnp.arange(ROWS, dtype=jnp.int32)
    live = (row_index < valid_counts[0, 0]).astype(WIDE)[:, None]
    pos = (block_owner[0][:, None] * ROWS + row_index[None]).reshape(-1)
    x, cot = tokens[0], cotangent[0]
    gain_one = norm1_gain.astype(WIDE)[:, None, None]
    gain_two = norm2_gain.astype(WIDE)[:, None, None]
    wa_own, wm_own = weights_out(attn_weight, mlp_weight, gain_one, gain_two)
    ones, wa, grads, wm, qkv, probs, att, resid, two = front(x, live, cot, wa_own, wm_own, pos)
    acc, branch, grad_resid, branch_grad = mlp(two, resid, cot, live, grads, wm)
    layer_out, input_grad, slab_own, in_own, out_own = back(
        branch_grad, grad_resid, x, live, resid, branch, acc, ones, wa, qkv, probs, att
    )
    in_sum, out_sum, pair_sum, down_sum = weights_back(slab_own, in_own, out_own, mlp_weight.shape[2])
    attn_grad = jnp.concatenate([in_sum * gain_one, out_sum[:, None]], axis=1)
    mlp_grad = jnp.concatenate([pair_sum * gain_two, down_sum[:, None]], axis=1)
    gain_one_grad = jnp.sum(in_sum * attn_weight[:, :3].astype(WIDE), axis=(1, 2))
    gain_two_grad = jnp.sum(pair_sum * mlp_weight[:, :2].astype(WIDE), axis=(1, 2))
    return (layer_out[None], input_grad[None], gain_one_grad, attn_grad, gain_two_grad, mlp_grad)


def solution(mesh):
    token_spec = P("dp", "seq", None)
    row_spec = P(("seq", "dp"), None, None)
    gain_spec = P(("seq", "dp"))
    in_specs = (
        token_spec, P("dp", "seq"), P("dp", None), gain_spec, row_spec, gain_spec, row_spec, token_spec
    )
    out_specs = (token_spec, token_spec, gain_spec, row_spec, gain_spec, row_spec)
    return jax.shard_map(local, mesh=mesh, in_specs=in_specs, out_specs=out_specs, check_vma=False)
```

```python
import functools, math
import jax
import jax.numpy as jnp
from jax import lax
from jax.experimental import pallas as pl
from jax.experimental.pallas import tpu as pltpu
from jax.sharding import PartitionSpec as P

LOW = jnp.bfloat16
WIDE = jnp.float32
MESH = pl.DeviceIdType.MESH
EPS = 1e-05
HEAD_DIM = 128
ROWS = 128
MODEL = 2048
PART = 256
PROJ = 3 * PART
UNITS = 1408
SLAB = 3 * UNITS
PAIR = 2 * UNITS
FIRST = 80
MID = MODEL // 2


class Place:
    def __init__(self):
        self.seq, self.dp = lax.axis_index("seq"), lax.axis_index("dp")
        self.a, self.y = self.seq // 4, self.seq % 4
        self.b = 1 - self.a
        self.up, self.down, self.far = (self.y + 1) % 4, (self.y + 3) % 4, (self.y + 2) % 4
        self.z, self.h, self.core = self.dp // 4, self.dp // 2 % 2, self.dp % 2
        self.z_up, self.z_down, self.z_far = (self.z + 1) % 4, (self.z + 3) % 4, (self.z + 2) % 4
        self.x_dev = {"seq": self.b * 4 + self.y}
        self.up_dev = {"seq": self.a * 4 + self.up}
        self.down_dev = {"seq": self.a * 4 + self.down}
        self.h_dev = {"dp": self.member(self.z, 1 - self.h)}
        self.z_up_dev = {"dp": self.member(self.z_up, self.h)}
        self.z_down_dev = {"dp": self.member(self.z_down, self.h)}
        self.twin_dev = {"dp": self.dp + 1 - 2 * self.core}
        self.x = self.h * 2 + self.a
        self.x_up, self.x_down, self.x_far = (self.x + 1) % 4, (self.x + 3) % 4, (self.x + 2) % 4
        self.x_up_dev, self.x_down_dev = self.at_x(self.x_up), self.at_x(self.x_down)

    def member(self, z, h, twin=False):
        core = 1 - self.core if twin else self.core
        return z * 4 + h * 2 + core

    def at_x(self, x):
        return {"seq": x % 2 * 4 + self.y, "dp": self.member(self.z, x // 2)}

    def column(self, twin=False):
        return self.z * 4 + (1 - self.core if twin else self.core)

    def peers(self):
        return [{"seq": (self.seq + k) % 8} for k in range(1, 8)]


def enter(devices):
    barrier = pltpu.get_barrier_semaphore()
    for device in devices:
        pl.semaphore_signal(barrier, inc=1, device_id=device, device_id_type=MESH)
    pl.semaphore_wait(barrier, len(devices))


class Mail:
    def __init__(self, send, recv):
        self.send, self.recv = send, recv
        self.count, self.started = 0, {}

    def slots(self, n):
        first = self.count
        self.count += n
        return first

    def copy(self, slot, src, dst, device):
        return pltpu.make_async_remote_copy(
            src_ref=src, dst_ref=dst, send_sem=self.send.at[slot], recv_sem=self.recv.at[slot],
            device_id=device, device_id_type=MESH,
        )

    def go(self, slot, src, dst, device):
        copy = self.copy(slot, src, dst, device)
        copy.start()
        self.started[slot] = copy

    def arrived(self, slot, dst, device):
        self.copy(slot, dst, dst, device).wait_recv()

    def sent(self, slot):
        self.started.pop(slot).wait_send()

    def finish(self):
        for copy in self.started.values():
            copy.wait_send()


def gather_seq(me, mail, x_ref, out_ref):
    a, b, y, up, down, far = me.a, me.b, me.y, me.up, me.down, me.far
    XP, U, D = me.x_dev, me.up_dev, me.down_dev
    n = mail.slots(18)

    def cut(ref, rows, half):
        lo, hi = ((0, FIRST), (FIRST, ROWS))[rows]
        return ref.at[lo:hi] if half is None else ref.at[lo:hi, half * MID : half * MID + MID]

    def at(col, row, rows, half=None):
        return cut(out_ref.at[col * 4 + row], rows, half)

    def send(i, rows, dev):
        mail.go(n + i, cut(x_ref, rows, None), at(a, y, rows), dev)

    def fwd(i, ref, dev):
        mail.go(n + i, ref, ref, dev)

    def got(i, dst):
        mail.arrived(n + i, dst, XP)

    send(0, 0, XP)
    send(1, 0, U)
    send(2, 0, D)
    send(3, 1, U)
    send(4, 1, D)
    send(5, 1, XP)
    yield
    got(0, at(b, y, 0))
    fwd(6, at(b, y, 0), U)
    fwd(7, at(b, y, 0), D)
    yield
    got(1, at(a, down, 0))
    fwd(8, at(a, down, 0, 0), U)
    got(2, at(a, up, 0))
    fwd(9, at(a, up, 0, 1), D)
    yield
    got(3, at(a, down, 1))
    fwd(10, at(a, down, 1, 0), U)
    fwd(11, at(a, down, 1), XP)
    got(4, at(a, up, 1))
    fwd(12, at(a, up, 1, 1), D)
    fwd(13, at(a, up, 1), XP)
    yield
    got(5, at(b, y, 1))
    got(6, at(b, down, 0))
    fwd(14, at(b, down, 0, 0), U)
    got(7, at(b, up, 0))
    fwd(15, at(b, up, 0, 1), D)
    yield
    got(10, at(a, far, 1, 0))
    fwd(16, at(a, far, 1, 0), XP)
    got(12, at(a, far, 1, 1))
    fwd(17, at(a, far, 1, 1), XP)
    yield
    got(8, at(a, far, 0, 0))
    got(9, at(a, far, 0, 1))
    got(11, at(b, down, 1))
    got(13, at(b, up, 1))
    yield
    got(14, at(b, far, 0, 0))
    got(15, at(b, far, 0, 1))
    got(16, at(b, far, 1, 0))
    got(17, at(b, far, 1, 1))


def gather_y(me, mail, x_ref, out_ref):
    y, up, down, far = me.y, me.up, me.down, me.far
    U, D = me.up_dev, me.down_dev
    n = mail.slots(4)
    H = ROWS // 2
    mail.go(n, x_ref, out_ref.at[y], U)
    mail.go(n + 1, x_ref, out_ref.at[y], D)
    yield
    mail.arrived(n, out_ref.at[down], D)
    mail.go(n + 2, out_ref.at[down, 0:H], out_ref.at[down, 0:H], U)
    mail.arrived(n + 1, out_ref.at[up], U)
    mail.go(n + 3, out_ref.at[up, H:ROWS], out_ref.at[up, H:ROWS], D)
    yield
    mail.arrived(n + 2, out_ref.at[far, 0:H], D)
    mail.arrived(n + 3, out_ref.at[far, H:ROWS], U)


def scatter_y(me, mail, part, p2, p1, out):
    y, up, down, far = me.y, me.up, me.down, me.far
    U, D = me.up_dev, me.down_dev
    n = mail.slots(6)
    H = ROWS // 2
    mail.go(n + 2, part.at[up, H:ROWS], p1.at[0, H:ROWS], U)
    mail.go(n + 3, part.at[down, 0:H], p1.at[1, 0:H], D)
    yield
    mail.go(n, part.at[far, 0:H], p2.at[0], U)
    mail.go(n + 1, part.at[far, H:ROWS], p2.at[1], D)
    yield
    mail.arrived(n, p2.at[0], D)
    add(part.at[up, 0:H], p2.at[0])
    mail.go(n + 4, part.at[up, 0:H], p1.at[0, 0:H], U)
    mail.arrived(n + 1, p2.at[1], U)
    add(part.at[down, H:ROWS], p2.at[1])
    mail.go(n + 5, part.at[down, H:ROWS], p1.at[1, H:ROWS], D)
    yield
    mail.arrived(n + 2, p1.at[0, H:ROWS], D)
    mail.arrived(n + 5, p1.at[1, H:ROWS], U)
    out(H, ROWS, val(part.at[y, H:ROWS]) + val(p1.at[0, H:ROWS]) + val(p1.at[1, H:ROWS]))
    mail.arrived(n + 3, p1.at[1, 0:H], U)
    mail.arrived(n + 4, p1.at[0, 0:H], D)
    out(0, H, val(part.at[y, 0:H]) + val(p1.at[0, 0:H]) + val(p1.at[1, 0:H]))


def val(ref):
    return ref[...].astype(WIDE)


def add(dst, src):
    dst[...] = (val(dst) + val(src)).astype(LOW)


def swap_seq(me, mail, own_ref, all_ref, lo, hi):
    n = mail.slots(7)
    for k in range(1, 8):
        to = (me.seq + k) % 8
        mail.go(n + k - 1, own_ref.at[to, :, lo:hi], all_ref.at[me.seq, me.dp, :, lo:hi], {"seq": to})
    yield
    for k in range(1, 8):
        came = (me.seq + 8 - k) % 8
        mail.arrived(n + k - 1, all_ref.at[came, me.dp, :, lo:hi], me.x_dev)


def gather_dp(me, mail, ref):
    z, h = me.z, me.h
    n = mail.slots(19)
    HD, ZU, ZD, TW = me.h_dev, me.z_up_dev, me.z_down_dev, me.twin_dev

    def at(zz, hh, half=None, twin=False):
        d = me.member(zz, hh, twin)
        return ref.at[:, d] if half is None else ref.at[4 * half : 4 * half + 4, d]

    def fwd(i, r, dev):
        mail.go(n + i, r, r, dev)

    def got(i, r):
        mail.arrived(n + i, r, TW)

    hs = (h, 1 - h)
    fwd(0, at(z, h), HD)
    fwd(1, at(z, h), ZU)
    fwd(2, at(z, h), ZD)
    fwd(9, at(z, h), TW)
    yield
    got(0, at(z, 1 - h))
    fwd(3, at(z, 1 - h), ZU)
    fwd(4, at(z, 1 - h), ZD)
    fwd(10, at(z, 1 - h), TW)
    yield
    for k in range(2):
        got(1 + 2 * k, at(me.z_down, hs[k]))
        fwd(5 + 2 * k, at(me.z_down, hs[k], 0), ZU)
        fwd(11 + 2 * k, at(me.z_down, hs[k]), TW)
        yield
        got(2 + 2 * k, at(me.z_up, hs[k]))
        fwd(6 + 2 * k, at(me.z_up, hs[k], 1), ZD)
        fwd(12 + 2 * k, at(me.z_up, hs[k]), TW)
        yield
    for k in range(2):
        got(5 + 2 * k, at(me.z_far, hs[k], 0))
        fwd(15 + 2 * k, at(me.z_far, hs[k], 0), TW)
        got(6 + 2 * k, at(me.z_far, hs[k], 1))
        fwd(16 + 2 * k, at(me.z_far, hs[k], 1), TW)
        yield
    got(9, at(z, h, twin=True))
    got(10, at(z, 1 - h, twin=True))
    for k in range(2):
        got(11 + 2 * k, at(me.z_down, hs[k], twin=True))
        got(12 + 2 * k, at(me.z_up, hs[k], twin=True))
        got(15 + 2 * k, at(me.z_far, hs[k], 0, twin=True))
        got(16 + 2 * k, at(me.z_far, hs[k], 1, twin=True))


def swap_y(me, mail, own_ref, all_ref):
    n = mail.slots(3)
    for k in (2, 1, 3):
        to = (me.y + k) % 4
        mail.go(n + k - 1, own_ref.at[to], all_ref.at[me.seq, me.dp], {"seq": me.a * 4 + to})
    yield
    for k in (1, 3, 2):
        came = me.a * 4 + (me.y + 4 - k) % 4
        mail.arrived(n + k - 1, all_ref.at[came, me.dp], me.up_dev)


def slab(me, ref, x, z, half=None, twin=False):
    d = me.member(z, x // 2, twin)
    first = x % 2 * 4
    return ref.at[pl.ds(first, 4), d] if half is None else ref.at[pl.ds(first + 2 * half, 2), d]


def gather_xz(me, mail, ref):
    n = mail.slots(36)
    XU, XD, ZU, ZD, TW = me.x_up_dev, me.x_down_dev, me.z_up_dev, me.z_down_dev, me.twin_dev
    z, zu, zd, zf = me.z, me.z_up, me.z_down, me.z_far
    xs = (me.x, me.x_down, me.x_up, me.x_far)

    def at(x, zz, half=None, twin=False):
        return slab(me, ref, x, zz, half, twin)

    def fwd(i, r, dev):
        mail.go(n + i, r, r, dev)

    def got(i, r):
        mail.arrived(n + i, r, TW)

    def z_first(k):
        fwd(4 + 4 * k, at(xs[k], z), ZU)
        fwd(5 + 4 * k, at(xs[k], z), ZD)
        fwd(20 + 4 * k, at(xs[k], z), TW)

    def z_second(k):
        got(4 + 4 * k, at(xs[k], zd))
        fwd(6 + 4 * k, at(xs[k], zd, 0), ZU)
        fwd(21 + 4 * k, at(xs[k], zd), TW)
        got(5 + 4 * k, at(xs[k], zu))
        fwd(7 + 4 * k, at(xs[k], zu, 1), ZD)
        fwd(22 + 4 * k, at(xs[k], zu), TW)

    def z_third(k):
        got(6 + 4 * k, at(xs[k], zf, 0))
        got(7 + 4 * k, at(xs[k], zf, 1))
        fwd(23 + 4 * k, at(xs[k], zf), TW)

    z_first(0)
    yield
    fwd(0, at(me.x, z), XU)
    fwd(1, at(me.x, z), XD)
    yield
    got(0, at(me.x_down, z))
    fwd(2, at(me.x_down, z, 0), XU)
    got(1, at(me.x_up, z))
    fwd(3, at(me.x_up, z, 1), XD)
    z_first(1)
    z_first(2)
    yield
    got(2, at(me.x_far, z, 0))
    got(3, at(me.x_far, z, 1))
    z_first(3)
    yield
    for k in range(4):
        z_second(k)
        yield
    for k in range(4):
        z_third(k)
        yield
    for k in range(4):
        for i, zz in enumerate((z, zd, zu, zf)):
            got(20 + 4 * k + i, at(xs[k], zz, twin=True))


def add_slabs(dst, *sources):
    def one(i, carry):
        total = val(dst.at[i])
        for source in sources:
            total = total + val(source.at[i])
        dst[i] = total.astype(LOW)
        return carry

    lax.fori_loop(0, dst.shape[0], one, 0)


def halved(ref, half):
    k = ref.shape[0] // 2
    return ref.at[half * k : half * k + k]


class RingSum:
    def __init__(self, mail, at, places, devices, over, near):
        self.mail, self.at, self.places, self.devices = mail, at, places, devices
        self.over, self.near = over, near
        self.n = mail.slots(6)

    def first(self):
        own, up, down, far = self.places
        U, D = self.devices
        go, n = self.mail.go, self.n
        go(n, halved(self.at(far), 0), self.over.at[0], U)
        go(n + 1, halved(self.at(far), 1), self.over.at[1], D)
        go(n + 2, halved(self.at(up), 1), halved(self.near.at[0], 1), U)
        go(n + 3, halved(self.at(down), 0), halved(self.near.at[1], 0), D)

    def second(self):
        own, up, down, far = self.places
        U, D = self.devices
        go, got, n = self.mail.go, self.mail.arrived, self.n
        got(n, self.over.at[0], D)
        add_slabs(halved(self.at(up), 0), self.over.at[0])
        go(n + 4, halved(self.at(up), 0), halved(self.near.at[0], 0), U)
        got(n + 1, self.over.at[1], U)
        add_slabs(halved(self.at(down), 1), self.over.at[1])
        go(n + 5, halved(self.at(down), 1), halved(self.near.at[1], 1), D)

    def third(self):
        own = self.places[0]
        U, D = self.devices
        got, n = self.mail.arrived, self.n
        got(n + 2, halved(self.near.at[0], 1), D)
        got(n + 3, halved(self.near.at[1], 0), U)
        got(n + 4, halved(self.near.at[0], 0), D)
        got(n + 5, halved(self.near.at[1], 1), U)
        add_slabs(self.at(own), self.near.at[0], self.near.at[1])


def twin_sum(me, mail, stage, acc, order, product, kept=None):
    slots = stage.shape[0]
    n = mail.slots(len(order))

    def settle(i):
        mail.arrived(n + i, acc.at[order[i]], me.twin_dev)
        add_slabs(acc.at[order[i]], stage.at[i % slots, :, me.core])
        if kept is not None:
            kept(i)

    for i, s in enumerate(order):
        if i >= slots:
            mail.sent(n + i - slots)
        product(s, stage.at[i % slots])
        mail.go(n + i, stage.at[i % slots, :, 1 - me.core], acc.at[s], me.twin_dev)
        if i > 0:
            settle(i - 1)
        yield
    settle(len(order) - 1)
    for i in range(max(0, len(order) - slots), len(order)):
        mail.sent(n + i)


def scatter_xz(me, mail, acc, z_over, z_near, x_over, x_near):
    xs = (me.x_far, me.x, me.x_up, me.x_down)
    zs = (me.z, me.z_up, me.z_down, me.z_far)
    XU, XD, ZU, ZD = me.x_up_dev, me.x_down_dev, me.z_up_dev, me.z_down_dev

    def at(x):
        return lambda z: acc.at[pl.ds(x % 2 * 4, 4), z * 2 + x // 2]

    rings = [RingSum(mail, at(x), zs, (ZU, ZD), z_over.at[k], z_near.at[k]) for k, x in enumerate(xs)]
    ring = RingSum(mail, lambda x: at(x)(me.z), (me.x, me.x_up, me.x_down, me.x_far), (XU, XD), x_over, x_near)
    rings[0].first()
    yield
    rings[2].first()
    rings[3].first()
    rings[1].first()
    yield
    for k in (0, 2, 3, 1):
        rings[k].second()
        yield
    for k in (0, 2, 3):
        rings[k].third()
        yield
    ring.first()
    yield
    rings[1].third()
    yield
    ring.second()
    yield
    ring.third()


def scatter_hz(me, mail, acc, z_over, z_near, h_near):
    hs = (1 - me.h, me.h)
    zs = (me.z, me.z_up, me.z_down, me.z_far)

    def at(h):
        return lambda z: acc.at[:, z * 2 + h]

    rings = [RingSum(mail, at(h), zs, (me.z_up_dev, me.z_down_dev), z_over.at[k], z_near.at[k]) for k, h in enumerate(hs)]
    n = mail.slots(1)
    rings[0].first()
    rings[1].first()
    yield
    for k in range(2):
        rings[k].second()
        yield
    rings[0].third()
    mail.go(n, at(1 - me.h)(me.z), h_near, me.h_dev)
    yield
    rings[1].third()
    yield
    mail.arrived(n, h_near, me.h_dev)
    add_slabs(at(me.h)(me.z), h_near)


def send_y(me, mail, slab, result):
    n = mail.slots(3)
    for k in (2, 1, 3):
        to = (me.y + k) % 4
        mail.go(n + k - 1, slab.at[to], result.at[me.y], {"seq": me.a * 4 + to})
    result[me.y] = slab[me.y]
    yield
    for k in (1, 3, 2):
        mail.arrived(n + k - 1, result.at[(me.y + 4 - k) % 4], me.up_dev)


def send_seq(me, mail, slab, result, lo, hi):
    n = mail.slots(7)
    for k in range(1, 8):
        to = (me.seq + k) % 8
        mail.go(n + k - 1, slab.at[to, :, lo:hi], result.at[me.seq], {"seq": to})
    result[me.seq] = slab[me.seq, :, lo:hi]
    yield
    for k in range(1, 8):
        mail.arrived(n + k - 1, result.at[(me.seq + 8 - k) % 8], me.x_dev)


def scatter_bufs():
    late = ROWS - FIRST
    shapes = ((4, late, MODEL), (2, late, MID), (2, late, MODEL), (4, FIRST, MID), (4, FIRST, MODEL), (1, FIRST, MODEL))
    return [pltpu.VMEM(shape, LOW) for shape in shapes]


def scatter_seq(me, mail, part, bufs, out):
    a, b, y, up, down, far = me.a, me.b, me.y, me.up, me.down, me.far
    XP, U, D = me.x_dev, me.up_dev, me.down_dev
    qx, q2, q1, p2, p1, px = bufs
    n = mail.slots(23)
    halves = (pl.ds(0, MID), pl.ds(MID, MID))

    def go(i, src, dst, dev):
        mail.go(n + i, src, dst, dev)

    def got(i, dst):
        mail.arrived(n + i, dst, XP)

    def at(col, row, rows, half=None):
        lo, hi = ((0, FIRST), (FIRST, ROWS))[rows]
        ref = part.at[col * 4 + row]
        return ref.at[lo:hi] if half is None else ref.at[lo:hi, halves[half]]

    def lane(ref, k, half):
        return ref.at[k, :, halves[half]]

    for k, row in enumerate((far, down, up, y)):
        go(k, at(b, row, 1), qx.at[row], XP)
    cols = (b, a)

    def p_first(k):
        c, s = cols[k], 10 + 6 * k
        go(s, at(c, far, 0, 0), p2.at[2 * k], U)
        go(s + 1, at(c, far, 0, 1), p2.at[2 * k + 1], D)
        go(s + 2, at(c, up, 0, 1), lane(p1, 2 * k, 1), U)
        go(s + 3, at(c, down, 0, 0), lane(p1, 2 * k + 1, 0), D)

    def p_second(k):
        c, s = cols[k], 10 + 6 * k
        got(s, p2.at[2 * k])
        add(at(c, up, 0, 0), p2.at[2 * k])
        go(s + 4, at(c, up, 0, 0), lane(p1, 2 * k, 0), U)
        got(s + 1, p2.at[2 * k + 1])
        add(at(c, down, 0, 1), p2.at[2 * k + 1])
        go(s + 5, at(c, down, 0, 1), lane(p1, 2 * k + 1, 1), D)

    def p_third(k):
        s = 10 + 6 * k
        got(s + 2, lane(p1, 2 * k, 1))
        got(s + 3, lane(p1, 2 * k + 1, 0))
        got(s + 4, lane(p1, 2 * k, 0))
        got(s + 5, lane(p1, 2 * k + 1, 1))
        return val(at(cols[k], y, 0)) + val(p1.at[2 * k]) + val(p1.at[2 * k + 1])

    p_first(0)
    yield
    p_first(1)
    yield
    got(0, qx.at[far])
    add(at(a, far, 1), qx.at[far])
    go(4, at(a, far, 1, 0), q2.at[0], U)
    go(5, at(a, far, 1, 1), q2.at[1], D)
    yield
    p_second(0)
    yield
    got(1, qx.at[down])
    add(at(a, down, 1), qx.at[down])
    go(6, at(a, down, 1, 0), lane(q1, 1, 0), D)
    got(2, qx.at[up])
    add(at(a, up, 1), qx.at[up])
    go(7, at(a, up, 1, 1), lane(q1, 0, 1), U)
    yield
    p_second(1)
    yield
    rows = p_third(0)
    own = at(b, y, 0)
    own[...] = rows.astype(LOW)
    go(22, own, px.at[0], XP)
    yield
    got(4, q2.at[0])
    add(at(a, up, 1, 0), q2.at[0])
    go(8, at(a, up, 1, 0), lane(q1, 0, 0), U)
    got(5, q2.at[1])
    add(at(a, down, 1, 1), q2.at[1])
    go(9, at(a, down, 1, 1), lane(q1, 1, 1), D)
    yield
    rows = p_third(1)
    got(22, px.at[0])
    out(0, FIRST, rows + val(px.at[0]))
    yield
    got(3, qx.at[y])
    got(6, lane(q1, 1, 0))
    got(7, lane(q1, 0, 1))
    got(8, lane(q1, 0, 0))
    got(9, lane(q1, 1, 1))
    out(FIRST, ROWS, val(at(a, y, 1)) + val(qx.at[y]) + val(q1.at[0]) + val(q1.at[1]))


def run(*tasks):
    tasks = list(tasks)
    while tasks:
        for task in list(tasks):
            if next(task, tasks) is tasks:
                tasks.remove(task)


def step(task, count=1):
    for _ in range(count):
        next(task, None)


def finish(task, *others):
    k = 0
    while next(task, others) is not others:
        k += 1
        if k % 2 == 0 and others:
            step(others[k // 2 % len(others)])
def dot(a, b, dims=((1,), (0,))):
    return lax.dot_general(a, b, (dims, ((), ())), preferred_element_type=WIDE)


def row_scale(values):
    return lax.rsqrt(jnp.mean(values * values, axis=-1, keepdims=True) + EPS)


def front_kernel(
    x_ref, live_ref, cot_ref, wa_own, wm_own, pos_q, pos_k,
    one_out, wa_out, grad_all, wm, qkv_out, probs_out, att_out, resid, two,
    one_all, wa, grad_own, qkv, probs, att, ones_t, att_t, part, qx, q2, q1, p2, p1, px, send, recv, local_sem,
):
    me = Place()
    mail = Mail(send, recv)
    saves = []

    def save(src, dst):
        copy = pltpu.make_async_copy(src, dst, local_sem.at[len(saves)])
        copy.start()
        saves.append(copy)
        return copy

    enter(me.peers() + [me.h_dev, me.z_up_dev, me.z_down_dev, me.twin_dev, me.x_up_dev, me.x_down_dev])
    swap_a = swap_seq(me, mail, wa_own, wa, 0, PROJ)
    step(swap_a)
    swap_m = swap_y(me, mail, wm_own, wm)
    step(swap_m)
    keep_m = save(wm_own.at[me.y], wm.at[me.seq, me.dp])
    x = x_ref[...].astype(WIDE)
    one_all[me.seq] = (x * row_scale(x) * live_ref[...]).astype(LOW)
    gather_one = gather_seq(me, mail, one_all.at[me.seq], one_all)
    step(gather_one)
    wa[pl.ds(me.seq, 1), pl.ds(me.dp, 1), :, 0:PROJ] = wa_own[pl.ds(me.seq, 1), :, 0:PROJ][None]
    for k in range(8):
        wa[k, pl.ds(me.dp, 1), :, PROJ:] = wa_own[k, :, PROJ:][None]
    step(swap_a)
    gather_wa = gather_dp(me, mail, wa)
    step(gather_wa)
    grad_own[...] = (cot_ref[...].astype(WIDE) * live_ref[...]).astype(LOW)
    save(grad_own, grad_all.at[me.y])
    step(gather_one)
    step(gather_wa)
    step(gather_one)
    step(gather_wa, 2)
    step(gather_one)
    step(gather_wa, 2)
    step(swap_m)
    keep_m.wait()
    gather_wm = gather_xz(me, mail, wm)
    step(gather_wm, 2)
    step(gather_one, 2)
    gather_g = gather_y(me, mail, grad_own, grad_all)
    step(gather_g)
    run(gather_one, gather_wa)
    step(gather_wm)
    save(wa, wa_out)

    def project(i, carry):
        rows = one_all[pl.ds(i * 2, 2)].reshape(2 * ROWS, MODEL)
        weight = wa[:, :, :, 0:PROJ].reshape(MODEL, PROJ)
        qkv[pl.ds(pl.multiple_of(i * 256, 256), 256), :] = dot(rows, weight).astype(LOW)
        return carry

    def attend(i, carry):
        first = pl.multiple_of(i * ROWS, ROWS)
        rows = pl.ds(first, ROWS)
        allowed = pos_k[...] <= pos_q[rows, :]
        for head in range(2):
            lo, hi = head * HEAD_DIM, (head + 1) * HEAD_DIM
            q = qkv[rows, lo:hi]
            k = qkv[:, PART + lo : PART + hi]
            v = qkv[:, 2 * PART + lo : 2 * PART + hi]
            scores = dot(q, k, ((1,), (1,))) * (1.0 / math.sqrt(HEAD_DIM)) - math.log(8 * ROWS)
            p = jnp.where(allowed, 1.0 / (1.0 + jnp.exp(-scores)), 0.0).astype(LOW)
            probs[head, rows, :] = p
            att[rows, lo:hi] = dot(p, v).astype(LOW)
        return carry

    def out_project(col):
        rows = att[pl.ds(pl.multiple_of(col * 512, 512), 512), :]

        def piece(k, carry):
            weight = wa[k, :, :, PROJ:].reshape(PART, PART)
            columns = pl.ds(pl.multiple_of(k * PART, PART), PART)
            part[pl.ds(col * 4, 4), :, columns] = dot(rows, weight).reshape(4, ROWS, PART).astype(LOW)
            return carry

        lax.fori_loop(0, 8, piece, 0)

    lax.fori_loop(0, 4, project, 0)
    step(gather_g)
    save(qkv, qkv_out)

    def write(lo, hi, rows):
        total = x_ref[lo:hi].astype(WIDE) + rows
        resid[lo:hi] = total
        two[lo:hi] = (total * row_scale(total) * live_ref[lo:hi]).astype(LOW)

    scatter = scatter_seq(me, mail, part, (qx, q2, q1, p2, p1, px), write)
    lax.fori_loop(me.b * 4, me.b * 4 + 4, attend, 0)
    out_project(me.b)
    step(scatter)
    step(gather_wm)
    lax.fori_loop(me.a * 4, me.a * 4 + 4, attend, 0)
    out_project(me.a)
    step(scatter)
    save(probs, probs_out)
    finish(scatter, gather_wm)
    step(gather_wm)

    def turn(s, carry):
        columns = pl.ds(pl.multiple_of(s * 256, 256), 256)
        ones_t[s] = one_all[:, :, columns].reshape(8 * ROWS, 256).T
        return carry

    att_t[...] = att[...].T
    save(att_t, att_out)
    for i in range(4):
        lax.fori_loop(2 * i, 2 * i + 2, turn, 0)
        step(gather_wm)
    save(ones_t, one_out)
    run(gather_wm, gather_g)
    for copy in saves:
        if copy is not keep_m:
            copy.wait()
    mail.finish()


def front(x, live, cot, wa_own, wm_own, pos):
    vmem, anywhere = pl.BlockSpec(memory_space=pltpu.VMEM), pl.BlockSpec(memory_space=pl.ANY)
    shape = jax.ShapeDtypeStruct
    count = 7 + 18 + 19 + 3 + 36 + 4 + 23
    return pl.pallas_call(
        front_kernel,
        out_shape=(
            shape((8, 256, 1024), LOW), shape((8, 16, 16, 1024), LOW), shape((4, ROWS, MODEL), LOW),
            shape((8, 16, 16, SLAB), LOW), shape((1024, PROJ), LOW), shape((2, 1024, 1024), LOW),
            shape((PART, 1024), LOW), shape((ROWS, MODEL), WIDE), shape((ROWS, MODEL), LOW),
        ),
        in_specs=[vmem] * 4 + [anywhere] + [vmem] * 2,
        out_specs=(anywhere,) * 7 + (vmem, vmem),
        scratch_shapes=[
            pltpu.VMEM((8, ROWS, MODEL), LOW), pltpu.VMEM((8, 16, 16, 1024), LOW), pltpu.VMEM((ROWS, MODEL), LOW),
            pltpu.VMEM((1024, PROJ), LOW), pltpu.VMEM((2, 1024, 1024), LOW), pltpu.VMEM((1024, PART), LOW),
            pltpu.VMEM((8, 256, 1024), LOW), pltpu.VMEM((PART, 1024), LOW),
            pltpu.VMEM((8, ROWS, MODEL), LOW),
        ]
        + scatter_bufs()
        + [pltpu.SemaphoreType.DMA((count,)), pltpu.SemaphoreType.DMA((count,)), pltpu.SemaphoreType.DMA((8,))],
        compiler_params=pltpu.CompilerParams(collective_id=1, has_side_effects=True, vmem_limit_bytes=56 * 2**20),
        name="front",
    )(x, live, cot, wa_own, wm_own, pos[:, None], pos[None, :])
def mlp_kernel(
    two_ref, resid, cot_ref, live_ref, grad_all, wm_all,
    acc_out, branch_out, grad_resid, grad_branch,
    wm, grads, twos, hidden, pair, grads_t, part, branch, p2, p1,
    stage, acc, send, recv, local_sem,
):
    me = Place()
    mail = Mail(send, recv)
    saves = []

    def save(src, dst):
        copy = pltpu.make_async_copy(src, dst, local_sem.at[len(saves)])
        copy.start()
        saves.append(copy)
        return copy

    load_w = save(wm_all, wm)
    load_g = save(grad_all, grads)
    enter([me.up_dev, me.down_dev, me.twin_dev])
    twos[me.y] = two_ref[...]
    gather = gather_y(me, mail, twos.at[me.y], twos)
    step(gather)
    load_w.wait()
    load_g.wait()

    def rows_of(ref, blocks):
        return jnp.concatenate([ref[k] for k in blocks], axis=0)

    def put(ref, blocks, columns, values):
        for i, k in enumerate(blocks):
            ref[k, :, columns] = values[i * ROWS : (i + 1) * ROWS].astype(LOW)

    def hidden_tile(blocks, j, wide):
        start = j * 128
        if not isinstance(j, int):
            start = pl.multiple_of(start, 128)
        width = wide * 128
        weight = wm[:, :, :, pl.ds(2 * start, 2 * width)].reshape(MODEL, 2 * width)
        gate_up = dot(rows_of(twos, blocks), weight)
        down = wm[:, :, :, pl.ds(PAIR + start, width)].reshape(MODEL, width)
        grad_hidden = dot(rows_of(grads, blocks), down)
        low, pairs = [], []
        for i in range(wide):
            gate = gate_up[:, i * 256 : i * 256 + 128]
            up = gate_up[:, i * 256 + 128 : i * 256 + 256]
            back = grad_hidden[:, i * 128 : i * 128 + 128]
            squashed = 1.0 / (1.0 + jnp.exp(-gate))
            active = gate * squashed
            low.append(active * up)
            pairs.append(back * up * (squashed * (1.0 + gate * (1.0 - squashed))))
            pairs.append(back * active)
        put(hidden, blocks, pl.ds(start, width), jnp.concatenate(low, axis=1))
        put(pair, blocks, pl.ds(2 * start, 2 * width), jnp.concatenate(pairs, axis=1))

    def ahead(blocks):
        def tile(j, carry):
            hidden_tile(blocks, 2 * j, 2)
            return carry

        lax.fori_loop(0, 5, tile, 0)
        hidden_tile(blocks, 10, 1)

    def back(blocks):
        def tile(s, carry):
            columns = pl.ds(pl.multiple_of(s * 256, 256), 256)
            weight = wm[s, :, :, 0:PAIR].reshape(256, PAIR)
            put(part, blocks, columns, dot(rows_of(pair, blocks), weight, ((1,), (1,))))
            return carry

        lax.fori_loop(0, 8, tile, 0)

    def down_back(blocks):
        def tile(s, carry):
            columns = pl.ds(pl.multiple_of(s * 256, 256), 256)
            weight = wm[s, :, :, PAIR:].reshape(256, UNITS)
            put(branch, blocks, columns, dot(rows_of(hidden, blocks), weight, ((1,), (1,))))
            return carry

        lax.fori_loop(0, 8, tile, 0)

    def write(lo, hi, rows):
        x = resid[lo:hi]
        scale = row_scale(x)
        hat = x * scale
        inner = jnp.mean(rows * hat, axis=-1, keepdims=True)
        total = cot_ref[lo:hi].astype(WIDE) * live_ref[lo:hi] + scale * (rows - hat * inner)
        grad_resid[lo:hi] = total
        grad_branch[lo:hi] = total.astype(LOW)

    scatter = scatter_y(me, mail, part, p2, p1, write)
    ahead([me.y])

    def turn(s, carry):
        columns = pl.ds(pl.multiple_of(s * 256, 256), 256)
        grads_t[s] = grads[:, :, columns].reshape(4 * ROWS, 256).T
        return carry

    lax.fori_loop(0, 8, turn, 0)
    step(gather)
    ahead([me.up, me.down])
    back([me.up, me.down])
    step(scatter)
    step(gather)
    ahead([me.far])
    back([me.far])
    step(scatter)
    back([me.y])
    down_back([me.y, me.up, me.down, me.far])
    step(scatter)

    save(branch, branch_out)
    order = [me.a * 4 + i for i in range(4)] + [me.b * 4 + i for i in range(4)]

    def product(s, out):
        columns = pl.ds(pl.multiple_of(s * 256, 256), 256)
        rows = twos[:, :, columns].reshape(4 * ROWS, 256).T
        terms = dot(rows, pair[...].reshape(4 * ROWS, PAIR))
        out[:, :, :, 0:PAIR] = terms.reshape(8, 2, 16, PAIR).astype(LOW)
        terms = dot(grads_t[s], hidden[...].reshape(4 * ROWS, UNITS))
        out[:, :, :, PAIR:] = terms.reshape(8, 2, 16, UNITS).astype(LOW)

    def kept(i):
        save(acc.at[order[i]], acc_out.at[order[i]])

    twin = twin_sum(me, mail, stage, acc, order, product, kept)
    step(twin, 3)
    step(scatter)
    run(twin)
    run(scatter)
    for copy in saves[2:]:
        copy.wait()
    mail.finish()


def mlp(two, resid, cot, live, grad_all, wm):
    vmem, anywhere = pl.BlockSpec(memory_space=pltpu.VMEM), pl.BlockSpec(memory_space=pl.ANY)
    shape = jax.ShapeDtypeStruct
    blocks = (4, ROWS, MODEL)
    return pl.pallas_call(
        mlp_kernel,
        out_shape=(
            shape((8, 8, 16, SLAB), LOW), shape(blocks, LOW), shape((ROWS, MODEL), WIDE), shape((ROWS, MODEL), LOW),
        ),
        in_specs=[vmem] * 4 + [anywhere] * 2,
        out_specs=(anywhere,) * 2 + (vmem,) * 2,
        scratch_shapes=[
            pltpu.VMEM((8, 16, 16, SLAB), LOW), pltpu.VMEM(blocks, LOW), pltpu.VMEM(blocks, LOW),
            pltpu.VMEM((4, ROWS, UNITS), LOW), pltpu.VMEM((4, ROWS, PAIR), LOW), pltpu.VMEM((8, 256, 4 * ROWS), LOW), pltpu.VMEM(blocks, LOW),
            pltpu.VMEM(blocks, LOW), pltpu.VMEM((2, ROWS // 2, MODEL), LOW), pltpu.VMEM((2, ROWS, MODEL), LOW),
            pltpu.VMEM((2, 8, 2, 16, SLAB), LOW), pltpu.VMEM((8, 8, 16, SLAB), LOW),
            pltpu.SemaphoreType.DMA((24,)), pltpu.SemaphoreType.DMA((24,)), pltpu.SemaphoreType.DMA((11,)),
        ],
        compiler_params=pltpu.CompilerParams(collective_id=2, has_side_effects=True, vmem_limit_bytes=62 * 2**20),
        name="mlp",
    )(two, resid, cot, live, grad_all, wm)
def back_kernel(
    branch_grad, grad_resid, x_ref, live_ref, resid, branch_all, acc_all, one_all, wa_all, qkv_all, probs_all, att_all,
    layer_out, input_grad, slab_own, in_own, out_own,
    acc, z_over, z_near, x_over, x_near, grads, branch, b2, b1, part, qx, q2, q1, p2, p1, px,
    wa, acc_a, az_over, az_near, h_near, ones_t, qkv, probs, att_t, grad_att, grad_proj, grad_k, grad_v, stage_a,
    send, recv, local_sem,
):
    me = Place()
    mail = Mail(send, recv)
    loads = []

    def load(src, dst):
        copy = pltpu.make_async_copy(src, dst, local_sem.at[len(loads)])
        copy.start()
        loads.append(copy)
        return copy

    load_acc = [load(acc_all.at[pl.ds(col * 4, 4)], acc.at[pl.ds(col * 4, 4)]) for col in (me.a, me.b)]
    enter(me.peers() + [me.h_dev, me.z_up_dev, me.z_down_dev, me.x_up_dev, me.x_down_dev, me.twin_dev])
    grads[me.seq] = branch_grad[...]
    gather = gather_seq(me, mail, grads.at[me.seq], grads)
    step(gather)
    load_wa = load(wa_all, wa)
    load_branch = load(branch_all, branch)
    waits = [load(*both) for both in ((qkv_all, qkv), (att_all, att_t), (one_all, ones_t))]
    fetch = [load(probs_all.at[:, 256 * i : 256 * i + 256], probs.at[i]) for i in range(2)]
    order = [me.a * 4 + i for i in range(4)] + [me.b * 4 + i for i in range(4)]

    def columns_of(s, width=256):
        return pl.ds(pl.multiple_of(s * width, width), width)

    def slab_sums():
        yield from scatter_xz(me, mail, acc, z_over, z_near, x_over, x_near)
        yield from send_y(me, mail, acc.at[pl.ds(me.a * 4, 4), me.z * 2 + me.h], slab_own)

    sums = slab_sums()

    load_acc[0].wait()
    step(sums)
    load_acc[1].wait()
    step(sums)
    step(gather, 4)

    def write_out(lo, hi, rows):
        layer_out[lo:hi] = (live_ref[lo:hi] * (resid[lo:hi] + rows)).astype(LOW)

    out_sum = scatter_y(me, mail, branch, b2, b1, write_out)
    load_branch.wait()
    step(out_sum, 2)
    run(gather)
    def write_grad(lo, hi, rows):
        x = x_ref[lo:hi].astype(WIDE)
        scale = row_scale(x)
        hat = x * scale
        inner = jnp.mean(rows * hat, axis=-1, keepdims=True)
        input_grad[lo:hi] = grad_resid[lo:hi] + live_ref[lo:hi] * scale * (rows - hat * inner)

    grad_sum = scatter_seq(me, mail, part, (qx, q2, q1, p2, p1, px), write_grad)

    load_wa.wait()
    for wait in waits:
        wait.wait()
    head_scale = 1.0 / math.sqrt(HEAD_DIM)

    def attended_grad(i, carry):
        total = jnp.zeros((256, PART), WIDE)
        for k in range(8):
            rows = grads[pl.ds(i * 2, 2), :, k * PART : k * PART + PART].reshape(256, PART)
            total = total + dot(rows, wa[k, :, :, PROJ:].reshape(PART, PART), ((1,), (1,)))
        grad_att[columns_of(i), :] = total.astype(LOW)
        return carry

    lax.fori_loop(0, 4, attended_grad, 0)
    grad_k[...] = jnp.zeros_like(grad_k)
    grad_v[...] = jnp.zeros_like(grad_v)

    def attend_back(i):
        rows = pl.ds(256 * i, 256)
        for head in range(2):
            lo, hi = head * HEAD_DIM, (head + 1) * HEAD_DIM
            low = probs[i % 2, head]
            p = low.astype(WIDE)
            g = grad_att[rows, lo:hi]
            back = dot(g, qkv[:, 2 * PART + lo : 2 * PART + hi], ((1,), (1,)))
            grad_s = (back * (p * (1.0 - p))).astype(LOW)
            grad_q = dot(grad_s, qkv[:, PART + lo : PART + hi]) * head_scale
            grad_proj[rows, lo:hi] = grad_q.astype(LOW)
            grad_v[:, lo:hi] += dot(low, g, ((0,), (0,)))
            grad_k[:, lo:hi] += dot(grad_s, qkv[rows, lo:hi], ((0,), (0,)))

    for i in range(4):
        fetch[i].wait()
        attend_back(i)
        if i == 1:
            step(out_sum)
        if i < 2:
            fetch.append(load(probs_all.at[:, 256 * i + 512 : 256 * i + 768], probs.at[i]))
        step(sums)
    grad_proj[:, PART : 2 * PART] = (grad_k[...] * head_scale).astype(LOW)
    grad_proj[:, 2 * PART :] = grad_v[...].astype(LOW)

    def norm_terms(col):
        rows = grad_proj[columns_of(col, 512), :]

        def piece(s, carry):
            weight = wa[s, :, :, 0:PROJ].reshape(256, PROJ)
            terms = dot(rows, weight, ((1,), (1,)))
            part[pl.ds(col * 4, 4), :, columns_of(s)] = terms.reshape(4, ROWS, 256).astype(LOW)
            return carry

        lax.fori_loop(0, 8, piece, 0)

    def product(s, out):
        terms = dot(ones_t[s], grad_proj[...])
        out[:, :, :, 0:PROJ] = terms.reshape(8, 2, 16, PROJ).astype(LOW)
        rows = grads[:, :, columns_of(s)].reshape(8 * ROWS, 256)
        out[:, :, :, PROJ:] = dot(att_t[...], rows).reshape(8, 2, 16, PART).astype(LOW)

    twin = twin_sum(me, mail, stage_a, acc_a, order, product)
    norm_terms(me.b)
    step(grad_sum)
    step(twin, 9)
    norm_terms(me.a)
    step(grad_sum)

    def proj_sums():
        yield from scatter_hz(me, mail, acc_a, az_over, az_near, h_near)
        own = acc_a.at[:, me.z * 2 + me.h]
        out_own[...] = own[:, :, PROJ:]
        yield from send_seq(me, mail, own, in_own, 0, PROJ)

    rest = proj_sums()
    step(rest)
    finish(grad_sum, sums)
    run(rest, sums, out_sum)
    mail.finish()


def back(branch_grad, grad_resid, x, live, resid, branch, acc, ones, wa, qkv, probs, att):
    vmem, anywhere = pl.BlockSpec(memory_space=pltpu.VMEM), pl.BlockSpec(memory_space=pl.ANY)
    shape = jax.ShapeDtypeStruct
    count = 18 + 30 + 3 + 6 + 23 + 8 + 13 + 7
    return pl.pallas_call(
        back_kernel,
        out_shape=(
            shape((ROWS, MODEL), LOW), shape((ROWS, MODEL), WIDE), shape((4, 16, SLAB), LOW),
            shape((8, 16, PROJ), LOW), shape((8, 16, PART), LOW),
        ),
        in_specs=[vmem] * 5 + [anywhere] * 7,
        out_specs=(vmem,) * 5,
        scratch_shapes=[
            pltpu.VMEM((8, 8, 16, SLAB), LOW), pltpu.VMEM((4, 2, 2, 16, SLAB), LOW), pltpu.VMEM((4, 2, 4, 16, SLAB), LOW),
            pltpu.VMEM((2, 2, 16, SLAB), LOW), pltpu.VMEM((2, 4, 16, SLAB), LOW), pltpu.VMEM((8, ROWS, MODEL), LOW),
            pltpu.VMEM((4, ROWS, MODEL), LOW), pltpu.VMEM((2, ROWS // 2, MODEL), LOW), pltpu.VMEM((2, ROWS, MODEL), LOW),
            pltpu.VMEM((8, ROWS, MODEL), LOW),
        ]
        + scatter_bufs()
        + [
            pltpu.VMEM((8, 16, 16, 1024), LOW), pltpu.VMEM((8, 8, 16, 1024), LOW), pltpu.VMEM((2, 2, 4, 16, 1024), LOW),
            pltpu.VMEM((2, 2, 8, 16, 1024), LOW), pltpu.VMEM((8, 16, 1024), LOW),
            pltpu.VMEM((8, 256, 1024), LOW),
            pltpu.VMEM((1024, PROJ), LOW), pltpu.VMEM((2, 2, 256, 1024), LOW), pltpu.VMEM((PART, 1024), LOW),
            pltpu.VMEM((1024, PART), LOW), pltpu.VMEM((1024, PROJ), LOW),
            pltpu.VMEM((1024, PART), WIDE), pltpu.VMEM((1024, PART), WIDE), pltpu.VMEM((2, 8, 2, 16, 1024), LOW),
            pltpu.SemaphoreType.DMA((count,)), pltpu.SemaphoreType.DMA((count,)), pltpu.SemaphoreType.DMA((12,)),
        ],
        compiler_params=pltpu.CompilerParams(collective_id=3, has_side_effects=True, vmem_limit_bytes=62 * 2**20),
        name="back",
    )(branch_grad, grad_resid, x, live, resid, branch, acc, ones, wa, qkv, probs, att)
def weights_out(attn_weight, mlp_weight, gain_one, gain_two):
    proj = (attn_weight[:, :3].astype(WIDE) * gain_one).astype(LOW).reshape(16, 3, 8, PART)
    proj = proj.transpose(2, 0, 1, 3).reshape(8, 16, PROJ)
    out = attn_weight[:, 3].reshape(16, 8, PART).transpose(1, 0, 2)
    units = mlp_weight.shape[2] // 4
    spare = UNITS - units
    pair = (mlp_weight[:, :2].astype(WIDE) * gain_two).astype(LOW).reshape(16, 2, 4, units)
    pair = jnp.pad(pair, ((0, 0), (0, 0), (0, 0), (0, spare))).reshape(16, 2, 4, UNITS // 128, 128)
    pair = pair.transpose(2, 0, 3, 1, 4).reshape(4, 16, PAIR)
    down = jnp.pad(mlp_weight[:, 2].reshape(16, 4, units), ((0, 0), (0, 0), (0, spare))).transpose(1, 0, 2)
    return jnp.concatenate([proj, out], axis=2), jnp.concatenate([pair, down], axis=2)


def weights_back(slab, proj, out, units):
    pair, down = slab[..., :PAIR], slab[..., PAIR:]
    proj = proj.reshape(8, 16, 3, PART).transpose(1, 2, 0, 3).reshape(16, 3, MODEL).astype(WIDE)
    out = out.transpose(1, 0, 2).reshape(16, MODEL).astype(WIDE)
    pair = pair.reshape(4, 16, UNITS // 128, 2, 128).transpose(1, 3, 0, 2, 4).reshape(16, 2, 4, UNITS)
    pair = pair[..., : units // 4].reshape(16, 2, units).astype(WIDE)
    down = down[..., : units // 4].transpose(1, 0, 2).reshape(16, units).astype(WIDE)
    return proj, out, pair, down


def local(
    tokens, valid_counts, block_owner, norm1_gain, attn_weight, norm2_gain, mlp_weight, cotangent
):
    row_index = jnp.arange(ROWS, dtype=jnp.int32)
    live = (row_index < valid_counts[0, 0]).astype(WIDE)[:, None]
    pos = (block_owner[0][:, None] * ROWS + row_index[None]).reshape(-1)
    x, cot = tokens[0], cotangent[0]
    gain_one = norm1_gain.astype(WIDE)[:, None, None]
    gain_two = norm2_gain.astype(WIDE)[:, None, None]
    wa_own, wm_own = weights_out(attn_weight, mlp_weight, gain_one, gain_two)
    ones, wa, grads, wm, qkv, probs, att, resid, two = front(x, live, cot, wa_own, wm_own, pos)
    acc, branch, grad_resid, branch_grad = mlp(two, resid, cot, live, grads, wm)
    layer_out, input_grad, slab_own, in_own, out_own = back(
        branch_grad, grad_resid, x, live, resid, branch, acc, ones, wa, qkv, probs, att
    )
    in_sum, out_sum, pair_sum, down_sum = weights_back(slab_own, in_own, out_own, mlp_weight.shape[2])
    attn_grad = jnp.concatenate([in_sum * gain_one, out_sum[:, None]], axis=1)
    mlp_grad = jnp.concatenate([pair_sum * gain_two, down_sum[:, None]], axis=1)
    gain_one_grad = jnp.sum(in_sum * attn_weight[:, :3].astype(WIDE), axis=(1, 2))
    gain_two_grad = jnp.sum(pair_sum * mlp_weight[:, :2].astype(WIDE), axis=(1, 2))
    return (layer_out[None], input_grad[None], gain_one_grad, attn_grad, gain_two_grad, mlp_grad)


def solution(mesh):
    token_spec = P("dp", "seq", None)
    row_spec = P(("seq", "dp"), None, None)
    gain_spec = P(("seq", "dp"))
    in_specs = (
        token_spec, P("dp", "seq"), P("dp", None), gain_spec, row_spec, gain_spec, row_spec, token_spec
    )
    out_specs = (token_spec, token_spec, gain_spec, row_spec, gain_spec, row_spec)
    return jax.shard_map(local, mesh=mesh, in_specs=in_specs, out_specs=out_specs, check_vma=False)
```

```python
import functools, math
import jax
import jax.numpy as jnp
from jax import lax
from jax.experimental import pallas as pl
from jax.experimental.pallas import tpu as pltpu
from jax.sharding import PartitionSpec as P

LOW = jnp.bfloat16
WIDE = jnp.float32
MESH = pl.DeviceIdType.MESH
EPS = 1e-05
HEAD_DIM = 128
ROWS = 128
MODEL = 2048
PART = 256
PROJ = 3 * PART
UNITS = 1408
SLAB = 3 * UNITS
PAIR = 2 * UNITS
FIRST = 96
MID = MODEL // 2


class Place:
    def __init__(self):
        self.seq, self.dp = lax.axis_index("seq"), lax.axis_index("dp")
        self.a, self.y = self.seq // 4, self.seq % 4
        self.b = 1 - self.a
        self.up, self.down, self.far = (self.y + 1) % 4, (self.y + 3) % 4, (self.y + 2) % 4
        self.z, self.h, self.core = self.dp // 4, self.dp // 2 % 2, self.dp % 2
        self.z_up, self.z_down, self.z_far = (self.z + 1) % 4, (self.z + 3) % 4, (self.z + 2) % 4
        self.x_dev = {"seq": self.b * 4 + self.y}
        self.up_dev = {"seq": self.a * 4 + self.up}
        self.down_dev = {"seq": self.a * 4 + self.down}
        self.h_dev = {"dp": self.member(self.z, 1 - self.h)}
        self.z_up_dev = {"dp": self.member(self.z_up, self.h)}
        self.z_down_dev = {"dp": self.member(self.z_down, self.h)}
        self.twin_dev = {"dp": self.dp + 1 - 2 * self.core}
        self.x = self.h * 2 + self.a
        self.x_up, self.x_down, self.x_far = (self.x + 1) % 4, (self.x + 3) % 4, (self.x + 2) % 4
        self.x_up_dev, self.x_down_dev = self.at_x(self.x_up), self.at_x(self.x_down)

    def member(self, z, h, twin=False):
        core = 1 - self.core if twin else self.core
        return z * 4 + h * 2 + core

    def at_x(self, x):
        return {"seq": x % 2 * 4 + self.y, "dp": self.member(self.z, x // 2)}

    def column(self, twin=False):
        return self.z * 4 + (1 - self.core if twin else self.core)

    def peers(self):
        return [{"seq": (self.seq + k) % 8} for k in range(1, 8)]


def greet(devices):
    barrier = pltpu.get_barrier_semaphore()
    for device in devices:
        pl.semaphore_signal(barrier, inc=1, device_id=device, device_id_type=MESH)
    return lambda: pl.semaphore_wait(barrier, len(devices))


class Mail:
    def __init__(self, send, recv):
        self.send, self.recv = send, recv
        self.count, self.started = 0, {}

    def slots(self, n):
        first = self.count
        self.count += n
        return first

    def copy(self, slot, src, dst, device):
        return pltpu.make_async_remote_copy(
            src_ref=src, dst_ref=dst, send_sem=self.send.at[slot], recv_sem=self.recv.at[slot],
            device_id=device, device_id_type=MESH,
        )

    def go(self, slot, src, dst, device):
        copy = self.copy(slot, src, dst, device)
        copy.start()
        self.started[slot] = copy

    def arrived(self, slot, dst, device):
        self.copy(slot, dst, dst, device).wait_recv()

    def sent(self, slot):
        self.started.pop(slot).wait_send()

    def finish(self):
        for copy in self.started.values():
            copy.wait_send()


def gather_seq(me, mail, x_ref, out_ref):
    a, b, y, up, down, far = me.a, me.b, me.y, me.up, me.down, me.far
    XP, U, D = me.x_dev, me.up_dev, me.down_dev
    n = mail.slots(18)

    def cut(ref, rows, half):
        lo, hi = ((0, FIRST), (FIRST, ROWS))[rows]
        return ref.at[lo:hi] if half is None else ref.at[lo:hi, half * MID : half * MID + MID]

    def at(col, row, rows, half=None):
        return cut(out_ref.at[col * 4 + row], rows, half)

    def send(i, rows, dev):
        mail.go(n + i, cut(x_ref, rows, None), at(a, y, rows), dev)

    def fwd(i, ref, dev):
        mail.go(n + i, ref, ref, dev)

    def got(i, dst):
        mail.arrived(n + i, dst, XP)

    send(0, 0, XP)
    send(1, 0, U)
    send(2, 0, D)
    send(3, 1, U)
    send(4, 1, D)
    send(5, 1, XP)
    yield
    got(0, at(b, y, 0))
    fwd(6, at(b, y, 0), U)
    fwd(7, at(b, y, 0), D)
    yield
    got(1, at(a, down, 0))
    fwd(8, at(a, down, 0, 0), U)
    got(2, at(a, up, 0))
    fwd(9, at(a, up, 0, 1), D)
    yield
    got(3, at(a, down, 1))
    fwd(10, at(a, down, 1, 0), U)
    fwd(11, at(a, down, 1), XP)
    got(4, at(a, up, 1))
    fwd(12, at(a, up, 1, 1), D)
    fwd(13, at(a, up, 1), XP)
    yield
    got(5, at(b, y, 1))
    got(6, at(b, down, 0))
    fwd(14, at(b, down, 0, 0), U)
    got(7, at(b, up, 0))
    fwd(15, at(b, up, 0, 1), D)
    yield
    got(10, at(a, far, 1, 0))
    fwd(16, at(a, far, 1, 0), XP)
    got(12, at(a, far, 1, 1))
    fwd(17, at(a, far, 1, 1), XP)
    yield
    got(8, at(a, far, 0, 0))
    got(9, at(a, far, 0, 1))
    got(11, at(b, down, 1))
    got(13, at(b, up, 1))
    yield
    got(14, at(b, far, 0, 0))
    got(15, at(b, far, 0, 1))
    got(16, at(b, far, 1, 0))
    got(17, at(b, far, 1, 1))


def gather_y(me, mail, x_ref, out_ref):
    y, up, down, far = me.y, me.up, me.down, me.far
    U, D = me.up_dev, me.down_dev
    n = mail.slots(4)
    H = ROWS // 2
    mail.go(n, x_ref, out_ref.at[y], U)
    mail.go(n + 1, x_ref, out_ref.at[y], D)
    yield
    mail.arrived(n, out_ref.at[down], D)
    mail.go(n + 2, out_ref.at[down, 0:H], out_ref.at[down, 0:H], U)
    mail.arrived(n + 1, out_ref.at[up], U)
    mail.go(n + 3, out_ref.at[up, H:ROWS], out_ref.at[up, H:ROWS], D)
    yield
    mail.arrived(n + 2, out_ref.at[far, 0:H], D)
    mail.arrived(n + 3, out_ref.at[far, H:ROWS], U)


def scatter_y(me, mail, part, p2, p1, out):
    y, up, down, far = me.y, me.up, me.down, me.far
    U, D = me.up_dev, me.down_dev
    n = mail.slots(6)
    left, right = pl.ds(0, MID), pl.ds(MID, MID)
    mail.go(n, part.at[far, :, left], p2.at[0], U)
    mail.go(n + 3, part.at[down, :, left], p1.at[1, :, left], D)
    yield
    mail.go(n + 1, part.at[far, :, right], p2.at[1], D)
    mail.go(n + 2, part.at[up, :, right], p1.at[0, :, right], U)
    yield
    mail.arrived(n, p2.at[0], D)
    add(part.at[up, :, left], p2.at[0])
    mail.go(n + 4, part.at[up, :, left], p1.at[0, :, left], U)
    mail.arrived(n + 1, p2.at[1], U)
    add(part.at[down, :, right], p2.at[1])
    mail.go(n + 5, part.at[down, :, right], p1.at[1, :, right], D)
    yield
    mail.arrived(n + 2, p1.at[0, :, right], D)
    mail.arrived(n + 3, p1.at[1, :, left], U)
    mail.arrived(n + 4, p1.at[0, :, left], D)
    mail.arrived(n + 5, p1.at[1, :, right], U)
    out(0, ROWS, val(part.at[y]) + val(p1.at[0]) + val(p1.at[1]))


def val(ref):
    return ref[...].astype(WIDE)


def add(dst, src):
    dst[...] = (val(dst) + val(src)).astype(LOW)


def swap_seq(me, mail, own_ref, all_ref, lo, hi):
    n = mail.slots(7)
    for k in range(1, 8):
        to = (me.seq + k) % 8
        mail.go(n + k - 1, own_ref.at[to, :, lo:hi], all_ref.at[me.seq, me.dp, :, lo:hi], {"seq": to})
    yield
    for k in range(1, 8):
        came = (me.seq + 8 - k) % 8
        mail.arrived(n + k - 1, all_ref.at[came, me.dp, :, lo:hi], me.x_dev)


def gather_dp(me, mail, ref):
    z, h = me.z, me.h
    n = mail.slots(19)
    HD, ZU, ZD, TW = me.h_dev, me.z_up_dev, me.z_down_dev, me.twin_dev

    def at(zz, hh, half=None, twin=False):
        d = me.member(zz, hh, twin)
        return ref.at[:, d] if half is None else ref.at[4 * half : 4 * half + 4, d]

    def fwd(i, r, dev):
        mail.go(n + i, r, r, dev)

    def got(i, r):
        mail.arrived(n + i, r, TW)

    hs = (h, 1 - h)
    fwd(0, at(z, h), HD)
    fwd(1, at(z, h), ZU)
    fwd(2, at(z, h), ZD)
    fwd(9, at(z, h), TW)
    yield
    got(0, at(z, 1 - h))
    fwd(3, at(z, 1 - h), ZU)
    fwd(4, at(z, 1 - h), ZD)
    fwd(10, at(z, 1 - h), TW)
    yield
    for k in range(2):
        got(1 + 2 * k, at(me.z_down, hs[k]))
        fwd(5 + 2 * k, at(me.z_down, hs[k], 0), ZU)
        fwd(11 + 2 * k, at(me.z_down, hs[k]), TW)
        yield
        got(2 + 2 * k, at(me.z_up, hs[k]))
        fwd(6 + 2 * k, at(me.z_up, hs[k], 1), ZD)
        fwd(12 + 2 * k, at(me.z_up, hs[k]), TW)
        yield
    for k in range(2):
        got(5 + 2 * k, at(me.z_far, hs[k], 0))
        fwd(15 + 2 * k, at(me.z_far, hs[k], 0), TW)
        got(6 + 2 * k, at(me.z_far, hs[k], 1))
        fwd(16 + 2 * k, at(me.z_far, hs[k], 1), TW)
        yield
    got(9, at(z, h, twin=True))
    got(10, at(z, 1 - h, twin=True))
    for k in range(2):
        got(11 + 2 * k, at(me.z_down, hs[k], twin=True))
        got(12 + 2 * k, at(me.z_up, hs[k], twin=True))
        got(15 + 2 * k, at(me.z_far, hs[k], 0, twin=True))
        got(16 + 2 * k, at(me.z_far, hs[k], 1, twin=True))


def swap_y(me, mail, own_ref, all_ref):
    n = mail.slots(3)
    for k in (2, 1, 3):
        to = (me.y + k) % 4
        mail.go(n + k - 1, own_ref.at[to], all_ref.at[me.seq, me.dp], {"seq": me.a * 4 + to})
    yield
    for k in (1, 3, 2):
        came = me.a * 4 + (me.y + 4 - k) % 4
        mail.arrived(n + k - 1, all_ref.at[came, me.dp], me.up_dev)


def slab(me, ref, x, z, half=None, twin=False):
    d = me.member(z, x // 2, twin)
    first = x % 2 * 4
    return ref.at[pl.ds(first, 4), d] if half is None else ref.at[pl.ds(first + 2 * half, 2), d]


def gather_xz(me, mail, ref):
    n = mail.slots(36)
    XU, XD, ZU, ZD, TW = me.x_up_dev, me.x_down_dev, me.z_up_dev, me.z_down_dev, me.twin_dev
    z, zu, zd, zf = me.z, me.z_up, me.z_down, me.z_far
    xs = (me.x, me.x_down, me.x_up, me.x_far)

    def at(x, zz, half=None, twin=False):
        return slab(me, ref, x, zz, half, twin)

    def fwd(i, r, dev):
        mail.go(n + i, r, r, dev)

    def got(i, r):
        mail.arrived(n + i, r, TW)

    def z_first(k):
        fwd(4 + 4 * k, at(xs[k], z), ZU)
        fwd(5 + 4 * k, at(xs[k], z), ZD)
        fwd(20 + 4 * k, at(xs[k], z), TW)

    def z_second(k):
        got(4 + 4 * k, at(xs[k], zd))
        fwd(6 + 4 * k, at(xs[k], zd, 0), ZU)
        fwd(21 + 4 * k, at(xs[k], zd), TW)
        got(5 + 4 * k, at(xs[k], zu))
        fwd(7 + 4 * k, at(xs[k], zu, 1), ZD)
        fwd(22 + 4 * k, at(xs[k], zu), TW)

    def z_third(k):
        got(6 + 4 * k, at(xs[k], zf, 0))
        got(7 + 4 * k, at(xs[k], zf, 1))
        fwd(23 + 4 * k, at(xs[k], zf), TW)

    z_first(0)
    yield
    fwd(0, at(me.x, z), XU)
    fwd(1, at(me.x, z), XD)
    yield
    got(0, at(me.x_down, z))
    fwd(2, at(me.x_down, z, 0), XU)
    got(1, at(me.x_up, z))
    fwd(3, at(me.x_up, z, 1), XD)
    z_first(1)
    z_first(2)
    yield
    got(2, at(me.x_far, z, 0))
    got(3, at(me.x_far, z, 1))
    z_first(3)
    yield
    for k in range(4):
        z_second(k)
        yield
    for k in range(4):
        z_third(k)
        yield
    for k in range(4):
        for i, zz in enumerate((z, zd, zu, zf)):
            got(20 + 4 * k + i, at(xs[k], zz, twin=True))


def add_slabs(dst, *sources):
    def one(i, carry):
        total = val(dst.at[i])
        for source in sources:
            total = total + val(source.at[i])
        dst[i] = total.astype(LOW)
        return carry

    lax.fori_loop(0, dst.shape[0], one, 0)


def halved(ref, half):
    k = ref.shape[0] // 2
    return ref.at[half * k : half * k + k]


class RingSum:
    def __init__(self, mail, at, places, devices, over, near):
        self.mail, self.at, self.places, self.devices = mail, at, places, devices
        self.over, self.near = over, near
        self.n = mail.slots(6)

    def first(self):
        own, up, down, far = self.places
        U, D = self.devices
        go, n = self.mail.go, self.n
        go(n, halved(self.at(far), 0), self.over.at[0], U)
        go(n + 1, halved(self.at(far), 1), self.over.at[1], D)
        go(n + 2, halved(self.at(up), 1), halved(self.near.at[0], 1), U)
        go(n + 3, halved(self.at(down), 0), halved(self.near.at[1], 0), D)

    def second(self):
        own, up, down, far = self.places
        U, D = self.devices
        go, got, n = self.mail.go, self.mail.arrived, self.n
        got(n, self.over.at[0], D)
        add_slabs(halved(self.at(up), 0), self.over.at[0])
        go(n + 4, halved(self.at(up), 0), halved(self.near.at[0], 0), U)
        got(n + 1, self.over.at[1], U)
        add_slabs(halved(self.at(down), 1), self.over.at[1])
        go(n + 5, halved(self.at(down), 1), halved(self.near.at[1], 1), D)

    def third(self):
        own = self.places[0]
        U, D = self.devices
        got, n = self.mail.arrived, self.n
        got(n + 2, halved(self.near.at[0], 1), D)
        got(n + 3, halved(self.near.at[1], 0), U)
        got(n + 4, halved(self.near.at[0], 0), D)
        got(n + 5, halved(self.near.at[1], 1), U)
        add_slabs(self.at(own), self.near.at[0], self.near.at[1])


def twin_sum(me, mail, stage, acc, order, product, kept=None):
    slots = stage.shape[0]
    n = mail.slots(len(order))

    def settle(i):
        mail.arrived(n + i, acc.at[order[i]], me.twin_dev)
        add_slabs(acc.at[order[i]], stage.at[i % slots, :, me.core])
        if kept is not None:
            kept(i)

    for i, s in enumerate(order):
        if i >= slots:
            mail.sent(n + i - slots)
        product(s, stage.at[i % slots])
        mail.go(n + i, stage.at[i % slots, :, 1 - me.core], acc.at[s], me.twin_dev)
        if i > 0:
            settle(i - 1)
        yield
    settle(len(order) - 1)
    for i in range(max(0, len(order) - slots), len(order)):
        mail.sent(n + i)


def scatter_z(me, mail, acc, z_over, z_near):
    xs = (me.x_far, me.x, me.x_up, me.x_down)
    zs = (me.z, me.z_up, me.z_down, me.z_far)

    def at(x):
        return lambda z: acc.at[pl.ds(x % 2 * 4, 4), z * 2 + x // 2]

    rings = [RingSum(mail, at(x), zs, (me.z_up_dev, me.z_down_dev), z_over.at[k], z_near.at[k]) for k, x in enumerate(xs)]
    rings[0].first()
    yield
    rings[2].first()
    rings[3].first()
    rings[1].first()
    yield
    for k in (0, 2, 3, 1):
        rings[k].second()
        yield
    for k in (0, 2, 3):
        rings[k].third()
        yield
    rings[1].third()


def scatter_x(me, mail, at, x_over, x_near):
    places = (me.x, me.x_up, me.x_down, me.x_far)
    ring = RingSum(mail, at, places, (me.x_up_dev, me.x_down_dev), x_over, x_near)
    ring.first()
    yield
    ring.second()
    yield
    ring.third()


def scatter_hz(me, mail, acc, z_over, z_near, h_near):
    hs = (1 - me.h, me.h)
    zs = (me.z, me.z_up, me.z_down, me.z_far)

    def at(h):
        return lambda z: acc.at[:, z * 2 + h]

    rings = [RingSum(mail, at(h), zs, (me.z_up_dev, me.z_down_dev), z_over.at[k], z_near.at[k]) for k, h in enumerate(hs)]
    n = mail.slots(1)
    rings[0].first()
    rings[1].first()
    yield
    for k in range(2):
        rings[k].second()
        yield
    rings[0].third()
    mail.go(n, at(1 - me.h)(me.z), h_near, me.h_dev)
    yield
    rings[1].third()
    yield
    mail.arrived(n, h_near, me.h_dev)
    add_slabs(at(me.h)(me.z), h_near)


def send_y(me, mail, slab, result):
    n = mail.slots(3)
    for k in (2, 1, 3):
        to = (me.y + k) % 4
        mail.go(n + k - 1, slab.at[to], result.at[me.y], {"seq": me.a * 4 + to})
    result[me.y] = slab[me.y]
    yield
    for k in (1, 3, 2):
        mail.arrived(n + k - 1, result.at[(me.y + 4 - k) % 4], me.up_dev)


def send_seq(me, mail, slab, result, lo, hi):
    n = mail.slots(7)
    for k in range(1, 8):
        to = (me.seq + k) % 8
        mail.go(n + k - 1, slab.at[to, :, lo:hi], result.at[me.seq], {"seq": to})
    result[me.seq] = slab[me.seq, :, lo:hi]
    yield
    for k in range(1, 8):
        mail.arrived(n + k - 1, result.at[(me.seq + 8 - k) % 8], me.x_dev)


def scatter_bufs():
    late = ROWS - FIRST
    shapes = ((4, late, MODEL), (2, late, MID), (2, late, MODEL), (4, FIRST, MID), (4, FIRST, MODEL), (1, FIRST, MODEL))
    return [pltpu.VMEM(shape, LOW) for shape in shapes]


def scatter_seq(me, mail, part, bufs, out):
    a, b, y, up, down, far = me.a, me.b, me.y, me.up, me.down, me.far
    XP, U, D = me.x_dev, me.up_dev, me.down_dev
    qx, q2, q1, p2, p1, px = bufs
    n = mail.slots(23)
    halves = (pl.ds(0, MID), pl.ds(MID, MID))

    def go(i, src, dst, dev):
        mail.go(n + i, src, dst, dev)

    def got(i, dst):
        mail.arrived(n + i, dst, XP)

    def at(col, row, rows, half=None):
        lo, hi = ((0, FIRST), (FIRST, ROWS))[rows]
        ref = part.at[col * 4 + row]
        return ref.at[lo:hi] if half is None else ref.at[lo:hi, halves[half]]

    def lane(ref, k, half):
        return ref.at[k, :, halves[half]]

    for k, row in enumerate((far, down, up, y)):
        go(k, at(b, row, 1), qx.at[row], XP)
    cols = (b, a)

    def p_first(k):
        c, s = cols[k], 10 + 6 * k
        go(s, at(c, far, 0, 0), p2.at[2 * k], U)
        go(s + 1, at(c, far, 0, 1), p2.at[2 * k + 1], D)
        go(s + 2, at(c, up, 0, 1), lane(p1, 2 * k, 1), U)
        go(s + 3, at(c, down, 0, 0), lane(p1, 2 * k + 1, 0), D)

    def p_second(k):
        c, s = cols[k], 10 + 6 * k
        got(s, p2.at[2 * k])
        add(at(c, up, 0, 0), p2.at[2 * k])
        go(s + 4, at(c, up, 0, 0), lane(p1, 2 * k, 0), U)
        got(s + 1, p2.at[2 * k + 1])
        add(at(c, down, 0, 1), p2.at[2 * k + 1])
        go(s + 5, at(c, down, 0, 1), lane(p1, 2 * k + 1, 1), D)

    def p_third(k):
        s = 10 + 6 * k
        got(s + 2, lane(p1, 2 * k, 1))
        got(s + 3, lane(p1, 2 * k + 1, 0))
        got(s + 4, lane(p1, 2 * k, 0))
        got(s + 5, lane(p1, 2 * k + 1, 1))
        return val(at(cols[k], y, 0)) + val(p1.at[2 * k]) + val(p1.at[2 * k + 1])

    p_first(0)
    yield
    p_first(1)
    yield
    got(0, qx.at[far])
    add(at(a, far, 1), qx.at[far])
    go(4, at(a, far, 1, 0), q2.at[0], U)
    go(5, at(a, far, 1, 1), q2.at[1], D)
    yield
    p_second(0)
    yield
    got(1, qx.at[down])
    add(at(a, down, 1), qx.at[down])
    go(6, at(a, down, 1, 0), lane(q1, 1, 0), D)
    got(2, qx.at[up])
    add(at(a, up, 1), qx.at[up])
    go(7, at(a, up, 1, 1), lane(q1, 0, 1), U)
    yield
    p_second(1)
    yield
    rows = p_third(0)
    own = at(b, y, 0)
    own[...] = rows.astype(LOW)
    go(22, own, px.at[0], XP)
    yield
    got(4, q2.at[0])
    add(at(a, up, 1, 0), q2.at[0])
    go(8, at(a, up, 1, 0), lane(q1, 0, 0), U)
    got(5, q2.at[1])
    add(at(a, down, 1, 1), q2.at[1])
    go(9, at(a, down, 1, 1), lane(q1, 1, 1), D)
    yield
    rows = p_third(1)
    got(22, px.at[0])
    out(0, FIRST, rows + val(px.at[0]))
    yield
    got(3, qx.at[y])
    got(6, lane(q1, 1, 0))
    got(7, lane(q1, 0, 1))
    got(8, lane(q1, 0, 0))
    got(9, lane(q1, 1, 1))
    out(FIRST, ROWS, val(at(a, y, 1)) + val(qx.at[y]) + val(q1.at[0]) + val(q1.at[1]))


def run(*tasks):
    tasks = list(tasks)
    while tasks:
        for task in list(tasks):
            if next(task, tasks) is tasks:
                tasks.remove(task)


def step(task, count=1):
    for _ in range(count):
        next(task, None)


def finish(task, *others):
    k = 0
    while next(task, others) is not others:
        k += 1
        if k % 2 == 0 and others:
            step(others[k // 2 % len(others)])
def dot(a, b, dims=((1,), (0,))):
    return lax.dot_general(a, b, (dims, ((), ())), preferred_element_type=WIDE)


def row_scale(values):
    return lax.rsqrt(jnp.mean(values * values, axis=-1, keepdims=True) + EPS)


def column(row_ref):
    shape = (16, 16)
    here = lax.broadcasted_iota(jnp.int32, shape, 0) == lax.broadcasted_iota(jnp.int32, shape, 1)
    return jnp.sum(jnp.where(here, row_ref[...].astype(WIDE), 0.0), axis=1, keepdims=True)


def live_rows(count_ref):
    return jnp.where(lax.broadcasted_iota(jnp.int32, (ROWS, 1), 0) < count_ref[0, 0], 1.0, 0.0).astype(WIDE)


def front_kernel(
    x_ref, count_ref, owner_ref, cot_ref, attn_ref, mlp_ref, gain_one, gain_two,
    one_out, wa_out, grad_all, wm, qkv_out, probs_out, att_out, two_all, resid,
    one_all, wa, grad_own, qkv, probs, att, ones_t, att_t, two, wa_own, wm_own, pos_k, part, qx, q2, q1, p2, p1, px, send, recv, local_sem,
):
    me = Place()
    mail = Mail(send, recv)
    saves = []

    def save(src, dst):
        copy = pltpu.make_async_copy(src, dst, local_sem.at[len(saves)])
        copy.start()
        saves.append(copy)
        return copy

    ready = greet(me.peers() + [me.h_dev, me.z_up_dev, me.z_down_dev, me.twin_dev, me.x_up_dev, me.x_down_dev])
    live = live_rows(count_ref)
    x = x_ref[...].astype(WIDE)
    one_all[me.seq] = (x * row_scale(x) * live).astype(LOW)
    ready()
    gather_one = gather_seq(me, mail, one_all.at[me.seq], one_all)
    step(gather_one)
    gain = column(gain_one)
    for slot in range(4):
        weight = attn_ref[:, slot, :].astype(WIDE)
        if slot < 3:
            weight = weight * gain
        for to in range(8):
            wa_own[to, :, slot * PART : slot * PART + PART] = weight[:, to * PART : to * PART + PART].astype(LOW)
    swap_a = swap_seq(me, mail, wa_own, wa, 0, PROJ)
    step(swap_a)
    gain = column(gain_two)
    units = mlp_ref.shape[2] // 4
    for slot in range(3):
        weight = mlp_ref[:, slot, :].astype(WIDE)
        if slot < 2:
            weight = weight * gain
        for to in range(4):
            piece = weight if to == 0 else pltpu.roll(weight, (4 - to) * units, 1)
            piece = piece[:, 0:UNITS]
            piece = jnp.where(lax.broadcasted_iota(jnp.int32, piece.shape, 1) < units, piece, 0.0).astype(LOW)
            for tile in range(UNITS // 128):
                first = PAIR + tile * 128 if slot == 2 else (2 * tile + slot) * 128
                wm_own[to, :, first : first + 128] = piece[:, tile * 128 : tile * 128 + 128]
    swap_m = swap_y(me, mail, wm_own, wm)
    step(swap_m)
    keep_m = save(wm_own.at[me.y], wm.at[me.seq, me.dp])
    for block in range(8):
        columns = lax.broadcasted_iota(jnp.int32, (1, ROWS), 1)
        pos_k[:, block * ROWS : block * ROWS + ROWS] = columns + owner_ref[0, block] * ROWS
    wa[pl.ds(me.seq, 1), pl.ds(me.dp, 1), :, 0:PROJ] = wa_own[pl.ds(me.seq, 1), :, 0:PROJ][None]
    for k in range(8):
        wa[k, pl.ds(me.dp, 1), :, PROJ:] = wa_own[k, :, PROJ:][None]
    step(swap_a)
    gather_wa = gather_dp(me, mail, wa)
    step(gather_wa)
    grad_own[...] = (cot_ref[...].astype(WIDE) * live).astype(LOW)
    save(grad_own, grad_all.at[me.y])
    step(gather_one)
    step(gather_wa)
    step(gather_one)
    step(gather_wa, 2)
    step(gather_one)
    step(gather_wa, 2)
    step(swap_m)
    keep_m.wait()
    gather_wm = gather_xz(me, mail, wm)
    step(gather_wm, 2)
    step(gather_one, 2)
    gather_g = gather_y(me, mail, grad_own, grad_all)
    step(gather_g)
    step(gather_one)
    run(gather_wa)

    def project(i, carry):
        rows = one_all[pl.ds(i * 2, 2)].reshape(2 * ROWS, MODEL)
        weight = wa[:, :, :, 0:PROJ].reshape(MODEL, PROJ)
        qkv[pl.ds(pl.multiple_of(i * 256, 256), 256), :] = dot(rows, weight).astype(LOW)
        return carry

    lax.fori_loop(me.a * 2, me.a * 2 + 2, project, 0)
    run(gather_one)
    step(gather_wm)
    save(wa, wa_out)

    def attend(i, carry):
        first = pl.multiple_of(i * ROWS, ROWS)
        rows = pl.ds(first, ROWS)
        allowed = pos_k[...] <= lax.broadcasted_iota(jnp.int32, (ROWS, 1), 0) + owner_ref[0, i] * ROWS
        for head in range(2):
            lo, hi = head * HEAD_DIM, (head + 1) * HEAD_DIM
            q = qkv[rows, lo:hi]
            k = qkv[:, PART + lo : PART + hi]
            v = qkv[:, 2 * PART + lo : 2 * PART + hi]
            odds = jnp.exp2(math.log2(8 * ROWS) - dot(q, k, ((1,), (1,))) * (math.log2(math.e) / math.sqrt(HEAD_DIM)))
            p = jnp.where(allowed, 1.0 / (1.0 + odds), 0.0).astype(LOW)
            probs[head, rows, :] = p
            att[rows, lo:hi] = dot(p, v).astype(LOW)
        return carry

    def out_project(col):
        rows = att[pl.ds(pl.multiple_of(col * 512, 512), 512), :]

        def piece(k, carry):
            weight = wa[k, :, :, PROJ:].reshape(PART, PART)
            columns = pl.ds(pl.multiple_of(k * PART, PART), PART)
            part[pl.ds(col * 4, 4), :, columns] = dot(rows, weight).reshape(4, ROWS, PART).astype(LOW)
            return carry

        lax.fori_loop(0, 8, piece, 0)

    lax.fori_loop(me.b * 2, me.b * 2 + 2, project, 0)
    step(gather_g)
    save(qkv, qkv_out)

    def write(lo, hi, rows):
        total = x_ref[lo:hi].astype(WIDE) + rows
        resid[lo:hi] = total
        two[lo:hi] = (total * row_scale(total) * live[lo:hi]).astype(LOW)

    scatter = scatter_seq(me, mail, part, (qx, q2, q1, p2, p1, px), write)
    lax.fori_loop(me.b * 4, me.b * 4 + 4, attend, 0)
    out_project(me.b)
    step(scatter)
    step(gather_wm)
    lax.fori_loop(me.a * 4, me.a * 4 + 4, attend, 0)
    out_project(me.a)
    step(scatter)
    save(probs, probs_out)
    finish(scatter, gather_wm)
    gather_two = gather_y(me, mail, two, two_all)
    step(gather_two)
    save(two, two_all.at[me.y])
    step(gather_wm)

    def turn(s, carry):
        columns = pl.ds(pl.multiple_of(s * 256, 256), 256)
        ones_t[s] = one_all[:, :, columns].reshape(8 * ROWS, 256).T
        return carry

    att_t[...] = att[...].T
    save(att_t, att_out)
    for i in range(4):
        lax.fori_loop(2 * i, 2 * i + 2, turn, 0)
        step(gather_wm)
        if i == 1:
            step(gather_two)
    save(ones_t, one_out)
    run(gather_wm, gather_g, gather_two)
    for copy in saves:
        if copy is not keep_m:
            copy.wait()
    mail.finish()


def front(x, counts, owners, cot, attn_weight, mlp_weight, gain_one, gain_two):
    vmem, anywhere = pl.BlockSpec(memory_space=pltpu.VMEM), pl.BlockSpec(memory_space=pl.ANY)
    shape = jax.ShapeDtypeStruct
    count = 7 + 18 + 19 + 3 + 36 + 4 + 23 + 4
    return pl.pallas_call(
        front_kernel,
        out_shape=(
            shape((8, 256, 1024), LOW), shape((8, 16, 16, 1024), LOW), shape((4, ROWS, MODEL), LOW),
            shape((8, 16, 16, SLAB), LOW), shape((1024, PROJ), LOW), shape((2, 1024, 1024), LOW),
            shape((PART, 1024), LOW), shape((4, ROWS, MODEL), LOW), shape((ROWS, MODEL), WIDE),
        ),
        in_specs=[vmem] + [pl.BlockSpec(memory_space=pltpu.SMEM)] * 2 + [vmem] * 5,
        out_specs=(anywhere,) * 8 + (vmem,),
        scratch_shapes=[
            pltpu.VMEM((8, ROWS, MODEL), LOW), pltpu.VMEM((8, 16, 16, 1024), LOW), pltpu.VMEM((ROWS, MODEL), LOW),
            pltpu.VMEM((1024, PROJ), LOW), pltpu.VMEM((2, 1024, 1024), LOW), pltpu.VMEM((1024, PART), LOW),
            pltpu.VMEM((8, 256, 1024), LOW), pltpu.VMEM((PART, 1024), LOW), pltpu.VMEM((ROWS, MODEL), LOW),
            pltpu.VMEM((8, 16, 1024), LOW), pltpu.VMEM((4, 16, SLAB), LOW), pltpu.VMEM((1, 1024), jnp.int32),
            pltpu.VMEM((8, ROWS, MODEL), LOW),
        ]
        + scatter_bufs()
        + [pltpu.SemaphoreType.DMA((count,)), pltpu.SemaphoreType.DMA((count,)), pltpu.SemaphoreType.DMA((9,))],
        compiler_params=pltpu.CompilerParams(collective_id=1, has_side_effects=True, vmem_limit_bytes=56 * 2**20),
        name="front",
    )(x, counts, owners, cot, attn_weight, mlp_weight, gain_one, gain_two)
def mlp_kernel(
    resid, cot_ref, count_ref, two_all, grad_all, wm_all,
    acc_out, branch_out, branch_grads, grad_resid, down_out,
    wm, grads, twos, hidden, pair, part, branch, p2, p1, grad_branch,
    stage_d, acc_d, z_over, z_near, stage, acc, send, recv, local_sem, wm_sem,
):
    me = Place()
    mail = Mail(send, recv)
    saves = []

    def save(src, dst):
        copy = pltpu.make_async_copy(src, dst, local_sem.at[len(saves)])
        copy.start()
        saves.append(copy)
        return copy

    live = live_rows(count_ref)
    loads = [save(two_all, twos), save(grad_all, grads)]

    def weights(j, wide):
        for first, each, sem in ((0, 256, 0), (PAIR, 128, 6)):
            columns = pl.ds(pl.multiple_of(first + j * each, 128), wide * each)
            yield pltpu.make_async_copy(
                wm_all.at[:, :, :, columns], wm.at[:, :, :, columns], wm_sem.at[sem + j // 2]
            )

    for j in range(0, UNITS // 128, 2):
        for copy in weights(j, min(2, UNITS // 128 - j)):
            copy.start()
    ready = greet([me.x_dev, me.up_dev, me.down_dev, me.z_up_dev, me.z_down_dev, me.twin_dev])
    for load in loads:
        load.wait()

    def tall(ref, columns=slice(None)):
        values = ref[:, :, columns]
        return values.reshape(4 * ROWS, values.shape[2])

    def put(ref, columns, values):
        ref[:, :, columns] = values.reshape(4, ROWS, values.shape[1]).astype(LOW)

    def ahead(j, wide):
        for copy in weights(j, wide):
            copy.wait()
        start = pl.multiple_of(j * 128, 128)
        width = wide * 128
        weight = wm[:, :, :, pl.ds(2 * start, 2 * width)].reshape(MODEL, 2 * width)
        gate_up = dot(tall(twos), weight)
        down = wm[:, :, :, pl.ds(PAIR + start, width)].reshape(MODEL, width)
        grad_hidden = dot(tall(grads), down)
        low, pairs = [], []
        for i in range(wide):
            gate = gate_up[:, i * 256 : i * 256 + 128]
            up = gate_up[:, i * 256 + 128 : i * 256 + 256]
            grad = grad_hidden[:, i * 128 : i * 128 + 128]
            squashed = 1.0 / (1.0 + jnp.exp(-gate))
            active = gate * squashed
            low.append(active * up)
            pairs.append(grad * up * (squashed * (1.0 + gate * (1.0 - squashed))))
            pairs.append(grad * active)
        put(hidden, pl.ds(start, width), jnp.concatenate(low, axis=1))
        put(pair, pl.ds(2 * start, 2 * width), jnp.concatenate(pairs, axis=1))

    def ahead_tile(j, carry):
        ahead(2 * j, 2)
        return carry

    def back(s, carry):
        columns = pl.ds(pl.multiple_of(s * 256, 256), 256)
        weight = wm[s, :, :, 0:PAIR].reshape(256, PAIR)
        put(part, columns, dot(tall(pair), weight, ((1,), (1,))))
        return carry

    def down_back(s, carry):
        columns = pl.ds(pl.multiple_of(s * 256, 256), 256)
        weight = wm[s, :, :, PAIR:].reshape(256, UNITS)
        put(branch, columns, dot(tall(hidden), weight, ((1,), (1,))))
        return carry

    def write(lo, hi, rows):
        x = resid[lo:hi]
        scale = row_scale(x)
        hat = x * scale
        inner = jnp.mean(rows * hat, axis=-1, keepdims=True)
        total = cot_ref[lo:hi].astype(WIDE) * live[lo:hi] + scale * (rows - hat * inner)
        grad_resid[lo:hi] = total
        grad_branch[lo:hi] = total.astype(LOW)

    order = [me.a * 4 + i for i in range(4)] + [me.b * 4 + i for i in range(4)]

    def columns_t(ref, s):
        return ref[:, :, pl.ds(pl.multiple_of(s * 256, 256), 256)].reshape(4 * ROWS, 256).T

    def down_product(s, out):
        terms = dot(columns_t(grads, s), hidden[...].reshape(4 * ROWS, UNITS))
        out[...] = terms.reshape(8, 2, 16, UNITS).astype(LOW)

    def pair_product(s, out):
        terms = dot(columns_t(twos, s), pair[...].reshape(4 * ROWS, PAIR))
        out[...] = terms.reshape(8, 2, 16, PAIR).astype(LOW)

    def kept(i):
        save(acc.at[order[i]], acc_out.at[order[i]])

    scatter = scatter_y(me, mail, part, p2, p1, write)
    twin_d = twin_sum(me, mail, stage_d, acc_d, order, down_product)
    twin = twin_sum(me, mail, stage, acc, order, pair_product, kept)
    sums = scatter_z(me, mail, acc_d, z_over, z_near)
    gather = gather_seq(me, mail, grad_branch, branch_grads)
    lax.fori_loop(0, 5, ahead_tile, 0)
    ahead(10, 1)
    lax.fori_loop(0, 4, back, 0)
    ready()
    step(scatter)
    lax.fori_loop(4, 8, back, 0)
    step(scatter)
    run(twin_d)
    step(sums, 2)
    step(scatter)
    step(twin, 3)
    step(sums, 2)
    step(twin, 3)
    step(scatter)
    step(gather)
    keep = save(grad_branch, branch_grads.at[me.seq])
    step(sums, 2)
    run(twin)
    step(gather)
    for i in range(5):
        if i < 4:
            lax.fori_loop(2 * i, 2 * i + 2, down_back, 0)
        step(sums)
        step(gather)
    save(branch, branch_out)
    run(sums)
    for x in range(4):
        save(acc_d.at[x % 2 * 4 : x % 2 * 4 + 4, me.z * 2 + x // 2], down_out.at[x])
    run(gather)
    for copy in saves[2:]:
        copy.wait()
    mail.finish()


def mlp(resid, cot, counts, twos, grads, wm):
    vmem, anywhere = pl.BlockSpec(memory_space=pltpu.VMEM), pl.BlockSpec(memory_space=pl.ANY)
    shape = jax.ShapeDtypeStruct
    blocks = (4, ROWS, MODEL)
    count = 6 + 8 + 8 + 24 + 18
    return pl.pallas_call(
        mlp_kernel,
        out_shape=(
            shape((8, 8, 16, PAIR), LOW), shape(blocks, LOW), shape((8, ROWS, MODEL), LOW), shape((ROWS, MODEL), WIDE),
            shape((4, 4, 16, UNITS), LOW),
        ),
        in_specs=[vmem] * 2 + [pl.BlockSpec(memory_space=pltpu.SMEM)] + [anywhere] * 3,
        out_specs=(anywhere,) * 3 + (vmem, anywhere),
        scratch_shapes=[
            pltpu.VMEM((8, 16, 16, SLAB), LOW), pltpu.VMEM(blocks, LOW), pltpu.VMEM(blocks, LOW),
            pltpu.VMEM((4, ROWS, UNITS), LOW), pltpu.VMEM((4, ROWS, PAIR), LOW), pltpu.VMEM(blocks, LOW),
            pltpu.VMEM(blocks, LOW), pltpu.VMEM((2, ROWS, MID), LOW), pltpu.VMEM((2, ROWS, MODEL), LOW),
            pltpu.VMEM((ROWS, MODEL), LOW),
            pltpu.VMEM((2, 8, 2, 16, UNITS), LOW), pltpu.VMEM((8, 8, 16, UNITS), LOW),
            pltpu.VMEM((4, 2, 2, 16, UNITS), LOW), pltpu.VMEM((4, 2, 4, 16, UNITS), LOW),
            pltpu.VMEM((2, 8, 2, 16, PAIR), LOW), pltpu.VMEM((8, 8, 16, PAIR), LOW),
            pltpu.SemaphoreType.DMA((count,)), pltpu.SemaphoreType.DMA((count,)), pltpu.SemaphoreType.DMA((16,)), pltpu.SemaphoreType.DMA((12,)),
        ],
        compiler_params=pltpu.CompilerParams(collective_id=2, has_side_effects=True, vmem_limit_bytes=62 * 2**20),
        name="mlp",
    )(resid, cot, counts, twos, grads, wm)
def back_kernel(
    grad_resid, x_ref, count_ref, resid, attn_ref, mlp_ref, gain_one, gain_two, down_all, branch_grads, branch_all, acc_all, one_all, wa_all, qkv_all, probs_all, att_all,
    layer_out, input_grad, attn_grad, mlp_grad, gain_grads,
    down, dx_over, dx_near, down_own, pair_own, in_own, acc, z_over, z_near, x_over, x_near, grads, branch, b2, b1, part, qx, q2, q1, p2, p1, px,
    wa, acc_a, az_over, az_near, h_near, ones_t, qkv, probs, att_t, grad_att, grad_proj, grad_k, grad_v, stage_a,
    send, recv, local_sem,
):
    me = Place()
    mail = Mail(send, recv)
    loads = []
    live = live_rows(count_ref)

    def load(src, dst):
        copy = pltpu.make_async_copy(src, dst, local_sem.at[len(loads)])
        copy.start()
        loads.append(copy)
        return copy

    load_acc = [load(acc_all.at[pl.ds(col * 4, 4)], acc.at[pl.ds(col * 4, 4)]) for col in (me.a, me.b)]
    load_down = load(down_all, down)
    load_branch = load(branch_all, branch)
    ready = greet(me.peers() + [me.h_dev, me.z_up_dev, me.z_down_dev, me.x_up_dev, me.x_down_dev, me.twin_dev])
    load_grads = load(branch_grads, grads)
    load_wa = load(wa_all, wa)
    waits = [load(*both) for both in ((qkv_all, qkv), (att_all, att_t), (one_all, ones_t))]
    fetch = [load(probs_all.at[:, 256 * i : 256 * i + 256], probs.at[i]) for i in range(2)]
    order = [me.a * 4 + i for i in range(4)] + [me.b * 4 + i for i in range(4)]

    def columns_of(s, width=256):
        return pl.ds(pl.multiple_of(s * width, width), width)

    def down_sums():
        yield from scatter_x(me, mail, lambda x: down.at[x], dx_over, dx_near)
        yield from send_y(me, mail, down.at[me.x], down_own)

    def pair_sums():
        yield from scatter_z(me, mail, acc, z_over, z_near)
        yield from scatter_x(me, mail, lambda x: acc.at[pl.ds(x % 2 * 4, 4), me.z * 2 + x // 2], x_over, x_near)
        yield from send_y(me, mail, acc.at[pl.ds(me.a * 4, 4), me.z * 2 + me.h], pair_own)

    downs = down_sums()
    sums = pair_sums()

    load_acc[0].wait()
    ready()
    step(sums)
    load_acc[1].wait()
    step(sums)
    load_down.wait()
    step(downs)
    def write_out(lo, hi, rows):
        layer_out[lo:hi] = (live[lo:hi] * (resid[lo:hi] + rows)).astype(LOW)

    out_sum = scatter_y(me, mail, branch, b2, b1, write_out)
    load_branch.wait()
    step(out_sum, 2)
    load_grads.wait()
    def write_grad(lo, hi, rows):
        x = x_ref[lo:hi].astype(WIDE)
        scale = row_scale(x)
        hat = x * scale
        inner = jnp.mean(rows * hat, axis=-1, keepdims=True)
        input_grad[lo:hi] = grad_resid[lo:hi] + live[lo:hi] * scale * (rows - hat * inner)

    grad_sum = scatter_seq(me, mail, part, (qx, q2, q1, p2, p1, px), write_grad)

    load_wa.wait()
    for wait in waits:
        wait.wait()
    head_scale = 1.0 / math.sqrt(HEAD_DIM)

    def attended_grad(i, carry):
        total = jnp.zeros((256, PART), WIDE)
        for k in range(8):
            rows = grads[pl.ds(i * 2, 2), :, k * PART : k * PART + PART].reshape(256, PART)
            total = total + dot(rows, wa[k, :, :, PROJ:].reshape(PART, PART), ((1,), (1,)))
        grad_att[columns_of(i), :] = total.astype(LOW)
        return carry

    lax.fori_loop(0, 4, attended_grad, 0)
    grad_k[...] = jnp.zeros_like(grad_k)
    grad_v[...] = jnp.zeros_like(grad_v)

    def attend_back(i):
        rows = pl.ds(256 * i, 256)
        for head in range(2):
            lo, hi = head * HEAD_DIM, (head + 1) * HEAD_DIM
            low = probs[i % 2, head]
            p = low.astype(WIDE)
            g = grad_att[rows, lo:hi]
            back = dot(g, qkv[:, 2 * PART + lo : 2 * PART + hi], ((1,), (1,)))
            grad_s = (back * (p * (1.0 - p))).astype(LOW)
            grad_q = dot(grad_s, qkv[:, PART + lo : PART + hi]) * head_scale
            grad_proj[rows, lo:hi] = grad_q.astype(LOW)
            grad_v[:, lo:hi] += dot(low, g, ((0,), (0,)))
            grad_k[:, lo:hi] += dot(grad_s, qkv[rows, lo:hi], ((0,), (0,)))

    for i in range(4):
        fetch[i].wait()
        attend_back(i)
        if i < 2:
            fetch.append(load(probs_all.at[:, 256 * i + 512 : 256 * i + 768], probs.at[i]))
        if i == 1:
            step(sums)
        if i == 2:
            step(downs)
        if i == 3:
            step(out_sum)
    grad_proj[:, PART : 2 * PART] = (grad_k[...] * head_scale).astype(LOW)
    grad_proj[:, 2 * PART :] = grad_v[...].astype(LOW)

    def norm_terms(col):
        rows = grad_proj[columns_of(col, 512), :]

        def piece(s, carry):
            weight = wa[s, :, :, 0:PROJ].reshape(256, PROJ)
            terms = dot(rows, weight, ((1,), (1,)))
            part[pl.ds(col * 4, 4), :, columns_of(s)] = terms.reshape(4, ROWS, 256).astype(LOW)
            return carry

        lax.fori_loop(0, 8, piece, 0)

    def product(s, out):
        terms = dot(ones_t[s], grad_proj[...])
        out[:, :, :, 0:PROJ] = terms.reshape(8, 2, 16, PROJ).astype(LOW)
        rows = grads[:, :, columns_of(s)].reshape(8 * ROWS, 256)
        out[:, :, :, PROJ:] = dot(att_t[...], rows).reshape(8, 2, 16, PART).astype(LOW)

    twin = twin_sum(me, mail, stage_a, acc_a, order, product)
    norm_terms(me.b)
    step(grad_sum)
    norm_terms(me.a)
    step(grad_sum)
    step(twin, 3)
    step(grad_sum)
    step(downs)
    step(twin, 3)
    step(grad_sum)
    step(sums)
    step(twin, 3)

    def proj_sums():
        yield from scatter_hz(me, mail, acc_a, az_over, az_near, h_near)
        own = acc_a.at[:, me.z * 2 + me.h]
        yield from send_seq(me, mail, own, in_own, 0, PROJ)

    rest = proj_sums()
    step(rest)
    finish(grad_sum, sums, rest)
    own = acc_a.at[:, me.z * 2 + me.h]
    gain = column(gain_one)
    sum_one = jnp.zeros((16, 1), WIDE)
    run(sums, out_sum, downs)
    units = mlp_ref.shape[2] // 4
    spare = jnp.zeros((16, mlp_ref.shape[2] - UNITS), WIDE)
    gain_mlp = column(gain_two)
    sum_two = jnp.zeros((16, 1), WIDE)
    for slot in range(3):
        whole = None
        for src in range(4):
            if slot == 2:
                piece = down_own[src].astype(WIDE)
            else:
                firsts = [(2 * tile + slot) * 128 for tile in range(UNITS // 128)]
                piece = jnp.concatenate([pair_own[src, :, f : f + 128].astype(WIDE) for f in firsts], axis=1)
            piece = jnp.concatenate([piece, spare], axis=1)
            whole = piece if src == 0 else whole + pltpu.roll(piece, src * units, 1)
        if slot < 2:
            sum_two = sum_two + jnp.sum(whole * mlp_ref[:, slot, :].astype(WIDE), axis=1, keepdims=True)
            whole = whole * gain_mlp
        mlp_grad[:, slot, :] = whole
    run(rest)
    for slot in range(4):
        if slot < 3:
            pieces = [in_own[src, :, slot * PART : slot * PART + PART] for src in range(8)]
        else:
            pieces = [own[k, :, PROJ:] for k in range(8)]
        whole = jnp.concatenate([piece.astype(WIDE) for piece in pieces], axis=1)
        if slot < 3:
            sum_one = sum_one + jnp.sum(whole * attn_ref[:, slot, :].astype(WIDE), axis=1, keepdims=True)
            whole = whole * gain
        attn_grad[:, slot, :] = whole
    gain_grads[:, 0:128] = jnp.broadcast_to(sum_one, (16, 128))
    gain_grads[:, 128:256] = jnp.broadcast_to(sum_two, (16, 128))
    mail.finish()


def back(grad_resid, x, counts, resid, attn_weight, mlp_weight, gain_one, gain_two, down, grads, branch, acc, ones, wa, qkv, probs, att):
    vmem, anywhere = pl.BlockSpec(memory_space=pltpu.VMEM), pl.BlockSpec(memory_space=pl.ANY)
    shape = jax.ShapeDtypeStruct
    count = 9 + 30 + 3 + 6 + 23 + 8 + 13 + 7
    return pl.pallas_call(
        back_kernel,
        out_shape=(
            shape((ROWS, MODEL), LOW), shape((ROWS, MODEL), WIDE), shape(attn_weight.shape, WIDE),
            shape(mlp_weight.shape, WIDE), shape((16, 256), WIDE),
        ),
        in_specs=[vmem] * 2 + [pl.BlockSpec(memory_space=pltpu.SMEM)] + [vmem] * 5 + [anywhere] * 9,
        out_specs=(vmem,) * 5,
        scratch_shapes=[
            pltpu.VMEM((4, 4, 16, UNITS), LOW), pltpu.VMEM((2, 2, 16, UNITS), LOW), pltpu.VMEM((2, 4, 16, UNITS), LOW),
            pltpu.VMEM((4, 16, UNITS), LOW), pltpu.VMEM((4, 16, PAIR), LOW), pltpu.VMEM((8, 16, PROJ), LOW), pltpu.VMEM((8, 8, 16, PAIR), LOW), pltpu.VMEM((4, 2, 2, 16, PAIR), LOW), pltpu.VMEM((4, 2, 4, 16, PAIR), LOW),
            pltpu.VMEM((2, 2, 16, PAIR), LOW), pltpu.VMEM((2, 4, 16, PAIR), LOW), pltpu.VMEM((8, ROWS, MODEL), LOW),
            pltpu.VMEM((4, ROWS, MODEL), LOW), pltpu.VMEM((2, ROWS, MID), LOW), pltpu.VMEM((2, ROWS, MODEL), LOW),
            pltpu.VMEM((8, ROWS, MODEL), LOW),
        ]
        + scatter_bufs()
        + [
            pltpu.VMEM((8, 16, 16, 1024), LOW), pltpu.VMEM((8, 8, 16, 1024), LOW), pltpu.VMEM((2, 2, 4, 16, 1024), LOW),
            pltpu.VMEM((2, 2, 8, 16, 1024), LOW), pltpu.VMEM((8, 16, 1024), LOW),
            pltpu.VMEM((8, 256, 1024), LOW),
            pltpu.VMEM((1024, PROJ), LOW), pltpu.VMEM((2, 2, 256, 1024), LOW), pltpu.VMEM((PART, 1024), LOW),
            pltpu.VMEM((1024, PART), LOW), pltpu.VMEM((1024, PROJ), LOW),
            pltpu.VMEM((1024, PART), WIDE), pltpu.VMEM((1024, PART), WIDE), pltpu.VMEM((2, 8, 2, 16, 1024), LOW),
            pltpu.SemaphoreType.DMA((count,)), pltpu.SemaphoreType.DMA((count,)), pltpu.SemaphoreType.DMA((14,)),
        ],
        compiler_params=pltpu.CompilerParams(collective_id=3, has_side_effects=True, vmem_limit_bytes=62 * 2**20),
        name="back",
    )(grad_resid, x, counts, resid, attn_weight, mlp_weight, gain_one, gain_two, down, grads, branch, acc, ones, wa, qkv, probs, att)
def local(
    tokens, valid_counts, block_owner, norm1_gain, attn_weight, norm2_gain, mlp_weight, cotangent
):
    x, cot = tokens[0], cotangent[0]
    gain_one, gain_two = norm1_gain[None], norm2_gain[None]
    ones, wa, grads, wm, qkv, probs, att, twos, resid = front(
        x, valid_counts, block_owner, cot, attn_weight, mlp_weight, gain_one, gain_two
    )
    acc, branch, branch_grads, grad_resid, down = mlp(resid, cot, valid_counts, twos, grads, wm)
    layer_out, input_grad, attn_grad, mlp_grad, gain_grads = back(
        grad_resid, x, valid_counts, resid, attn_weight, mlp_weight, gain_one, gain_two, down,
        branch_grads, branch, acc, ones, wa, qkv, probs, att,
    )
    return (layer_out[None], input_grad[None], gain_grads[:, 0], attn_grad, gain_grads[:, 128], mlp_grad)


def solution(mesh):
    token_spec = P("dp", "seq", None)
    row_spec = P(("seq", "dp"), None, None)
    gain_spec = P(("seq", "dp"))
    in_specs = (
        token_spec, P("dp", "seq"), P("dp", None), gain_spec, row_spec, gain_spec, row_spec, token_spec
    )
    out_specs = (token_spec, token_spec, gain_spec, row_spec, gain_spec, row_spec)
    return jax.shard_map(local, mesh=mesh, in_specs=in_specs, out_specs=out_specs, check_vma=False)
```

```python
import functools, math
import jax
import jax.numpy as jnp
from jax import lax
from jax.experimental import pallas as pl
from jax.experimental.pallas import tpu as pltpu
from jax.sharding import PartitionSpec as P

LOW = jnp.bfloat16
WIDE = jnp.float32
MESH = pl.DeviceIdType.MESH
EPS = 1e-05
HEAD_DIM = 128
ROWS = 128
MODEL = 2048
PART = 256
PROJ = 3 * PART
UNITS = 1408
SLAB = 3 * UNITS
PAIR = 2 * UNITS
FIRST = 96
MID = MODEL // 2


class Place:
    def __init__(self):
        self.seq, self.dp = lax.axis_index("seq"), lax.axis_index("dp")
        self.a, self.y = self.seq // 4, self.seq % 4
        self.b = 1 - self.a
        self.up, self.down, self.far = (self.y + 1) % 4, (self.y + 3) % 4, (self.y + 2) % 4
        self.z, self.h, self.core = self.dp // 4, self.dp // 2 % 2, self.dp % 2
        self.z_up, self.z_down, self.z_far = (self.z + 1) % 4, (self.z + 3) % 4, (self.z + 2) % 4
        self.x_dev = {"seq": self.b * 4 + self.y}
        self.up_dev = {"seq": self.a * 4 + self.up}
        self.down_dev = {"seq": self.a * 4 + self.down}
        self.h_dev = {"dp": self.member(self.z, 1 - self.h)}
        self.z_up_dev = {"dp": self.member(self.z_up, self.h)}
        self.z_down_dev = {"dp": self.member(self.z_down, self.h)}
        self.twin_dev = {"dp": self.dp + 1 - 2 * self.core}
        self.x = self.h * 2 + self.a
        self.x_up, self.x_down, self.x_far = (self.x + 1) % 4, (self.x + 3) % 4, (self.x + 2) % 4
        self.x_up_dev, self.x_down_dev = self.at_x(self.x_up), self.at_x(self.x_down)

    def member(self, z, h, twin=False):
        core = 1 - self.core if twin else self.core
        return z * 4 + h * 2 + core

    def at_x(self, x):
        return {"seq": x % 2 * 4 + self.y, "dp": self.member(self.z, x // 2)}

    def column(self, twin=False):
        return self.z * 4 + (1 - self.core if twin else self.core)

    def peers(self):
        return [{"seq": (self.seq + k) % 8} for k in range(1, 8)]


def greet(devices):
    barrier = pltpu.get_barrier_semaphore()
    for device in devices:
        pl.semaphore_signal(barrier, inc=1, device_id=device, device_id_type=MESH)
    return lambda: pl.semaphore_wait(barrier, len(devices))


class Mail:
    def __init__(self, send, recv):
        self.send, self.recv = send, recv
        self.count, self.started = 0, {}

    def slots(self, n):
        first = self.count
        self.count += n
        return first

    def copy(self, slot, src, dst, device):
        return pltpu.make_async_remote_copy(
            src_ref=src, dst_ref=dst, send_sem=self.send.at[slot], recv_sem=self.recv.at[slot],
            device_id=device, device_id_type=MESH,
        )

    def go(self, slot, src, dst, device):
        copy = self.copy(slot, src, dst, device)
        copy.start()
        self.started[slot] = copy

    def arrived(self, slot, dst, device):
        self.copy(slot, dst, dst, device).wait_recv()

    def sent(self, slot):
        self.started.pop(slot).wait_send()

    def finish(self):
        for copy in self.started.values():
            copy.wait_send()


def gather_seq(me, mail, x_ref, out_ref):
    a, b, y, up, down, far = me.a, me.b, me.y, me.up, me.down, me.far
    XP, U, D = me.x_dev, me.up_dev, me.down_dev
    n = mail.slots(18)

    def cut(ref, rows, half):
        lo, hi = ((0, FIRST), (FIRST, ROWS))[rows]
        return ref.at[lo:hi] if half is None else ref.at[lo:hi, half * MID : half * MID + MID]

    def at(col, row, rows, half=None):
        return cut(out_ref.at[col * 4 + row], rows, half)

    def send(i, rows, dev):
        mail.go(n + i, cut(x_ref, rows, None), at(a, y, rows), dev)

    def fwd(i, ref, dev):
        mail.go(n + i, ref, ref, dev)

    def got(i, dst):
        mail.arrived(n + i, dst, XP)

    send(0, 0, XP)
    send(1, 0, U)
    send(2, 0, D)
    send(3, 1, U)
    send(4, 1, D)
    send(5, 1, XP)
    yield
    got(0, at(b, y, 0))
    fwd(6, at(b, y, 0), U)
    fwd(7, at(b, y, 0), D)
    yield
    got(1, at(a, down, 0))
    fwd(8, at(a, down, 0, 0), U)
    got(2, at(a, up, 0))
    fwd(9, at(a, up, 0, 1), D)
    yield
    got(3, at(a, down, 1))
    fwd(10, at(a, down, 1, 0), U)
    fwd(11, at(a, down, 1), XP)
    got(4, at(a, up, 1))
    fwd(12, at(a, up, 1, 1), D)
    fwd(13, at(a, up, 1), XP)
    yield
    got(5, at(b, y, 1))
    got(6, at(b, down, 0))
    fwd(14, at(b, down, 0, 0), U)
    got(7, at(b, up, 0))
    fwd(15, at(b, up, 0, 1), D)
    yield
    got(10, at(a, far, 1, 0))
    fwd(16, at(a, far, 1, 0), XP)
    got(12, at(a, far, 1, 1))
    fwd(17, at(a, far, 1, 1), XP)
    yield
    got(8, at(a, far, 0, 0))
    got(9, at(a, far, 0, 1))
    got(11, at(b, down, 1))
    got(13, at(b, up, 1))
    yield
    got(14, at(b, far, 0, 0))
    got(15, at(b, far, 0, 1))
    got(16, at(b, far, 1, 0))
    got(17, at(b, far, 1, 1))


def gather_y(me, mail, x_ref, out_ref):
    y, up, down, far = me.y, me.up, me.down, me.far
    U, D = me.up_dev, me.down_dev
    n = mail.slots(4)
    H = ROWS // 2
    mail.go(n, x_ref, out_ref.at[y], U)
    mail.go(n + 1, x_ref, out_ref.at[y], D)
    yield
    mail.arrived(n, out_ref.at[down], D)
    mail.go(n + 2, out_ref.at[down, 0:H], out_ref.at[down, 0:H], U)
    mail.arrived(n + 1, out_ref.at[up], U)
    mail.go(n + 3, out_ref.at[up, H:ROWS], out_ref.at[up, H:ROWS], D)
    yield
    mail.arrived(n + 2, out_ref.at[far, 0:H], D)
    mail.arrived(n + 3, out_ref.at[far, H:ROWS], U)


def scatter_y(me, mail, part, p2, p1, out):
    y, up, down, far = me.y, me.up, me.down, me.far
    U, D = me.up_dev, me.down_dev
    n = mail.slots(6)
    left, right = pl.ds(0, MID), pl.ds(MID, MID)
    mail.go(n, part.at[far, :, left], p2.at[0], U)
    mail.go(n + 3, part.at[down, :, left], p1.at[1, :, left], D)
    yield
    mail.go(n + 1, part.at[far, :, right], p2.at[1], D)
    mail.go(n + 2, part.at[up, :, right], p1.at[0, :, right], U)
    yield
    mail.arrived(n, p2.at[0], D)
    add(part.at[up, :, left], p2.at[0])
    mail.go(n + 4, part.at[up, :, left], p1.at[0, :, left], U)
    mail.arrived(n + 1, p2.at[1], U)
    add(part.at[down, :, right], p2.at[1])
    mail.go(n + 5, part.at[down, :, right], p1.at[1, :, right], D)
    yield
    mail.arrived(n + 2, p1.at[0, :, right], D)
    mail.arrived(n + 3, p1.at[1, :, left], U)
    mail.arrived(n + 4, p1.at[0, :, left], D)
    mail.arrived(n + 5, p1.at[1, :, right], U)
    out(0, ROWS, val(part.at[y]) + val(p1.at[0]) + val(p1.at[1]))


def val(ref):
    return ref[...].astype(WIDE)


def add(dst, src):
    dst[...] = (val(dst) + val(src)).astype(LOW)


def swap_seq(me, mail, own_ref, all_ref, lo, hi):
    n = mail.slots(7)
    for k in range(1, 8):
        to = (me.seq + k) % 8
        mail.go(n + k - 1, own_ref.at[to, :, lo:hi], all_ref.at[me.seq, me.dp, :, lo:hi], {"seq": to})
    yield
    for k in range(1, 8):
        came = (me.seq + 8 - k) % 8
        mail.arrived(n + k - 1, all_ref.at[came, me.dp, :, lo:hi], me.x_dev)


def gather_dp(me, mail, ref):
    z, h = me.z, me.h
    n = mail.slots(19)
    HD, ZU, ZD, TW = me.h_dev, me.z_up_dev, me.z_down_dev, me.twin_dev

    def at(zz, hh, half=None, twin=False):
        d = me.member(zz, hh, twin)
        return ref.at[:, d] if half is None else ref.at[4 * half : 4 * half + 4, d]

    def fwd(i, r, dev):
        mail.go(n + i, r, r, dev)

    def got(i, r):
        mail.arrived(n + i, r, TW)

    hs = (h, 1 - h)
    fwd(0, at(z, h), HD)
    fwd(1, at(z, h), ZU)
    fwd(2, at(z, h), ZD)
    fwd(9, at(z, h), TW)
    yield
    got(0, at(z, 1 - h))
    fwd(3, at(z, 1 - h), ZU)
    fwd(4, at(z, 1 - h), ZD)
    fwd(10, at(z, 1 - h), TW)
    yield
    for k in range(2):
        got(1 + 2 * k, at(me.z_down, hs[k]))
        fwd(5 + 2 * k, at(me.z_down, hs[k], 0), ZU)
        fwd(11 + 2 * k, at(me.z_down, hs[k]), TW)
        yield
        got(2 + 2 * k, at(me.z_up, hs[k]))
        fwd(6 + 2 * k, at(me.z_up, hs[k], 1), ZD)
        fwd(12 + 2 * k, at(me.z_up, hs[k]), TW)
        yield
    for k in range(2):
        got(5 + 2 * k, at(me.z_far, hs[k], 0))
        fwd(15 + 2 * k, at(me.z_far, hs[k], 0), TW)
        got(6 + 2 * k, at(me.z_far, hs[k], 1))
        fwd(16 + 2 * k, at(me.z_far, hs[k], 1), TW)
        yield
    got(9, at(z, h, twin=True))
    got(10, at(z, 1 - h, twin=True))
    for k in range(2):
        got(11 + 2 * k, at(me.z_down, hs[k], twin=True))
        got(12 + 2 * k, at(me.z_up, hs[k], twin=True))
        got(15 + 2 * k, at(me.z_far, hs[k], 0, twin=True))
        got(16 + 2 * k, at(me.z_far, hs[k], 1, twin=True))


def swap_y(me, mail, own_ref, all_ref):
    n = mail.slots(3)
    for k in (2, 1, 3):
        to = (me.y + k) % 4
        mail.go(n + k - 1, own_ref.at[to], all_ref.at[me.seq, me.dp], {"seq": me.a * 4 + to})
    yield
    for k in (1, 3, 2):
        came = me.a * 4 + (me.y + 4 - k) % 4
        mail.arrived(n + k - 1, all_ref.at[came, me.dp], me.up_dev)


def slab(me, ref, x, z, half=None, twin=False):
    d = me.member(z, x // 2, twin)
    first = x % 2 * 4
    return ref.at[pl.ds(first, 4), d] if half is None else ref.at[pl.ds(first + 2 * half, 2), d]


def gather_xz(me, mail, ref):
    n = mail.slots(36)
    XU, XD, ZU, ZD, TW = me.x_up_dev, me.x_down_dev, me.z_up_dev, me.z_down_dev, me.twin_dev
    z, zu, zd, zf = me.z, me.z_up, me.z_down, me.z_far
    xs = (me.x, me.x_down, me.x_up, me.x_far)

    def at(x, zz, half=None, twin=False):
        return slab(me, ref, x, zz, half, twin)

    def fwd(i, r, dev):
        mail.go(n + i, r, r, dev)

    def got(i, r):
        mail.arrived(n + i, r, TW)

    def z_first(k):
        fwd(4 + 4 * k, at(xs[k], z), ZU)
        fwd(5 + 4 * k, at(xs[k], z), ZD)
        fwd(20 + 4 * k, at(xs[k], z), TW)

    def z_second(k):
        got(4 + 4 * k, at(xs[k], zd))
        fwd(6 + 4 * k, at(xs[k], zd, 0), ZU)
        fwd(21 + 4 * k, at(xs[k], zd), TW)
        got(5 + 4 * k, at(xs[k], zu))
        fwd(7 + 4 * k, at(xs[k], zu, 1), ZD)
        fwd(22 + 4 * k, at(xs[k], zu), TW)

    def z_third(k):
        got(6 + 4 * k, at(xs[k], zf, 0))
        got(7 + 4 * k, at(xs[k], zf, 1))
        fwd(23 + 4 * k, at(xs[k], zf), TW)

    z_first(0)
    yield
    fwd(0, at(me.x, z), XU)
    fwd(1, at(me.x, z), XD)
    yield
    got(0, at(me.x_down, z))
    fwd(2, at(me.x_down, z, 0), XU)
    got(1, at(me.x_up, z))
    fwd(3, at(me.x_up, z, 1), XD)
    z_first(1)
    z_first(2)
    yield
    got(2, at(me.x_far, z, 0))
    got(3, at(me.x_far, z, 1))
    z_first(3)
    yield
    for k in range(4):
        z_second(k)
        yield
    for k in range(4):
        z_third(k)
        yield
    for k in range(4):
        for i, zz in enumerate((z, zd, zu, zf)):
            got(20 + 4 * k + i, at(xs[k], zz, twin=True))


def add_slabs(dst, *sources):
    def one(i, carry):
        total = val(dst.at[i])
        for source in sources:
            total = total + val(source.at[i])
        dst[i] = total.astype(LOW)
        return carry

    lax.fori_loop(0, dst.shape[0], one, 0)


def halved(ref, half):
    k = ref.shape[0] // 2
    return ref.at[half * k : half * k + k]


class RingSum:
    def __init__(self, mail, at, places, devices, over, near):
        self.mail, self.at, self.places, self.devices = mail, at, places, devices
        self.over, self.near = over, near
        self.n = mail.slots(6)

    def first(self):
        own, up, down, far = self.places
        U, D = self.devices
        go, n = self.mail.go, self.n
        go(n, halved(self.at(far), 0), self.over.at[0], U)
        go(n + 1, halved(self.at(far), 1), self.over.at[1], D)
        go(n + 2, halved(self.at(up), 1), halved(self.near.at[0], 1), U)
        go(n + 3, halved(self.at(down), 0), halved(self.near.at[1], 0), D)

    def second(self):
        own, up, down, far = self.places
        U, D = self.devices
        go, got, n = self.mail.go, self.mail.arrived, self.n
        got(n, self.over.at[0], D)
        add_slabs(halved(self.at(up), 0), self.over.at[0])
        go(n + 4, halved(self.at(up), 0), halved(self.near.at[0], 0), U)
        got(n + 1, self.over.at[1], U)
        add_slabs(halved(self.at(down), 1), self.over.at[1])
        go(n + 5, halved(self.at(down), 1), halved(self.near.at[1], 1), D)

    def third(self):
        own = self.places[0]
        U, D = self.devices
        got, n = self.mail.arrived, self.n
        got(n + 2, halved(self.near.at[0], 1), D)
        got(n + 3, halved(self.near.at[1], 0), U)
        got(n + 4, halved(self.near.at[0], 0), D)
        got(n + 5, halved(self.near.at[1], 1), U)
        add_slabs(self.at(own), self.near.at[0], self.near.at[1])


def twin_sum(me, mail, stage, acc, order, product, kept=None):
    slots = stage.shape[0]
    n = mail.slots(len(order))

    def settle(i):
        mail.arrived(n + i, acc.at[order[i]], me.twin_dev)
        add_slabs(acc.at[order[i]], stage.at[i % slots, :, me.core])
        if kept is not None:
            kept(i)

    for i, s in enumerate(order):
        if i >= slots:
            mail.sent(n + i - slots)
        product(s, stage.at[i % slots])
        mail.go(n + i, stage.at[i % slots, :, 1 - me.core], acc.at[s], me.twin_dev)
        if i > 0:
            settle(i - 1)
        yield
    settle(len(order) - 1)
    for i in range(max(0, len(order) - slots), len(order)):
        mail.sent(n + i)


def scatter_z(me, mail, acc, xs, z_over, z_near):
    zs = (me.z, me.z_up, me.z_down, me.z_far)

    def at(x):
        return lambda z: acc.at[pl.ds(x % 2 * 4, 4), z * 2 + x // 2]

    rings = [RingSum(mail, at(x), zs, (me.z_up_dev, me.z_down_dev), z_over.at[k], z_near.at[k]) for k, x in enumerate(xs)]
    rings[0].first()
    yield
    for ring in rings[1:]:
        ring.first()
    yield
    for ring in rings:
        ring.second()
        yield
    for ring in rings[:-1]:
        ring.third()
        yield
    rings[-1].third()


def scatter_x(me, mail, at, x_over, x_near):
    places = (me.x, me.x_up, me.x_down, me.x_far)
    ring = RingSum(mail, at, places, (me.x_up_dev, me.x_down_dev), x_over, x_near)
    ring.first()
    yield
    ring.second()
    yield
    ring.third()


def scatter_hz(me, mail, acc, z_over, z_near, h_near):
    hs = (1 - me.h, me.h)
    zs = (me.z, me.z_up, me.z_down, me.z_far)

    def at(h):
        return lambda z: acc.at[:, z * 2 + h]

    rings = [RingSum(mail, at(h), zs, (me.z_up_dev, me.z_down_dev), z_over.at[k], z_near.at[k]) for k, h in enumerate(hs)]
    n = mail.slots(1)
    rings[0].first()
    rings[1].first()
    yield
    for k in range(2):
        rings[k].second()
        yield
    rings[0].third()
    mail.go(n, at(1 - me.h)(me.z), h_near, me.h_dev)
    yield
    rings[1].third()
    yield
    mail.arrived(n, h_near, me.h_dev)
    add_slabs(at(me.h)(me.z), h_near)


def send_y(me, mail, slab, result):
    n = mail.slots(3)
    for k in (2, 1, 3):
        to = (me.y + k) % 4
        mail.go(n + k - 1, slab.at[to], result.at[me.y], {"seq": me.a * 4 + to})
    result[me.y] = slab[me.y]
    yield
    for k in (1, 3, 2):
        mail.arrived(n + k - 1, result.at[(me.y + 4 - k) % 4], me.up_dev)


def send_seq(me, mail, slab, result, lo, hi):
    n = mail.slots(7)
    for k in range(1, 8):
        to = (me.seq + k) % 8
        mail.go(n + k - 1, slab.at[to, :, lo:hi], result.at[me.seq], {"seq": to})
    result[me.seq] = slab[me.seq, :, lo:hi]
    yield
    for k in range(1, 8):
        mail.arrived(n + k - 1, result.at[(me.seq + 8 - k) % 8], me.x_dev)


def scatter_bufs():
    late = ROWS - FIRST
    shapes = ((4, late, MODEL), (2, late, MID), (2, late, MODEL), (4, FIRST, MID), (4, FIRST, MODEL), (1, FIRST, MODEL))
    return [pltpu.VMEM(shape, LOW) for shape in shapes]


def scatter_seq(me, mail, part, bufs, out):
    a, b, y, up, down, far = me.a, me.b, me.y, me.up, me.down, me.far
    XP, U, D = me.x_dev, me.up_dev, me.down_dev
    qx, q2, q1, p2, p1, px = bufs
    n = mail.slots(23)
    halves = (pl.ds(0, MID), pl.ds(MID, MID))

    def go(i, src, dst, dev):
        mail.go(n + i, src, dst, dev)

    def got(i, dst):
        mail.arrived(n + i, dst, XP)

    def at(col, row, rows, half=None):
        lo, hi = ((0, FIRST), (FIRST, ROWS))[rows]
        ref = part.at[col * 4 + row]
        return ref.at[lo:hi] if half is None else ref.at[lo:hi, halves[half]]

    def lane(ref, k, half):
        return ref.at[k, :, halves[half]]

    for k, row in enumerate((far, down, up, y)):
        go(k, at(b, row, 1), qx.at[row], XP)
    cols = (b, a)

    def p_first(k):
        c, s = cols[k], 10 + 6 * k
        go(s, at(c, far, 0, 0), p2.at[2 * k], U)
        go(s + 1, at(c, far, 0, 1), p2.at[2 * k + 1], D)
        go(s + 2, at(c, up, 0, 1), lane(p1, 2 * k, 1), U)
        go(s + 3, at(c, down, 0, 0), lane(p1, 2 * k + 1, 0), D)

    def p_second(k):
        c, s = cols[k], 10 + 6 * k
        got(s, p2.at[2 * k])
        add(at(c, up, 0, 0), p2.at[2 * k])
        go(s + 4, at(c, up, 0, 0), lane(p1, 2 * k, 0), U)
        got(s + 1, p2.at[2 * k + 1])
        add(at(c, down, 0, 1), p2.at[2 * k + 1])
        go(s + 5, at(c, down, 0, 1), lane(p1, 2 * k + 1, 1), D)

    def p_third(k):
        s = 10 + 6 * k
        got(s + 2, lane(p1, 2 * k, 1))
        got(s + 3, lane(p1, 2 * k + 1, 0))
        got(s + 4, lane(p1, 2 * k, 0))
        got(s + 5, lane(p1, 2 * k + 1, 1))
        return val(at(cols[k], y, 0)) + val(p1.at[2 * k]) + val(p1.at[2 * k + 1])

    p_first(0)
    yield
    p_first(1)
    yield
    got(0, qx.at[far])
    add(at(a, far, 1), qx.at[far])
    go(4, at(a, far, 1, 0), q2.at[0], U)
    go(5, at(a, far, 1, 1), q2.at[1], D)
    yield
    p_second(0)
    yield
    got(1, qx.at[down])
    add(at(a, down, 1), qx.at[down])
    go(6, at(a, down, 1, 0), lane(q1, 1, 0), D)
    got(2, qx.at[up])
    add(at(a, up, 1), qx.at[up])
    go(7, at(a, up, 1, 1), lane(q1, 0, 1), U)
    yield
    p_second(1)
    yield
    rows = p_third(0)
    own = at(b, y, 0)
    own[...] = rows.astype(LOW)
    go(22, own, px.at[0], XP)
    yield
    got(4, q2.at[0])
    add(at(a, up, 1, 0), q2.at[0])
    go(8, at(a, up, 1, 0), lane(q1, 0, 0), U)
    got(5, q2.at[1])
    add(at(a, down, 1, 1), q2.at[1])
    go(9, at(a, down, 1, 1), lane(q1, 1, 1), D)
    yield
    rows = p_third(1)
    got(22, px.at[0])
    out(0, FIRST, rows + val(px.at[0]))
    yield
    got(3, qx.at[y])
    got(6, lane(q1, 1, 0))
    got(7, lane(q1, 0, 1))
    got(8, lane(q1, 0, 0))
    got(9, lane(q1, 1, 1))
    out(FIRST, ROWS, val(at(a, y, 1)) + val(qx.at[y]) + val(q1.at[0]) + val(q1.at[1]))


def run(*tasks):
    tasks = list(tasks)
    while tasks:
        for task in list(tasks):
            if next(task, tasks) is tasks:
                tasks.remove(task)


def step(task, count=1):
    for _ in range(count):
        next(task, None)


def beside(task, other):
    for _ in task:
        step(other)
        yield


def finish(task, *others):
    k = 0
    while next(task, others) is not others:
        k += 1
        if k % 2 == 0 and others:
            step(others[k // 2 % len(others)])
def dot(a, b, dims=((1,), (0,))):
    return lax.dot_general(a, b, (dims, ((), ())), preferred_element_type=WIDE)


def row_scale(values):
    return lax.rsqrt(jnp.mean(values * values, axis=-1, keepdims=True) + EPS)


def column(row_ref):
    shape = (16, 16)
    here = lax.broadcasted_iota(jnp.int32, shape, 0) == lax.broadcasted_iota(jnp.int32, shape, 1)
    return jnp.sum(jnp.where(here, row_ref[...].astype(WIDE), 0.0), axis=1, keepdims=True)


def live_rows(count_ref):
    return jnp.where(lax.broadcasted_iota(jnp.int32, (ROWS, 1), 0) < count_ref[0, 0], 1.0, 0.0).astype(WIDE)


def front_kernel(
    x_ref, count_ref, owner_ref, cot_ref, attn_ref, mlp_ref, gain_one, gain_two,
    one_out, wa_out, grad_all, wm, qkv_out, probs_out, att_out, two_all, resid,
    one_all, wa, grad_own, qkv, probs, att, ones_t, att_t, two, wa_own, wm_own, pos_k, part, qx, q2, q1, p2, p1, px, send, recv, local_sem,
):
    me = Place()
    mail = Mail(send, recv)
    saves = []

    def save(src, dst):
        copy = pltpu.make_async_copy(src, dst, local_sem.at[len(saves)])
        copy.start()
        saves.append(copy)
        return copy

    ready = greet(me.peers() + [me.h_dev, me.z_up_dev, me.z_down_dev, me.twin_dev, me.x_up_dev, me.x_down_dev])
    live = live_rows(count_ref)
    x = x_ref[...].astype(WIDE)
    one_all[me.seq] = (x * row_scale(x) * live).astype(LOW)
    ready()
    gather_one = gather_seq(me, mail, one_all.at[me.seq], one_all)
    step(gather_one)
    gain = column(gain_one)
    for slot in range(4):
        weight = attn_ref[:, slot, :].astype(WIDE)
        if slot < 3:
            weight = weight * gain
        for to in range(8):
            wa_own[to, :, slot * PART : slot * PART + PART] = weight[:, to * PART : to * PART + PART].astype(LOW)
    swap_a = swap_seq(me, mail, wa_own, wa, 0, PROJ)
    step(swap_a)
    gain = column(gain_two)
    units = mlp_ref.shape[2] // 4
    for slot in range(3):
        weight = mlp_ref[:, slot, :].astype(WIDE)
        if slot < 2:
            weight = weight * gain
        for to in range(4):
            piece = weight if to == 0 else pltpu.roll(weight, (4 - to) * units, 1)
            piece = piece[:, 0:UNITS]
            piece = jnp.where(lax.broadcasted_iota(jnp.int32, piece.shape, 1) < units, piece, 0.0).astype(LOW)
            for tile in range(UNITS // 128):
                first = PAIR + tile * 128 if slot == 2 else (2 * tile + slot) * 128
                wm_own[to, :, first : first + 128] = piece[:, tile * 128 : tile * 128 + 128]
    swap_m = swap_y(me, mail, wm_own, wm)
    step(swap_m)
    keep_m = save(wm_own.at[me.y], wm.at[me.seq, me.dp])
    for block in range(8):
        columns = lax.broadcasted_iota(jnp.int32, (1, ROWS), 1)
        pos_k[:, block * ROWS : block * ROWS + ROWS] = columns + owner_ref[0, block] * ROWS
    wa[pl.ds(me.seq, 1), pl.ds(me.dp, 1), :, 0:PROJ] = wa_own[pl.ds(me.seq, 1), :, 0:PROJ][None]
    for k in range(8):
        wa[k, pl.ds(me.dp, 1), :, PROJ:] = wa_own[k, :, PROJ:][None]
    step(swap_a)
    gather_wa = gather_dp(me, mail, wa)
    step(gather_wa)
    grad_own[...] = (cot_ref[...].astype(WIDE) * live).astype(LOW)
    save(grad_own, grad_all.at[me.y])
    step(gather_one)
    step(gather_wa)
    step(gather_one)
    step(gather_wa, 2)
    step(gather_one)
    step(gather_wa, 2)
    step(swap_m)
    keep_m.wait()
    gather_wm = gather_xz(me, mail, wm)
    step(gather_wm, 2)
    step(gather_one, 2)
    gather_g = gather_y(me, mail, grad_own, grad_all)
    step(gather_g)
    step(gather_one)
    run(gather_wa)

    def project(i, carry):
        rows = one_all[pl.ds(i * 2, 2)].reshape(2 * ROWS, MODEL)
        weight = wa[:, :, :, 0:PROJ].reshape(MODEL, PROJ)
        qkv[pl.ds(pl.multiple_of(i * 256, 256), 256), :] = dot(rows, weight).astype(LOW)
        return carry

    lax.fori_loop(me.a * 2, me.a * 2 + 2, project, 0)
    run(gather_one)
    step(gather_wm)
    save(wa, wa_out)

    def attend(i, carry):
        first = pl.multiple_of(i * ROWS, ROWS)
        rows = pl.ds(first, ROWS)
        allowed = pos_k[...] <= lax.broadcasted_iota(jnp.int32, (ROWS, 1), 0) + owner_ref[0, i] * ROWS
        for head in range(2):
            lo, hi = head * HEAD_DIM, (head + 1) * HEAD_DIM
            q = qkv[rows, lo:hi]
            k = qkv[:, PART + lo : PART + hi]
            v = qkv[:, 2 * PART + lo : 2 * PART + hi]
            odds = jnp.exp2(math.log2(8 * ROWS) - dot(q, k, ((1,), (1,))) * (math.log2(math.e) / math.sqrt(HEAD_DIM)))
            p = jnp.where(allowed, 1.0 / (1.0 + odds), 0.0).astype(LOW)
            probs[head, rows, :] = p
            att[rows, lo:hi] = dot(p, v).astype(LOW)
        return carry

    def out_project(col):
        rows = att[pl.ds(pl.multiple_of(col * 512, 512), 512), :]

        def piece(k, carry):
            weight = wa[k, :, :, PROJ:].reshape(PART, PART)
            columns = pl.ds(pl.multiple_of(k * PART, PART), PART)
            part[pl.ds(col * 4, 4), :, columns] = dot(rows, weight).reshape(4, ROWS, PART).astype(LOW)
            return carry

        lax.fori_loop(0, 8, piece, 0)

    lax.fori_loop(me.b * 2, me.b * 2 + 2, project, 0)
    step(gather_g)
    save(qkv, qkv_out)

    def write(lo, hi, rows):
        total = x_ref[lo:hi].astype(WIDE) + rows
        resid[lo:hi] = total
        two[lo:hi] = (total * row_scale(total) * live[lo:hi]).astype(LOW)

    scatter = scatter_seq(me, mail, part, (qx, q2, q1, p2, p1, px), write)
    lax.fori_loop(me.b * 4, me.b * 4 + 4, attend, 0)
    out_project(me.b)
    step(scatter)
    step(gather_wm)
    lax.fori_loop(me.a * 4, me.a * 4 + 4, attend, 0)
    out_project(me.a)
    step(scatter)
    save(probs, probs_out)
    finish(scatter, gather_wm)
    gather_two = gather_y(me, mail, two, two_all)
    step(gather_two)
    save(two, two_all.at[me.y])
    step(gather_wm)

    def turn(s, carry):
        columns = pl.ds(pl.multiple_of(s * 256, 256), 256)
        ones_t[s] = one_all[:, :, columns].reshape(8 * ROWS, 256).T
        return carry

    att_t[...] = att[...].T
    save(att_t, att_out)
    for i in range(4):
        lax.fori_loop(2 * i, 2 * i + 2, turn, 0)
        step(gather_wm)
        if i == 1:
            step(gather_two)
    save(ones_t, one_out)
    run(gather_wm, gather_g, gather_two)
    for copy in saves:
        if copy is not keep_m:
            copy.wait()
    mail.finish()


def front(x, counts, owners, cot, attn_weight, mlp_weight, gain_one, gain_two):
    vmem, anywhere = pl.BlockSpec(memory_space=pltpu.VMEM), pl.BlockSpec(memory_space=pl.ANY)
    shape = jax.ShapeDtypeStruct
    count = 7 + 18 + 19 + 3 + 36 + 4 + 23 + 4
    return pl.pallas_call(
        front_kernel,
        out_shape=(
            shape((8, 256, 1024), LOW), shape((8, 16, 16, 1024), LOW), shape((4, ROWS, MODEL), LOW),
            shape((8, 16, 16, SLAB), LOW), shape((1024, PROJ), LOW), shape((2, 1024, 1024), LOW),
            shape((PART, 1024), LOW), shape((4, ROWS, MODEL), LOW), shape((ROWS, MODEL), WIDE),
        ),
        in_specs=[vmem] + [pl.BlockSpec(memory_space=pltpu.SMEM)] * 2 + [vmem] * 5,
        out_specs=(anywhere,) * 8 + (vmem,),
        scratch_shapes=[
            pltpu.VMEM((8, ROWS, MODEL), LOW), pltpu.VMEM((8, 16, 16, 1024), LOW), pltpu.VMEM((ROWS, MODEL), LOW),
            pltpu.VMEM((1024, PROJ), LOW), pltpu.VMEM((2, 1024, 1024), LOW), pltpu.VMEM((1024, PART), LOW),
            pltpu.VMEM((8, 256, 1024), LOW), pltpu.VMEM((PART, 1024), LOW), pltpu.VMEM((ROWS, MODEL), LOW),
            pltpu.VMEM((8, 16, 1024), LOW), pltpu.VMEM((4, 16, SLAB), LOW), pltpu.VMEM((1, 1024), jnp.int32),
            pltpu.VMEM((8, ROWS, MODEL), LOW),
        ]
        + scatter_bufs()
        + [pltpu.SemaphoreType.DMA((count,)), pltpu.SemaphoreType.DMA((count,)), pltpu.SemaphoreType.DMA((9,))],
        compiler_params=pltpu.CompilerParams(collective_id=1, has_side_effects=True, vmem_limit_bytes=56 * 2**20),
        name="front",
    )(x, counts, owners, cot, attn_weight, mlp_weight, gain_one, gain_two)
def mlp_kernel(
    resid, cot_ref, count_ref, two_all, grad_all, wm_all,
    acc_out, branch_out, branch_grads, grad_resid, down_out,
    wm, grads, twos, hidden, pair, part, branch, p2, p1, grad_branch,
    stage_d, acc_d, z_over, z_near, pz_over, pz_near, stage, acc, send, recv, local_sem, wm_sem,
):
    me = Place()
    mail = Mail(send, recv)
    saves, first_saves = [], []

    def save(src, dst):
        copy = pltpu.make_async_copy(src, dst, local_sem.at[len(saves)])
        copy.start()
        saves.append(copy)
        return copy

    live = live_rows(count_ref)
    loads = [save(two_all, twos), save(grad_all, grads)]

    def weights(j, wide):
        for first, each, sem in ((0, 256, 0), (PAIR, 128, 6)):
            columns = pl.ds(pl.multiple_of(first + j * each, 128), wide * each)
            yield pltpu.make_async_copy(
                wm_all.at[:, :, :, columns], wm.at[:, :, :, columns], wm_sem.at[sem + j // 2]
            )

    for j in range(0, UNITS // 128, 2):
        for copy in weights(j, min(2, UNITS // 128 - j)):
            copy.start()
    ready = greet([me.x_dev, me.up_dev, me.down_dev, me.z_up_dev, me.z_down_dev, me.twin_dev])
    for load in loads:
        load.wait()

    def tall(ref, columns=slice(None)):
        values = ref[:, :, columns]
        return values.reshape(4 * ROWS, values.shape[2])

    def put(ref, columns, values):
        ref[:, :, columns] = values.reshape(4, ROWS, values.shape[1]).astype(LOW)

    def ahead(j, wide):
        for copy in weights(j, wide):
            copy.wait()
        start = pl.multiple_of(j * 128, 128)
        width = wide * 128
        weight = wm[:, :, :, pl.ds(2 * start, 2 * width)].reshape(MODEL, 2 * width)
        gate_up = dot(tall(twos), weight)
        down = wm[:, :, :, pl.ds(PAIR + start, width)].reshape(MODEL, width)
        grad_hidden = dot(tall(grads), down)
        low, pairs = [], []
        for i in range(wide):
            gate = gate_up[:, i * 256 : i * 256 + 128]
            up = gate_up[:, i * 256 + 128 : i * 256 + 256]
            grad = grad_hidden[:, i * 128 : i * 128 + 128]
            squashed = 1.0 / (1.0 + jnp.exp(-gate))
            active = gate * squashed
            low.append(active * up)
            pairs.append(grad * up * (squashed * (1.0 + gate * (1.0 - squashed))))
            pairs.append(grad * active)
        put(hidden, pl.ds(start, width), jnp.concatenate(low, axis=1))
        put(pair, pl.ds(2 * start, 2 * width), jnp.concatenate(pairs, axis=1))

    def ahead_tile(j, carry):
        ahead(2 * j, 2)
        return carry

    def back(s, carry):
        columns = pl.ds(pl.multiple_of(s * 256, 256), 256)
        weight = wm[s, :, :, 0:PAIR].reshape(256, PAIR)
        put(part, columns, dot(tall(pair), weight, ((1,), (1,))))
        return carry

    def down_back(s, carry):
        columns = pl.ds(pl.multiple_of(s * 256, 256), 256)
        weight = wm[s, :, :, PAIR:].reshape(256, UNITS)
        put(branch, columns, dot(tall(hidden), weight, ((1,), (1,))))
        return carry

    def write(lo, hi, rows):
        x = resid[lo:hi]
        scale = row_scale(x)
        hat = x * scale
        inner = jnp.mean(rows * hat, axis=-1, keepdims=True)
        total = cot_ref[lo:hi].astype(WIDE) * live[lo:hi] + scale * (rows - hat * inner)
        grad_resid[lo:hi] = total
        grad_branch[lo:hi] = total.astype(LOW)

    order = [me.a * 4 + i for i in range(4)] + [me.b * 4 + i for i in range(4)]

    def columns_t(ref, s):
        return ref[:, :, pl.ds(pl.multiple_of(s * 256, 256), 256)].reshape(4 * ROWS, 256).T

    def down_product(s, out):
        terms = dot(columns_t(grads, s), hidden[...].reshape(4 * ROWS, UNITS))
        out[...] = terms.reshape(8, 2, 16, UNITS).astype(LOW)

    def pair_product(s, out):
        terms = dot(columns_t(twos, s), pair[...].reshape(4 * ROWS, PAIR))
        out[...] = terms.reshape(8, 2, 16, PAIR).astype(LOW)

    def kept(i):
        first_saves.append(save(acc.at[order[i]], acc_out.at[order[i]]))

    scatter = scatter_y(me, mail, part, p2, p1, write)
    twin_d = twin_sum(me, mail, stage_d, acc_d, order, down_product)
    twin = twin_sum(me, mail, stage, acc, order, pair_product, kept)
    sums = scatter_z(me, mail, acc_d, (me.x_far, me.x_up, me.x_down, me.x), z_over, z_near)
    early = scatter_z(me, mail, acc, (me.x_far, me.x_up), pz_over, pz_near)
    gather = gather_seq(me, mail, grad_branch, branch_grads)
    lax.fori_loop(0, 5, ahead_tile, 0)
    ahead(10, 1)
    lax.fori_loop(0, 4, back, 0)
    ready()
    step(scatter)
    lax.fori_loop(4, 8, back, 0)
    step(scatter)
    run(twin_d)
    step(sums, 2)
    step(scatter)
    step(twin, 3)
    step(sums, 2)
    step(twin, 3)
    step(scatter)
    step(gather)
    keep = save(grad_branch, branch_grads.at[me.seq])
    step(sums)
    run(twin)
    step(early, 2)
    step(sums)
    step(gather)
    for copy in first_saves:
        copy.wait()
    for i in range(5):
        if i < 4:
            lax.fori_loop(2 * i, 2 * i + 2, down_back, 0)
        step(sums if i < 3 else early)
        step(gather)
    save(branch, branch_out)
    finish(gather, sums, early)
    run(sums, early)
    for x in range(4):
        save(acc_d.at[x % 2 * 4 : x % 2 * 4 + 4, me.z * 2 + x // 2], down_out.at[x])
    for x in (me.x_far, me.x_up):
        place = pl.ds(x % 2 * 4, 4), me.z * 2 + x // 2
        save(acc.at[place], acc_out.at[place])
    for copy in saves[2:]:
        if not any(copy is first for first in first_saves):
            copy.wait()
    mail.finish()


def mlp(resid, cot, counts, twos, grads, wm):
    vmem, anywhere = pl.BlockSpec(memory_space=pltpu.VMEM), pl.BlockSpec(memory_space=pl.ANY)
    shape = jax.ShapeDtypeStruct
    blocks = (4, ROWS, MODEL)
    count = 6 + 8 + 8 + 24 + 12 + 18
    return pl.pallas_call(
        mlp_kernel,
        out_shape=(
            shape((8, 8, 16, PAIR), LOW), shape(blocks, LOW), shape((8, ROWS, MODEL), LOW), shape((ROWS, MODEL), WIDE),
            shape((4, 4, 16, UNITS), LOW),
        ),
        in_specs=[vmem] * 2 + [pl.BlockSpec(memory_space=pltpu.SMEM)] + [anywhere] * 3,
        out_specs=(anywhere,) * 3 + (vmem, anywhere),
        scratch_shapes=[
            pltpu.VMEM((8, 16, 16, SLAB), LOW), pltpu.VMEM(blocks, LOW), pltpu.VMEM(blocks, LOW),
            pltpu.VMEM((4, ROWS, UNITS), LOW), pltpu.VMEM((4, ROWS, PAIR), LOW), pltpu.VMEM(blocks, LOW),
            pltpu.VMEM(blocks, LOW), pltpu.VMEM((2, ROWS, MID), LOW), pltpu.VMEM((2, ROWS, MODEL), LOW),
            pltpu.VMEM((ROWS, MODEL), LOW),
            pltpu.VMEM((2, 8, 2, 16, UNITS), LOW), pltpu.VMEM((8, 8, 16, UNITS), LOW),
            pltpu.VMEM((4, 2, 2, 16, UNITS), LOW), pltpu.VMEM((4, 2, 4, 16, UNITS), LOW),
            pltpu.VMEM((2, 2, 2, 16, PAIR), LOW), pltpu.VMEM((2, 2, 4, 16, PAIR), LOW),
            pltpu.VMEM((2, 8, 2, 16, PAIR), LOW), pltpu.VMEM((8, 8, 16, PAIR), LOW),
            pltpu.SemaphoreType.DMA((count,)), pltpu.SemaphoreType.DMA((count,)), pltpu.SemaphoreType.DMA((18,)), pltpu.SemaphoreType.DMA((12,)),
        ],
        compiler_params=pltpu.CompilerParams(collective_id=2, has_side_effects=True, vmem_limit_bytes=62 * 2**20),
        name="mlp",
    )(resid, cot, counts, twos, grads, wm)
def back_kernel(
    grad_resid, x_ref, count_ref, resid, attn_ref, mlp_ref, gain_one, gain_two, down_all, branch_grads, branch_all, acc_all, one_all, wa_all, qkv_all, probs_all, att_all,
    layer_out, input_grad, attn_grad, mlp_grad, gain_grads,
    down, dx_over, dx_near, down_own, pair_own, in_own, acc, z_over, z_near, x_over, x_near, grads, branch, b2, b1, part, qx, q2, q1, p2, p1, px,
    wa, acc_a, az_over, az_near, h_near, ones_t, qkv, probs, att_t, grad_att, grad_proj, grad_k, grad_v, stage_a,
    send, recv, local_sem,
):
    me = Place()
    mail = Mail(send, recv)
    loads = []
    live = live_rows(count_ref)

    def load(src, dst):
        copy = pltpu.make_async_copy(src, dst, local_sem.at[len(loads)])
        copy.start()
        loads.append(copy)
        return copy

    load_acc = [load(acc_all.at[pl.ds(col * 4, 4)], acc.at[pl.ds(col * 4, 4)]) for col in (me.b, me.a)]
    load_down = load(down_all, down)
    load_branch = load(branch_all, branch)
    ready = greet(me.peers() + [me.h_dev, me.z_up_dev, me.z_down_dev, me.x_up_dev, me.x_down_dev, me.twin_dev])
    load_grads = load(branch_grads, grads)
    load_wa = load(wa_all, wa)
    waits = [load(*both) for both in ((qkv_all, qkv), (att_all, att_t), (one_all, ones_t))]
    fetch = [load(probs_all.at[:, 256 * i : 256 * i + 256], probs.at[i]) for i in range(2)]
    order = [me.a * 4 + i for i in range(4)] + [me.b * 4 + i for i in range(4)]

    def columns_of(s, width=256):
        return pl.ds(pl.multiple_of(s * width, width), width)

    def down_sums():
        yield from scatter_x(me, mail, lambda x: down.at[x], dx_over, dx_near)
        yield from send_y(me, mail, down.at[me.x], down_own)

    def pair_sums():
        yield from scatter_z(me, mail, acc, (me.x_down, me.x), z_over, z_near)
        yield from scatter_x(me, mail, lambda x: acc.at[pl.ds(x % 2 * 4, 4), me.z * 2 + x // 2], x_over, x_near)
        yield from send_y(me, mail, acc.at[pl.ds(me.a * 4, 4), me.z * 2 + me.h], pair_own)

    downs = down_sums()
    sums = pair_sums()

    load_acc[0].wait()
    ready()
    step(sums)
    load_acc[1].wait()
    step(sums)
    load_down.wait()
    step(downs)
    def write_out(lo, hi, rows):
        layer_out[lo:hi] = (live[lo:hi] * (resid[lo:hi] + rows)).astype(LOW)

    out_sum = scatter_y(me, mail, branch, b2, b1, write_out)
    load_branch.wait()
    step(out_sum, 2)
    load_grads.wait()
    def write_grad(lo, hi, rows):
        x = x_ref[lo:hi].astype(WIDE)
        scale = row_scale(x)
        hat = x * scale
        inner = jnp.mean(rows * hat, axis=-1, keepdims=True)
        input_grad[lo:hi] = grad_resid[lo:hi] + live[lo:hi] * scale * (rows - hat * inner)

    grad_sum = scatter_seq(me, mail, part, (qx, q2, q1, p2, p1, px), write_grad)

    load_wa.wait()
    for wait in waits:
        wait.wait()
    head_scale = 1.0 / math.sqrt(HEAD_DIM)

    def attended_grad(i, carry):
        total = jnp.zeros((256, PART), WIDE)
        for k in range(8):
            rows = grads[pl.ds(i * 2, 2), :, k * PART : k * PART + PART].reshape(256, PART)
            total = total + dot(rows, wa[k, :, :, PROJ:].reshape(PART, PART), ((1,), (1,)))
        grad_att[columns_of(i), :] = total.astype(LOW)
        return carry

    lax.fori_loop(0, 4, attended_grad, 0)
    grad_k[...] = jnp.zeros_like(grad_k)
    grad_v[...] = jnp.zeros_like(grad_v)

    def attend_back(i):
        rows = pl.ds(256 * i, 256)
        for head in range(2):
            lo, hi = head * HEAD_DIM, (head + 1) * HEAD_DIM
            low = probs[i % 2, head]
            p = low.astype(WIDE)
            g = grad_att[rows, lo:hi]
            back = dot(g, qkv[:, 2 * PART + lo : 2 * PART + hi], ((1,), (1,)))
            grad_s = (back * (p * (1.0 - p))).astype(LOW)
            grad_q = dot(grad_s, qkv[:, PART + lo : PART + hi]) * head_scale
            grad_proj[rows, lo:hi] = grad_q.astype(LOW)
            grad_v[:, lo:hi] += dot(low, g, ((0,), (0,)))
            grad_k[:, lo:hi] += dot(grad_s, qkv[rows, lo:hi], ((0,), (0,)))

    for i in range(4):
        fetch[i].wait()
        attend_back(i)
        if i < 2:
            fetch.append(load(probs_all.at[:, 256 * i + 512 : 256 * i + 768], probs.at[i]))
        if i == 1:
            step(sums)
        if i == 2:
            step(downs)
        if i == 3:
            step(out_sum)
    grad_proj[:, PART : 2 * PART] = (grad_k[...] * head_scale).astype(LOW)
    grad_proj[:, 2 * PART :] = grad_v[...].astype(LOW)

    def norm_terms(col):
        rows = grad_proj[columns_of(col, 512), :]

        def piece(s, carry):
            weight = wa[s, :, :, 0:PROJ].reshape(256, PROJ)
            terms = dot(rows, weight, ((1,), (1,)))
            part[pl.ds(col * 4, 4), :, columns_of(s)] = terms.reshape(4, ROWS, 256).astype(LOW)
            return carry

        lax.fori_loop(0, 8, piece, 0)

    def product(s, out):
        terms = dot(ones_t[s], grad_proj[...])
        out[:, :, :, 0:PROJ] = terms.reshape(8, 2, 16, PROJ).astype(LOW)
        rows = grads[:, :, columns_of(s)].reshape(8 * ROWS, 256)
        out[:, :, :, PROJ:] = dot(att_t[...], rows).reshape(8, 2, 16, PART).astype(LOW)

    twin = twin_sum(me, mail, stage_a, acc_a, order, product)
    norm_terms(me.b)
    step(grad_sum)
    norm_terms(me.a)
    step(grad_sum)
    step(twin, 3)
    step(grad_sum)
    step(downs)
    step(sums)
    step(twin, 3)
    step(grad_sum)
    step(sums)
    step(twin, 3)

    def proj_sums():
        yield from scatter_hz(me, mail, acc_a, az_over, az_near, h_near)
        own = acc_a.at[:, me.z * 2 + me.h]
        yield from send_seq(me, mail, own, in_own, 0, PROJ)

    rest = proj_sums()
    step(rest)
    run(grad_sum, sums, rest)
    own = acc_a.at[:, me.z * 2 + me.h]
    gain = column(gain_one)
    sum_one = jnp.zeros((16, 1), WIDE)
    run(beside(sums, rest), out_sum, downs)
    units = mlp_ref.shape[2] // 4
    spare = jnp.zeros((16, mlp_ref.shape[2] - UNITS), WIDE)
    gain_mlp = column(gain_two)
    sum_two = jnp.zeros((16, 1), WIDE)
    for slot in range(3):
        whole = None
        for src in range(4):
            if slot == 2:
                piece = down_own[src].astype(WIDE)
            else:
                firsts = [(2 * tile + slot) * 128 for tile in range(UNITS // 128)]
                piece = jnp.concatenate([pair_own[src, :, f : f + 128].astype(WIDE) for f in firsts], axis=1)
            piece = jnp.concatenate([piece, spare], axis=1)
            whole = piece if src == 0 else whole + pltpu.roll(piece, src * units, 1)
        if slot < 2:
            sum_two = sum_two + jnp.sum(whole * mlp_ref[:, slot, :].astype(WIDE), axis=1, keepdims=True)
            whole = whole * gain_mlp
        mlp_grad[:, slot, :] = whole
    run(rest)
    for slot in range(4):
        if slot < 3:
            pieces = [in_own[src, :, slot * PART : slot * PART + PART] for src in range(8)]
        else:
            pieces = [own[k, :, PROJ:] for k in range(8)]
        whole = jnp.concatenate([piece.astype(WIDE) for piece in pieces], axis=1)
        if slot < 3:
            sum_one = sum_one + jnp.sum(whole * attn_ref[:, slot, :].astype(WIDE), axis=1, keepdims=True)
            whole = whole * gain
        attn_grad[:, slot, :] = whole
    gain_grads[:, 0:128] = jnp.broadcast_to(sum_one, (16, 128))
    gain_grads[:, 128:256] = jnp.broadcast_to(sum_two, (16, 128))
    mail.finish()


def back(grad_resid, x, counts, resid, attn_weight, mlp_weight, gain_one, gain_two, down, grads, branch, acc, ones, wa, qkv, probs, att):
    vmem, anywhere = pl.BlockSpec(memory_space=pltpu.VMEM), pl.BlockSpec(memory_space=pl.ANY)
    shape = jax.ShapeDtypeStruct
    count = 9 + 18 + 3 + 6 + 23 + 8 + 13 + 7
    return pl.pallas_call(
        back_kernel,
        out_shape=(
            shape((ROWS, MODEL), LOW), shape((ROWS, MODEL), WIDE), shape(attn_weight.shape, WIDE),
            shape(mlp_weight.shape, WIDE), shape((16, 256), WIDE),
        ),
        in_specs=[vmem] * 2 + [pl.BlockSpec(memory_space=pltpu.SMEM)] + [vmem] * 5 + [anywhere] * 9,
        out_specs=(vmem,) * 5,
        scratch_shapes=[
            pltpu.VMEM((4, 4, 16, UNITS), LOW), pltpu.VMEM((2, 2, 16, UNITS), LOW), pltpu.VMEM((2, 4, 16, UNITS), LOW),
            pltpu.VMEM((4, 16, UNITS), LOW), pltpu.VMEM((4, 16, PAIR), LOW), pltpu.VMEM((8, 16, PROJ), LOW), pltpu.VMEM((8, 8, 16, PAIR), LOW), pltpu.VMEM((2, 2, 2, 16, PAIR), LOW), pltpu.VMEM((2, 2, 4, 16, PAIR), LOW),
            pltpu.VMEM((2, 2, 16, PAIR), LOW), pltpu.VMEM((2, 4, 16, PAIR), LOW), pltpu.VMEM((8, ROWS, MODEL), LOW),
            pltpu.VMEM((4, ROWS, MODEL), LOW), pltpu.VMEM((2, ROWS, MID), LOW), pltpu.VMEM((2, ROWS, MODEL), LOW),
            pltpu.VMEM((8, ROWS, MODEL), LOW),
        ]
        + scatter_bufs()
        + [
            pltpu.VMEM((8, 16, 16, 1024), LOW), pltpu.VMEM((8, 8, 16, 1024), LOW), pltpu.VMEM((2, 2, 4, 16, 1024), LOW),
            pltpu.VMEM((2, 2, 8, 16, 1024), LOW), pltpu.VMEM((8, 16, 1024), LOW),
            pltpu.VMEM((8, 256, 1024), LOW),
            pltpu.VMEM((1024, PROJ), LOW), pltpu.VMEM((2, 2, 256, 1024), LOW), pltpu.VMEM((PART, 1024), LOW),
            pltpu.VMEM((1024, PART), LOW), pltpu.VMEM((1024, PROJ), LOW),
            pltpu.VMEM((1024, PART), WIDE), pltpu.VMEM((1024, PART), WIDE), pltpu.VMEM((2, 8, 2, 16, 1024), LOW),
            pltpu.SemaphoreType.DMA((count,)), pltpu.SemaphoreType.DMA((count,)), pltpu.SemaphoreType.DMA((14,)),
        ],
        compiler_params=pltpu.CompilerParams(collective_id=3, has_side_effects=True, vmem_limit_bytes=62 * 2**20),
        name="back",
    )(grad_resid, x, counts, resid, attn_weight, mlp_weight, gain_one, gain_two, down, grads, branch, acc, ones, wa, qkv, probs, att)
def local(
    tokens, valid_counts, block_owner, norm1_gain, attn_weight, norm2_gain, mlp_weight, cotangent
):
    x, cot = tokens[0], cotangent[0]
    gain_one, gain_two = norm1_gain[None], norm2_gain[None]
    ones, wa, grads, wm, qkv, probs, att, twos, resid = front(
        x, valid_counts, block_owner, cot, attn_weight, mlp_weight, gain_one, gain_two
    )
    acc, branch, branch_grads, grad_resid, down = mlp(resid, cot, valid_counts, twos, grads, wm)
    layer_out, input_grad, attn_grad, mlp_grad, gain_grads = back(
        grad_resid, x, valid_counts, resid, attn_weight, mlp_weight, gain_one, gain_two, down,
        branch_grads, branch, acc, ones, wa, qkv, probs, att,
    )
    return (layer_out[None], input_grad[None], gain_grads[:, 0], attn_grad, gain_grads[:, 128], mlp_grad)


def solution(mesh):
    token_spec = P("dp", "seq", None)
    row_spec = P(("seq", "dp"), None, None)
    gain_spec = P(("seq", "dp"))
    in_specs = (
        token_spec, P("dp", "seq"), P("dp", None), gain_spec, row_spec, gain_spec, row_spec, token_spec
    )
    out_specs = (token_spec, token_spec, gain_spec, row_spec, gain_spec, row_spec)
    return jax.shard_map(local, mesh=mesh, in_specs=in_specs, out_specs=out_specs, check_vma=False)
```

```python
import functools, math
import jax
import jax.numpy as jnp
from jax import lax
from jax.experimental import pallas as pl
from jax.experimental.pallas import tpu as pltpu
from jax.sharding import PartitionSpec as P

LOW = jnp.bfloat16
WIDE = jnp.float32
MESH = pl.DeviceIdType.MESH
EPS = 1e-05
HEAD_DIM = 128
ROWS = 128
MODEL = 2048
PART = 256
PROJ = 3 * PART
UNITS = 1408
SLAB = 3 * UNITS
PAIR = 2 * UNITS
FIRST = 112
MID = MODEL // 2


class Place:
    def __init__(self):
        self.seq, self.dp = lax.axis_index("seq"), lax.axis_index("dp")
        self.a, self.y = self.seq // 4, self.seq % 4
        self.b = 1 - self.a
        self.up, self.down, self.far = (self.y + 1) % 4, (self.y + 3) % 4, (self.y + 2) % 4
        self.z, self.h, self.core = self.dp // 4, self.dp // 2 % 2, self.dp % 2
        self.z_up, self.z_down, self.z_far = (self.z + 1) % 4, (self.z + 3) % 4, (self.z + 2) % 4
        self.x_dev = {"seq": self.b * 4 + self.y}
        self.up_dev = {"seq": self.a * 4 + self.up}
        self.down_dev = {"seq": self.a * 4 + self.down}
        self.h_dev = {"dp": self.member(self.z, 1 - self.h)}
        self.z_up_dev = {"dp": self.member(self.z_up, self.h)}
        self.z_down_dev = {"dp": self.member(self.z_down, self.h)}
        self.twin_dev = {"dp": self.dp + 1 - 2 * self.core}
        self.x = self.h * 2 + self.a
        self.x_up, self.x_down, self.x_far = (self.x + 1) % 4, (self.x + 3) % 4, (self.x + 2) % 4
        self.x_up_dev, self.x_down_dev = self.at_x(self.x_up), self.at_x(self.x_down)

    def member(self, z, h, twin=False):
        core = 1 - self.core if twin else self.core
        return z * 4 + h * 2 + core

    def at_x(self, x):
        return {"seq": x % 2 * 4 + self.y, "dp": self.member(self.z, x // 2)}

    def column(self, twin=False):
        return self.z * 4 + (1 - self.core if twin else self.core)

    def peers(self):
        return [{"seq": (self.seq + k) % 8} for k in range(1, 8)]


def greet(devices):
    barrier = pltpu.get_barrier_semaphore()
    for device in devices:
        pl.semaphore_signal(barrier, inc=1, device_id=device, device_id_type=MESH)
    return lambda: pl.semaphore_wait(barrier, len(devices))


class Mail:
    def __init__(self, send, recv):
        self.send, self.recv = send, recv
        self.count, self.started = 0, {}

    def slots(self, n):
        first = self.count
        self.count += n
        return first

    def copy(self, slot, src, dst, device):
        return pltpu.make_async_remote_copy(
            src_ref=src, dst_ref=dst, send_sem=self.send.at[slot], recv_sem=self.recv.at[slot],
            device_id=device, device_id_type=MESH,
        )

    def go(self, slot, src, dst, device):
        copy = self.copy(slot, src, dst, device)
        copy.start()
        self.started[slot] = copy

    def arrived(self, slot, dst, device):
        self.copy(slot, dst, dst, device).wait_recv()

    def sent(self, slot):
        self.started.pop(slot).wait_send()

    def finish(self):
        for copy in self.started.values():
            copy.wait_send()


def gather_seq(me, mail, x_ref, out_ref):
    a, b, y, up, down, far = me.a, me.b, me.y, me.up, me.down, me.far
    XP, U, D = me.x_dev, me.up_dev, me.down_dev
    n = mail.slots(18)

    def cut(ref, rows, half):
        lo, hi = ((0, FIRST), (FIRST, ROWS))[rows]
        return ref.at[lo:hi] if half is None else ref.at[lo:hi, half * MID : half * MID + MID]

    def at(col, row, rows, half=None):
        return cut(out_ref.at[col * 4 + row], rows, half)

    def send(i, rows, dev):
        mail.go(n + i, cut(x_ref, rows, None), at(a, y, rows), dev)

    def fwd(i, ref, dev):
        mail.go(n + i, ref, ref, dev)

    def got(i, dst):
        mail.arrived(n + i, dst, XP)

    send(0, 0, XP)
    send(1, 0, U)
    send(2, 0, D)
    send(3, 1, U)
    send(4, 1, D)
    send(5, 1, XP)
    yield
    got(0, at(b, y, 0))
    fwd(6, at(b, y, 0), U)
    fwd(7, at(b, y, 0), D)
    yield
    got(1, at(a, down, 0))
    fwd(8, at(a, down, 0, 0), U)
    got(2, at(a, up, 0))
    fwd(9, at(a, up, 0, 1), D)
    yield
    got(3, at(a, down, 1))
    fwd(10, at(a, down, 1, 0), U)
    fwd(11, at(a, down, 1), XP)
    got(4, at(a, up, 1))
    fwd(12, at(a, up, 1, 1), D)
    fwd(13, at(a, up, 1), XP)
    yield
    got(5, at(b, y, 1))
    got(6, at(b, down, 0))
    fwd(14, at(b, down, 0, 0), U)
    got(7, at(b, up, 0))
    fwd(15, at(b, up, 0, 1), D)
    yield
    got(10, at(a, far, 1, 0))
    fwd(16, at(a, far, 1, 0), XP)
    got(12, at(a, far, 1, 1))
    fwd(17, at(a, far, 1, 1), XP)
    yield
    got(8, at(a, far, 0, 0))
    got(9, at(a, far, 0, 1))
    got(11, at(b, down, 1))
    got(13, at(b, up, 1))
    yield
    got(14, at(b, far, 0, 0))
    got(15, at(b, far, 0, 1))
    got(16, at(b, far, 1, 0))
    got(17, at(b, far, 1, 1))


def gather_y(me, mail, x_ref, out_ref):
    y, up, down, far = me.y, me.up, me.down, me.far
    U, D = me.up_dev, me.down_dev
    n = mail.slots(4)
    H = ROWS // 2
    mail.go(n, x_ref, out_ref.at[y], U)
    mail.go(n + 1, x_ref, out_ref.at[y], D)
    yield
    mail.arrived(n, out_ref.at[down], D)
    mail.go(n + 2, out_ref.at[down, 0:H], out_ref.at[down, 0:H], U)
    mail.arrived(n + 1, out_ref.at[up], U)
    mail.go(n + 3, out_ref.at[up, H:ROWS], out_ref.at[up, H:ROWS], D)
    yield
    mail.arrived(n + 2, out_ref.at[far, 0:H], D)
    mail.arrived(n + 3, out_ref.at[far, H:ROWS], U)


def scatter_y(me, mail, part, p2, p1, out):
    y, up, down, far = me.y, me.up, me.down, me.far
    U, D = me.up_dev, me.down_dev
    n = mail.slots(6)
    left, right = pl.ds(0, MID), pl.ds(MID, MID)
    mail.go(n, part.at[far, :, left], p2.at[0], U)
    mail.go(n + 3, part.at[down, :, left], p1.at[1, :, left], D)
    yield
    mail.go(n + 1, part.at[far, :, right], p2.at[1], D)
    mail.go(n + 2, part.at[up, :, right], p1.at[0, :, right], U)
    yield
    mail.arrived(n, p2.at[0], D)
    add(part.at[up, :, left], p2.at[0])
    mail.go(n + 4, part.at[up, :, left], p1.at[0, :, left], U)
    mail.arrived(n + 1, p2.at[1], U)
    add(part.at[down, :, right], p2.at[1])
    mail.go(n + 5, part.at[down, :, right], p1.at[1, :, right], D)
    yield
    mail.arrived(n + 2, p1.at[0, :, right], D)
    mail.arrived(n + 3, p1.at[1, :, left], U)
    mail.arrived(n + 4, p1.at[0, :, left], D)
    mail.arrived(n + 5, p1.at[1, :, right], U)
    out(0, ROWS, val(part.at[y]) + val(p1.at[0]) + val(p1.at[1]))


def val(ref):
    return ref[...].astype(WIDE)


def add(dst, src):
    dst[...] = (val(dst) + val(src)).astype(LOW)


def swap_seq(me, mail, own_ref, all_ref, lo, hi):
    n = mail.slots(7)
    for k in range(1, 8):
        to = (me.seq + k) % 8
        mail.go(n + k - 1, own_ref.at[to, :, lo:hi], all_ref.at[me.seq, me.dp, :, lo:hi], {"seq": to})
    yield
    for k in range(1, 8):
        came = (me.seq + 8 - k) % 8
        mail.arrived(n + k - 1, all_ref.at[came, me.dp, :, lo:hi], me.x_dev)


def gather_dp(me, mail, ref):
    z, h = me.z, me.h
    n = mail.slots(19)
    HD, ZU, ZD, TW = me.h_dev, me.z_up_dev, me.z_down_dev, me.twin_dev

    def at(zz, hh, half=None, twin=False):
        d = me.member(zz, hh, twin)
        return ref.at[:, d] if half is None else ref.at[4 * half : 4 * half + 4, d]

    def fwd(i, r, dev):
        mail.go(n + i, r, r, dev)

    def got(i, r):
        mail.arrived(n + i, r, TW)

    hs = (h, 1 - h)
    fwd(0, at(z, h), HD)
    fwd(1, at(z, h), ZU)
    fwd(2, at(z, h), ZD)
    fwd(9, at(z, h), TW)
    yield
    got(0, at(z, 1 - h))
    fwd(3, at(z, 1 - h), ZU)
    fwd(4, at(z, 1 - h), ZD)
    fwd(10, at(z, 1 - h), TW)
    yield
    for k in range(2):
        got(1 + 2 * k, at(me.z_down, hs[k]))
        fwd(5 + 2 * k, at(me.z_down, hs[k], 0), ZU)
        fwd(11 + 2 * k, at(me.z_down, hs[k]), TW)
        yield
        got(2 + 2 * k, at(me.z_up, hs[k]))
        fwd(6 + 2 * k, at(me.z_up, hs[k], 1), ZD)
        fwd(12 + 2 * k, at(me.z_up, hs[k]), TW)
        yield
    for k in range(2):
        got(5 + 2 * k, at(me.z_far, hs[k], 0))
        fwd(15 + 2 * k, at(me.z_far, hs[k], 0), TW)
        got(6 + 2 * k, at(me.z_far, hs[k], 1))
        fwd(16 + 2 * k, at(me.z_far, hs[k], 1), TW)
        yield
    got(9, at(z, h, twin=True))
    got(10, at(z, 1 - h, twin=True))
    for k in range(2):
        got(11 + 2 * k, at(me.z_down, hs[k], twin=True))
        got(12 + 2 * k, at(me.z_up, hs[k], twin=True))
        got(15 + 2 * k, at(me.z_far, hs[k], 0, twin=True))
        got(16 + 2 * k, at(me.z_far, hs[k], 1, twin=True))


def swap_y(me, mail, own_ref, all_ref):
    n = mail.slots(3)
    for k in (2, 1, 3):
        to = (me.y + k) % 4
        mail.go(n + k - 1, own_ref.at[to], all_ref.at[me.seq, me.dp], {"seq": me.a * 4 + to})
    yield
    for k in (1, 3, 2):
        came = me.a * 4 + (me.y + 4 - k) % 4
        mail.arrived(n + k - 1, all_ref.at[came, me.dp], me.up_dev)


def slab(me, ref, x, z, half=None, twin=False):
    d = me.member(z, x // 2, twin)
    first = x % 2 * 4
    return ref.at[pl.ds(first, 4), d] if half is None else ref.at[pl.ds(first + 2 * half, 2), d]


def gather_xz(me, mail, ref):
    n = mail.slots(36)
    XU, XD, ZU, ZD, TW = me.x_up_dev, me.x_down_dev, me.z_up_dev, me.z_down_dev, me.twin_dev
    z, zu, zd, zf = me.z, me.z_up, me.z_down, me.z_far
    xs = (me.x, me.x_down, me.x_up, me.x_far)

    def at(x, zz, half=None, twin=False):
        return slab(me, ref, x, zz, half, twin)

    def fwd(i, r, dev):
        mail.go(n + i, r, r, dev)

    def got(i, r):
        mail.arrived(n + i, r, TW)

    def z_first(k):
        fwd(4 + 4 * k, at(xs[k], z), ZU)
        fwd(5 + 4 * k, at(xs[k], z), ZD)
        fwd(20 + 4 * k, at(xs[k], z), TW)

    def z_second(k):
        got(4 + 4 * k, at(xs[k], zd))
        fwd(6 + 4 * k, at(xs[k], zd, 0), ZU)
        fwd(21 + 4 * k, at(xs[k], zd), TW)
        got(5 + 4 * k, at(xs[k], zu))
        fwd(7 + 4 * k, at(xs[k], zu, 1), ZD)
        fwd(22 + 4 * k, at(xs[k], zu), TW)

    def z_third(k):
        got(6 + 4 * k, at(xs[k], zf, 0))
        got(7 + 4 * k, at(xs[k], zf, 1))
        fwd(23 + 4 * k, at(xs[k], zf), TW)

    z_first(0)
    yield
    fwd(0, at(me.x, z), XU)
    fwd(1, at(me.x, z), XD)
    yield
    got(0, at(me.x_down, z))
    fwd(2, at(me.x_down, z, 0), XU)
    got(1, at(me.x_up, z))
    fwd(3, at(me.x_up, z, 1), XD)
    z_first(1)
    z_first(2)
    yield
    got(2, at(me.x_far, z, 0))
    got(3, at(me.x_far, z, 1))
    z_first(3)
    yield
    for k in range(4):
        z_second(k)
        yield
    for k in range(4):
        z_third(k)
        yield
    for k in range(4):
        for i, zz in enumerate((z, zd, zu, zf)):
            got(20 + 4 * k + i, at(xs[k], zz, twin=True))


def add_slabs(dst, *sources):
    def one(i, carry):
        total = val(dst.at[i])
        for source in sources:
            total = total + val(source.at[i])
        dst[i] = total.astype(LOW)
        return carry

    lax.fori_loop(0, dst.shape[0], one, 0)


def halved(ref, half):
    k = ref.shape[0] // 2
    return ref.at[half * k : half * k + k]


class RingSum:
    def __init__(self, mail, at, places, devices, over, near):
        self.mail, self.at, self.places, self.devices = mail, at, places, devices
        self.over, self.near = over, near
        self.n = mail.slots(6)

    def first(self):
        own, up, down, far = self.places
        U, D = self.devices
        go, n = self.mail.go, self.n
        go(n, halved(self.at(far), 0), self.over.at[0], U)
        go(n + 1, halved(self.at(far), 1), self.over.at[1], D)
        go(n + 2, halved(self.at(up), 1), halved(self.near.at[0], 1), U)
        go(n + 3, halved(self.at(down), 0), halved(self.near.at[1], 0), D)

    def second(self):
        own, up, down, far = self.places
        U, D = self.devices
        go, got, n = self.mail.go, self.mail.arrived, self.n
        got(n, self.over.at[0], D)
        add_slabs(halved(self.at(up), 0), self.over.at[0])
        go(n + 4, halved(self.at(up), 0), halved(self.near.at[0], 0), U)
        got(n + 1, self.over.at[1], U)
        add_slabs(halved(self.at(down), 1), self.over.at[1])
        go(n + 5, halved(self.at(down), 1), halved(self.near.at[1], 1), D)

    def third(self):
        own = self.places[0]
        U, D = self.devices
        got, n = self.mail.arrived, self.n
        got(n + 2, halved(self.near.at[0], 1), D)
        got(n + 3, halved(self.near.at[1], 0), U)
        got(n + 4, halved(self.near.at[0], 0), D)
        got(n + 5, halved(self.near.at[1], 1), U)
        add_slabs(self.at(own), self.near.at[0], self.near.at[1])


def twin_sum(me, mail, stage, acc, order, product, kept=None):
    slots = stage.shape[0]
    n = mail.slots(len(order))

    def settle(i):
        mail.arrived(n + i, acc.at[order[i]], me.twin_dev)
        add_slabs(acc.at[order[i]], stage.at[i % slots, :, me.core])
        if kept is not None:
            kept(i)

    for i, s in enumerate(order):
        if i >= slots:
            mail.sent(n + i - slots)
        product(s, stage.at[i % slots])
        mail.go(n + i, stage.at[i % slots, :, 1 - me.core], acc.at[s], me.twin_dev)
        if i > 0:
            settle(i - 1)
        yield
    settle(len(order) - 1)
    for i in range(max(0, len(order) - slots), len(order)):
        mail.sent(n + i)


def scatter_z(me, mail, acc, xs, z_over, z_near):
    zs = (me.z, me.z_up, me.z_down, me.z_far)

    def at(x):
        return lambda z: acc.at[pl.ds(x % 2 * 4, 4), z * 2 + x // 2]

    rings = [RingSum(mail, at(x), zs, (me.z_up_dev, me.z_down_dev), z_over.at[k], z_near.at[k]) for k, x in enumerate(xs)]
    rings[0].first()
    yield
    for ring in rings[1:]:
        ring.first()
    yield
    for ring in rings:
        ring.second()
        yield
    for ring in rings[:-1]:
        ring.third()
        yield
    rings[-1].third()


def scatter_x(me, mail, at, x_over, x_near):
    places = (me.x, me.x_up, me.x_down, me.x_far)
    ring = RingSum(mail, at, places, (me.x_up_dev, me.x_down_dev), x_over, x_near)
    ring.first()
    yield
    ring.second()
    yield
    ring.third()


def scatter_hz(me, mail, acc, z_over, z_near, h_near):
    hs = (1 - me.h, me.h)
    zs = (me.z, me.z_up, me.z_down, me.z_far)

    def at(h):
        return lambda z: acc.at[:, z * 2 + h]

    rings = [RingSum(mail, at(h), zs, (me.z_up_dev, me.z_down_dev), z_over.at[k], z_near.at[k]) for k, h in enumerate(hs)]
    n = mail.slots(1)
    rings[0].first()
    rings[1].first()
    yield
    for k in range(2):
        rings[k].second()
        yield
    rings[0].third()
    mail.go(n, at(1 - me.h)(me.z), h_near, me.h_dev)
    yield
    rings[1].third()
    yield
    mail.arrived(n, h_near, me.h_dev)
    add_slabs(at(me.h)(me.z), h_near)


def send_y(me, mail, slab, result):
    n = mail.slots(3)
    for k in (2, 1, 3):
        to = (me.y + k) % 4
        mail.go(n + k - 1, slab.at[to], result.at[me.y], {"seq": me.a * 4 + to})
    result[me.y] = slab[me.y]
    yield
    for k in (1, 3, 2):
        mail.arrived(n + k - 1, result.at[(me.y + 4 - k) % 4], me.up_dev)


def send_seq(me, mail, slab, result, lo, hi):
    n = mail.slots(7)
    for k in range(1, 8):
        to = (me.seq + k) % 8
        mail.go(n + k - 1, slab.at[to, :, lo:hi], result.at[me.seq], {"seq": to})
    result[me.seq] = slab[me.seq, :, lo:hi]
    yield
    for k in range(1, 8):
        mail.arrived(n + k - 1, result.at[(me.seq + 8 - k) % 8], me.x_dev)


def scatter_bufs():
    late = ROWS - FIRST
    shapes = ((4, late, MODEL), (2, late, MID), (2, late, MODEL), (4, FIRST, MID), (4, FIRST, MODEL), (1, FIRST, MODEL))
    return [pltpu.VMEM(shape, LOW) for shape in shapes]


def scatter_seq(me, mail, part, bufs, out):
    a, b, y, up, down, far = me.a, me.b, me.y, me.up, me.down, me.far
    XP, U, D = me.x_dev, me.up_dev, me.down_dev
    qx, q2, q1, p2, p1, px = bufs
    n = mail.slots(23)
    halves = (pl.ds(0, MID), pl.ds(MID, MID))

    def go(i, src, dst, dev):
        mail.go(n + i, src, dst, dev)

    def got(i, dst):
        mail.arrived(n + i, dst, XP)

    def at(col, row, rows, half=None):
        lo, hi = ((0, FIRST), (FIRST, ROWS))[rows]
        ref = part.at[col * 4 + row]
        return ref.at[lo:hi] if half is None else ref.at[lo:hi, halves[half]]

    def lane(ref, k, half):
        return ref.at[k, :, halves[half]]

    for k, row in enumerate((far, down, up, y)):
        go(k, at(b, row, 1), qx.at[row], XP)
    cols = (b, a)

    def p_first(k):
        c, s = cols[k], 10 + 6 * k
        go(s, at(c, far, 0, 0), p2.at[2 * k], U)
        go(s + 1, at(c, far, 0, 1), p2.at[2 * k + 1], D)
        go(s + 2, at(c, up, 0, 1), lane(p1, 2 * k, 1), U)
        go(s + 3, at(c, down, 0, 0), lane(p1, 2 * k + 1, 0), D)

    def p_second(k):
        c, s = cols[k], 10 + 6 * k
        got(s, p2.at[2 * k])
        add(at(c, up, 0, 0), p2.at[2 * k])
        go(s + 4, at(c, up, 0, 0), lane(p1, 2 * k, 0), U)
        got(s + 1, p2.at[2 * k + 1])
        add(at(c, down, 0, 1), p2.at[2 * k + 1])
        go(s + 5, at(c, down, 0, 1), lane(p1, 2 * k + 1, 1), D)

    def p_third(k):
        s = 10 + 6 * k
        got(s + 2, lane(p1, 2 * k, 1))
        got(s + 3, lane(p1, 2 * k + 1, 0))
        got(s + 4, lane(p1, 2 * k, 0))
        got(s + 5, lane(p1, 2 * k + 1, 1))
        return val(at(cols[k], y, 0)) + val(p1.at[2 * k]) + val(p1.at[2 * k + 1])

    p_first(0)
    yield
    p_first(1)
    yield
    got(0, qx.at[far])
    add(at(a, far, 1), qx.at[far])
    go(4, at(a, far, 1, 0), q2.at[0], U)
    go(5, at(a, far, 1, 1), q2.at[1], D)
    yield
    p_second(0)
    yield
    got(1, qx.at[down])
    add(at(a, down, 1), qx.at[down])
    go(6, at(a, down, 1, 0), lane(q1, 1, 0), D)
    got(2, qx.at[up])
    add(at(a, up, 1), qx.at[up])
    go(7, at(a, up, 1, 1), lane(q1, 0, 1), U)
    yield
    p_second(1)
    yield
    rows = p_third(0)
    own = at(b, y, 0)
    own[...] = rows.astype(LOW)
    go(22, own, px.at[0], XP)
    yield
    got(4, q2.at[0])
    add(at(a, up, 1, 0), q2.at[0])
    go(8, at(a, up, 1, 0), lane(q1, 0, 0), U)
    got(5, q2.at[1])
    add(at(a, down, 1, 1), q2.at[1])
    go(9, at(a, down, 1, 1), lane(q1, 1, 1), D)
    yield
    rows = p_third(1)
    got(22, px.at[0])
    out(0, FIRST, rows + val(px.at[0]))
    yield
    got(3, qx.at[y])
    got(6, lane(q1, 1, 0))
    got(7, lane(q1, 0, 1))
    got(8, lane(q1, 0, 0))
    got(9, lane(q1, 1, 1))
    out(FIRST, ROWS, val(at(a, y, 1)) + val(qx.at[y]) + val(q1.at[0]) + val(q1.at[1]))


def run(*tasks):
    tasks = list(tasks)
    while tasks:
        for task in list(tasks):
            if next(task, tasks) is tasks:
                tasks.remove(task)


def step(task, count=1):
    for _ in range(count):
        next(task, None)


def beside(task, other):
    for _ in task:
        step(other)
        yield


def finish(task, *others):
    k = 0
    while next(task, others) is not others:
        k += 1
        if k % 2 == 0 and others:
            step(others[k // 2 % len(others)])
def dot(a, b, dims=((1,), (0,))):
    return lax.dot_general(a, b, (dims, ((), ())), preferred_element_type=WIDE)


def row_scale(values):
    return lax.rsqrt(jnp.mean(values * values, axis=-1, keepdims=True) + EPS)


def column(row_ref):
    shape = (16, 16)
    here = lax.broadcasted_iota(jnp.int32, shape, 0) == lax.broadcasted_iota(jnp.int32, shape, 1)
    return jnp.sum(jnp.where(here, row_ref[...].astype(WIDE), 0.0), axis=1, keepdims=True)


def live_rows(count_ref):
    return jnp.where(lax.broadcasted_iota(jnp.int32, (ROWS, 1), 0) < count_ref[0, 0], 1.0, 0.0).astype(WIDE)


def front_kernel(
    x_ref, count_ref, owner_ref, cot_ref, attn_ref, mlp_ref, gain_one, gain_two,
    one_out, wa_out, grad_all, wm, qkv_out, probs_out, att_out, two_all, resid,
    one_all, wa, grad_own, qkv, probs, att, ones_t, att_t, two, wa_own, wm_own, pos_k, part, qx, q2, q1, p2, p1, px, send, recv, local_sem,
):
    me = Place()
    mail = Mail(send, recv)
    saves = []

    def save(src, dst):
        copy = pltpu.make_async_copy(src, dst, local_sem.at[len(saves)])
        copy.start()
        saves.append(copy)
        return copy

    ready = greet(me.peers() + [me.h_dev, me.z_up_dev, me.z_down_dev, me.twin_dev, me.x_up_dev, me.x_down_dev])
    live = live_rows(count_ref)
    x = x_ref[...].astype(WIDE)
    one_all[me.seq] = (x * row_scale(x) * live).astype(LOW)
    ready()
    gather_one = gather_seq(me, mail, one_all.at[me.seq], one_all)
    step(gather_one)
    gain = column(gain_one)
    for slot in range(4):
        weight = attn_ref[:, slot, :].astype(WIDE)
        if slot < 3:
            weight = weight * gain
        for to in range(8):
            wa_own[to, :, slot * PART : slot * PART + PART] = weight[:, to * PART : to * PART + PART].astype(LOW)
    swap_a = swap_seq(me, mail, wa_own, wa, 0, PROJ)
    step(swap_a)
    gain = column(gain_two)
    units = mlp_ref.shape[2] // 4
    for slot in range(3):
        weight = mlp_ref[:, slot, :].astype(WIDE)
        if slot < 2:
            weight = weight * gain
        for to in range(4):
            piece = weight if to == 0 else pltpu.roll(weight, (4 - to) * units, 1)
            piece = piece[:, 0:UNITS]
            piece = jnp.where(lax.broadcasted_iota(jnp.int32, piece.shape, 1) < units, piece, 0.0).astype(LOW)
            for tile in range(UNITS // 128):
                first = PAIR + tile * 128 if slot == 2 else (2 * tile + slot) * 128
                wm_own[to, :, first : first + 128] = piece[:, tile * 128 : tile * 128 + 128]
    swap_m = swap_y(me, mail, wm_own, wm)
    step(swap_m)
    keep_m = save(wm_own.at[me.y], wm.at[me.seq, me.dp])
    for block in range(8):
        columns = lax.broadcasted_iota(jnp.int32, (1, ROWS), 1)
        pos_k[:, block * ROWS : block * ROWS + ROWS] = columns + owner_ref[0, block] * ROWS
    wa[pl.ds(me.seq, 1), pl.ds(me.dp, 1), :, 0:PROJ] = wa_own[pl.ds(me.seq, 1), :, 0:PROJ][None]
    for k in range(8):
        wa[k, pl.ds(me.dp, 1), :, PROJ:] = wa_own[k, :, PROJ:][None]
    step(swap_a)
    gather_wa = gather_dp(me, mail, wa)
    step(gather_wa)
    grad_own[...] = (cot_ref[...].astype(WIDE) * live).astype(LOW)
    save(grad_own, grad_all.at[me.y])
    step(gather_one)
    step(gather_wa)
    step(gather_one)
    step(gather_wa, 2)
    step(gather_one)
    step(gather_wa, 2)
    step(swap_m)
    keep_m.wait()
    gather_wm = gather_xz(me, mail, wm)
    step(gather_wm, 2)
    step(gather_one, 2)
    gather_g = gather_y(me, mail, grad_own, grad_all)
    step(gather_g)
    step(gather_one)
    run(gather_wa)

    def project(i, carry):
        rows = one_all[pl.ds(i * 2, 2)].reshape(2 * ROWS, MODEL)
        weight = wa[:, :, :, 0:PROJ].reshape(MODEL, PROJ)
        qkv[pl.ds(pl.multiple_of(i * 256, 256), 256), :] = dot(rows, weight).astype(LOW)
        return carry

    lax.fori_loop(me.a * 2, me.a * 2 + 2, project, 0)
    run(gather_one)
    step(gather_wm)
    save(wa, wa_out)

    def attend(i, carry):
        first = pl.multiple_of(i * ROWS, ROWS)
        rows = pl.ds(first, ROWS)
        allowed = pos_k[...] <= lax.broadcasted_iota(jnp.int32, (ROWS, 1), 0) + owner_ref[0, i] * ROWS
        for head in range(2):
            lo, hi = head * HEAD_DIM, (head + 1) * HEAD_DIM
            q = qkv[rows, lo:hi]
            k = qkv[:, PART + lo : PART + hi]
            v = qkv[:, 2 * PART + lo : 2 * PART + hi]
            odds = jnp.exp2(math.log2(8 * ROWS) - dot(q, k, ((1,), (1,))) * (math.log2(math.e) / math.sqrt(HEAD_DIM)))
            p = jnp.where(allowed, 1.0 / (1.0 + odds), 0.0).astype(LOW)
            probs[head, rows, :] = p
            att[rows, lo:hi] = dot(p, v).astype(LOW)
        return carry

    def out_project(col):
        rows = att[pl.ds(pl.multiple_of(col * 512, 512), 512), :]

        def piece(k, carry):
            weight = wa[k, :, :, PROJ:].reshape(PART, PART)
            columns = pl.ds(pl.multiple_of(k * PART, PART), PART)
            part[pl.ds(col * 4, 4), :, columns] = dot(rows, weight).reshape(4, ROWS, PART).astype(LOW)
            return carry

        lax.fori_loop(0, 8, piece, 0)

    lax.fori_loop(me.b * 2, me.b * 2 + 2, project, 0)
    step(gather_g)
    save(qkv, qkv_out)

    def write(lo, hi, rows):
        total = x_ref[lo:hi].astype(WIDE) + rows
        resid[lo:hi] = total
        two[lo:hi] = (total * row_scale(total) * live[lo:hi]).astype(LOW)

    scatter = scatter_seq(me, mail, part, (qx, q2, q1, p2, p1, px), write)
    lax.fori_loop(me.b * 4, me.b * 4 + 4, attend, 0)
    out_project(me.b)
    step(scatter)
    step(gather_wm)
    lax.fori_loop(me.a * 4, me.a * 4 + 4, attend, 0)
    out_project(me.a)
    step(scatter)
    save(probs, probs_out)
    finish(scatter, gather_wm)
    gather_two = gather_y(me, mail, two, two_all)
    step(gather_two)
    save(two, two_all.at[me.y])
    step(gather_wm)

    def turn(s, carry):
        columns = pl.ds(pl.multiple_of(s * 256, 256), 256)
        ones_t[s] = one_all[:, :, columns].reshape(8 * ROWS, 256).T
        return carry

    att_t[...] = att[...].T
    save(att_t, att_out)
    for i in range(4):
        lax.fori_loop(2 * i, 2 * i + 2, turn, 0)
        step(gather_wm)
        if i == 1:
            step(gather_two)
    save(ones_t, one_out)
    run(gather_wm, gather_g, gather_two)
    for copy in saves:
        if copy is not keep_m:
            copy.wait()
    mail.finish()


def front(x, counts, owners, cot, attn_weight, mlp_weight, gain_one, gain_two):
    vmem, anywhere = pl.BlockSpec(memory_space=pltpu.VMEM), pl.BlockSpec(memory_space=pl.ANY)
    shape = jax.ShapeDtypeStruct
    count = 7 + 18 + 19 + 3 + 36 + 4 + 23 + 4
    return pl.pallas_call(
        front_kernel,
        out_shape=(
            shape((8, 256, 1024), LOW), shape((8, 16, 16, 1024), LOW), shape((4, ROWS, MODEL), LOW),
            shape((8, 16, 16, SLAB), LOW), shape((1024, PROJ), LOW), shape((2, 1024, 1024), LOW),
            shape((PART, 1024), LOW), shape((4, ROWS, MODEL), LOW), shape((ROWS, MODEL), WIDE),
        ),
        in_specs=[vmem] + [pl.BlockSpec(memory_space=pltpu.SMEM)] * 2 + [vmem] * 5,
        out_specs=(anywhere,) * 8 + (vmem,),
        scratch_shapes=[
            pltpu.VMEM((8, ROWS, MODEL), LOW), pltpu.VMEM((8, 16, 16, 1024), LOW), pltpu.VMEM((ROWS, MODEL), LOW),
            pltpu.VMEM((1024, PROJ), LOW), pltpu.VMEM((2, 1024, 1024), LOW), pltpu.VMEM((1024, PART), LOW),
            pltpu.VMEM((8, 256, 1024), LOW), pltpu.VMEM((PART, 1024), LOW), pltpu.VMEM((ROWS, MODEL), LOW),
            pltpu.VMEM((8, 16, 1024), LOW), pltpu.VMEM((4, 16, SLAB), LOW), pltpu.VMEM((1, 1024), jnp.int32),
            pltpu.VMEM((8, ROWS, MODEL), LOW),
        ]
        + scatter_bufs()
        + [pltpu.SemaphoreType.DMA((count,)), pltpu.SemaphoreType.DMA((count,)), pltpu.SemaphoreType.DMA((9,))],
        compiler_params=pltpu.CompilerParams(collective_id=1, has_side_effects=True, vmem_limit_bytes=56 * 2**20),
        name="front",
    )(x, counts, owners, cot, attn_weight, mlp_weight, gain_one, gain_two)
def mlp_kernel(
    resid, cot_ref, count_ref, two_all, grad_all, wm_all,
    acc_out, branch_out, branch_grads, grad_resid, down_out,
    wm, grads, twos, hidden, pair, part, branch, p2, p1, grad_branch,
    stage_d, acc_d, z_over, z_near, pz_over, pz_near, stage, acc, send, recv, local_sem, wm_sem,
):
    me = Place()
    mail = Mail(send, recv)
    saves, first_saves = [], []

    def save(src, dst):
        copy = pltpu.make_async_copy(src, dst, local_sem.at[len(saves)])
        copy.start()
        saves.append(copy)
        return copy

    live = live_rows(count_ref)
    loads = [save(two_all, twos), save(grad_all, grads)]

    def weights(j, wide):
        for first, each, sem in ((0, 256, 0), (PAIR, 128, 6)):
            columns = pl.ds(pl.multiple_of(first + j * each, 128), wide * each)
            yield pltpu.make_async_copy(
                wm_all.at[:, :, :, columns], wm.at[:, :, :, columns], wm_sem.at[sem + j // 2]
            )

    for j in range(0, UNITS // 128, 2):
        for copy in weights(j, min(2, UNITS // 128 - j)):
            copy.start()
    ready = greet([me.x_dev, me.up_dev, me.down_dev, me.z_up_dev, me.z_down_dev, me.twin_dev])
    for load in loads:
        load.wait()

    def tall(ref, columns=slice(None)):
        values = ref[:, :, columns]
        return values.reshape(4 * ROWS, values.shape[2])

    def put(ref, columns, values):
        ref[:, :, columns] = values.reshape(4, ROWS, values.shape[1]).astype(LOW)

    def ahead(j, wide):
        for copy in weights(j, wide):
            copy.wait()
        start = pl.multiple_of(j * 128, 128)
        width = wide * 128
        weight = wm[:, :, :, pl.ds(2 * start, 2 * width)].reshape(MODEL, 2 * width)
        gate_up = dot(tall(twos), weight)
        down = wm[:, :, :, pl.ds(PAIR + start, width)].reshape(MODEL, width)
        grad_hidden = dot(tall(grads), down)
        low, pairs = [], []
        for i in range(wide):
            gate = gate_up[:, i * 256 : i * 256 + 128]
            up = gate_up[:, i * 256 + 128 : i * 256 + 256]
            grad = grad_hidden[:, i * 128 : i * 128 + 128]
            squashed = 1.0 / (1.0 + jnp.exp(-gate))
            active = gate * squashed
            low.append(active * up)
            pairs.append(grad * up * (squashed * (1.0 + gate * (1.0 - squashed))))
            pairs.append(grad * active)
        put(hidden, pl.ds(start, width), jnp.concatenate(low, axis=1))
        put(pair, pl.ds(2 * start, 2 * width), jnp.concatenate(pairs, axis=1))

    def ahead_tile(j, carry):
        ahead(2 * j, 2)
        return carry

    def back(s, carry):
        columns = pl.ds(pl.multiple_of(s * 256, 256), 256)
        weight = wm[s, :, :, 0:PAIR].reshape(256, PAIR)
        put(part, columns, dot(tall(pair), weight, ((1,), (1,))))
        return carry

    def down_back(s, carry):
        columns = pl.ds(pl.multiple_of(s * 256, 256), 256)
        weight = wm[s, :, :, PAIR:].reshape(256, UNITS)
        put(branch, columns, dot(tall(hidden), weight, ((1,), (1,))))
        return carry

    def write(lo, hi, rows):
        x = resid[lo:hi]
        scale = row_scale(x)
        hat = x * scale
        inner = jnp.mean(rows * hat, axis=-1, keepdims=True)
        total = cot_ref[lo:hi].astype(WIDE) * live[lo:hi] + scale * (rows - hat * inner)
        grad_resid[lo:hi] = total
        grad_branch[lo:hi] = total.astype(LOW)

    order = [me.a * 4 + i for i in range(4)] + [me.b * 4 + i for i in range(4)]

    def columns_t(ref, s):
        return ref[:, :, pl.ds(pl.multiple_of(s * 256, 256), 256)].reshape(4 * ROWS, 256).T

    def down_product(s, out):
        terms = dot(columns_t(grads, s), hidden[...].reshape(4 * ROWS, UNITS))
        out[...] = terms.reshape(8, 2, 16, UNITS).astype(LOW)

    def pair_product(s, out):
        terms = dot(columns_t(twos, s), pair[...].reshape(4 * ROWS, PAIR))
        out[...] = terms.reshape(8, 2, 16, PAIR).astype(LOW)

    def kept(i):
        first_saves.append(save(acc.at[order[i]], acc_out.at[order[i]]))

    scatter = scatter_y(me, mail, part, p2, p1, write)
    twin_d = twin_sum(me, mail, stage_d, acc_d, order, down_product)
    twin = twin_sum(me, mail, stage, acc, order, pair_product, kept)
    sums = scatter_z(me, mail, acc_d, (me.x_far, me.x_up, me.x_down, me.x), z_over, z_near)
    early = scatter_z(me, mail, acc, (me.x_far, me.x_up), pz_over, pz_near)
    gather = gather_seq(me, mail, grad_branch, branch_grads)
    lax.fori_loop(0, 5, ahead_tile, 0)
    ahead(10, 1)
    lax.fori_loop(0, 4, back, 0)
    ready()
    step(scatter)
    lax.fori_loop(4, 8, back, 0)
    step(scatter)
    run(twin_d)
    step(sums, 2)
    step(scatter)
    step(twin, 3)
    step(sums, 2)
    step(twin, 3)
    step(scatter)
    step(gather)
    keep = save(grad_branch, branch_grads.at[me.seq])
    step(sums)
    run(twin)
    step(early, 2)
    step(sums)
    step(gather)
    for copy in first_saves:
        copy.wait()
    for i in range(5):
        if i < 4:
            lax.fori_loop(2 * i, 2 * i + 2, down_back, 0)
        step(sums if i < 3 else early)
        step(gather)
    save(branch, branch_out)
    finish(gather, sums, early)
    run(sums, early)
    for x in range(4):
        save(acc_d.at[x % 2 * 4 : x % 2 * 4 + 4, me.z * 2 + x // 2], down_out.at[x])
    for x in (me.x_far, me.x_up):
        place = pl.ds(x % 2 * 4, 4), me.z * 2 + x // 2
        save(acc.at[place], acc_out.at[place])
    for copy in saves[2:]:
        if not any(copy is first for first in first_saves):
            copy.wait()
    mail.finish()


def mlp(resid, cot, counts, twos, grads, wm):
    vmem, anywhere = pl.BlockSpec(memory_space=pltpu.VMEM), pl.BlockSpec(memory_space=pl.ANY)
    shape = jax.ShapeDtypeStruct
    blocks = (4, ROWS, MODEL)
    count = 6 + 8 + 8 + 24 + 12 + 18
    return pl.pallas_call(
        mlp_kernel,
        out_shape=(
            shape((8, 8, 16, PAIR), LOW), shape(blocks, LOW), shape((8, ROWS, MODEL), LOW), shape((ROWS, MODEL), WIDE),
            shape((4, 4, 16, UNITS), LOW),
        ),
        in_specs=[vmem] * 2 + [pl.BlockSpec(memory_space=pltpu.SMEM)] + [anywhere] * 3,
        out_specs=(anywhere,) * 3 + (vmem, anywhere),
        scratch_shapes=[
            pltpu.VMEM((8, 16, 16, SLAB), LOW), pltpu.VMEM(blocks, LOW), pltpu.VMEM(blocks, LOW),
            pltpu.VMEM((4, ROWS, UNITS), LOW), pltpu.VMEM((4, ROWS, PAIR), LOW), pltpu.VMEM(blocks, LOW),
            pltpu.VMEM(blocks, LOW), pltpu.VMEM((2, ROWS, MID), LOW), pltpu.VMEM((2, ROWS, MODEL), LOW),
            pltpu.VMEM((ROWS, MODEL), LOW),
            pltpu.VMEM((2, 8, 2, 16, UNITS), LOW), pltpu.VMEM((8, 8, 16, UNITS), LOW),
            pltpu.VMEM((4, 2, 2, 16, UNITS), LOW), pltpu.VMEM((4, 2, 4, 16, UNITS), LOW),
            pltpu.VMEM((2, 2, 2, 16, PAIR), LOW), pltpu.VMEM((2, 2, 4, 16, PAIR), LOW),
            pltpu.VMEM((2, 8, 2, 16, PAIR), LOW), pltpu.VMEM((8, 8, 16, PAIR), LOW),
            pltpu.SemaphoreType.DMA((count,)), pltpu.SemaphoreType.DMA((count,)), pltpu.SemaphoreType.DMA((18,)), pltpu.SemaphoreType.DMA((12,)),
        ],
        compiler_params=pltpu.CompilerParams(collective_id=2, has_side_effects=True, vmem_limit_bytes=62 * 2**20),
        name="mlp",
    )(resid, cot, counts, twos, grads, wm)
def back_kernel(
    grad_resid, x_ref, count_ref, resid, attn_ref, mlp_ref, gain_one, gain_two, down_all, branch_grads, branch_all, acc_all, one_all, wa_all, qkv_all, probs_all, att_all,
    layer_out, input_grad, attn_grad, mlp_grad, gain_grads,
    down, dx_over, dx_near, down_own, pair_own, in_own, acc, z_over, z_near, x_over, x_near, grads, branch, b2, b1, part, qx, q2, q1, p2, p1, px,
    wa, acc_a, az_over, az_near, h_near, ones_t, qkv, probs, att_t, grad_att, grad_proj, grad_k, grad_v, stage_a,
    send, recv, local_sem,
):
    me = Place()
    mail = Mail(send, recv)
    loads = []
    live = live_rows(count_ref)

    def load(src, dst):
        copy = pltpu.make_async_copy(src, dst, local_sem.at[len(loads)])
        copy.start()
        loads.append(copy)
        return copy

    load_acc = [load(acc_all.at[pl.ds(col * 4, 4)], acc.at[pl.ds(col * 4, 4)]) for col in (me.b, me.a)]
    load_down = load(down_all, down)
    load_branch = load(branch_all, branch)
    ready = greet(me.peers() + [me.h_dev, me.z_up_dev, me.z_down_dev, me.x_up_dev, me.x_down_dev, me.twin_dev])
    load_grads = load(branch_grads, grads)
    load_wa = load(wa_all, wa)
    waits = [load(*both) for both in ((qkv_all, qkv), (att_all, att_t), (one_all, ones_t))]
    fetch = [load(probs_all.at[:, 256 * i : 256 * i + 256], probs.at[i]) for i in range(2)]
    order = [me.a * 4 + i for i in range(4)] + [me.b * 4 + i for i in range(4)]

    def columns_of(s, width=256):
        return pl.ds(pl.multiple_of(s * width, width), width)

    def down_sums():
        yield from scatter_x(me, mail, lambda x: down.at[x], dx_over, dx_near)
        yield from send_y(me, mail, down.at[me.x], down_own)

    def pair_sums():
        yield from scatter_z(me, mail, acc, (me.x_down, me.x), z_over, z_near)
        yield from scatter_x(me, mail, lambda x: acc.at[pl.ds(x % 2 * 4, 4), me.z * 2 + x // 2], x_over, x_near)
        yield from send_y(me, mail, acc.at[pl.ds(me.a * 4, 4), me.z * 2 + me.h], pair_own)

    downs = down_sums()
    sums = pair_sums()

    load_acc[0].wait()
    ready()
    step(sums)
    load_acc[1].wait()
    step(sums)
    load_down.wait()
    step(downs)
    def write_out(lo, hi, rows):
        layer_out[lo:hi] = (live[lo:hi] * (resid[lo:hi] + rows)).astype(LOW)

    out_sum = scatter_y(me, mail, branch, b2, b1, write_out)
    load_branch.wait()
    step(out_sum, 2)
    load_grads.wait()
    def write_grad(lo, hi, rows):
        x = x_ref[lo:hi].astype(WIDE)
        scale = row_scale(x)
        hat = x * scale
        inner = jnp.mean(rows * hat, axis=-1, keepdims=True)
        input_grad[lo:hi] = grad_resid[lo:hi] + live[lo:hi] * scale * (rows - hat * inner)

    grad_sum = scatter_seq(me, mail, part, (qx, q2, q1, p2, p1, px), write_grad)

    load_wa.wait()
    for wait in waits:
        wait.wait()
    head_scale = 1.0 / math.sqrt(HEAD_DIM)

    def attended_grad(i, carry):
        total = jnp.zeros((256, PART), WIDE)
        for k in range(8):
            rows = grads[pl.ds(i * 2, 2), :, k * PART : k * PART + PART].reshape(256, PART)
            total = total + dot(rows, wa[k, :, :, PROJ:].reshape(PART, PART), ((1,), (1,)))
        grad_att[columns_of(i), :] = total.astype(LOW)
        return carry

    lax.fori_loop(0, 4, attended_grad, 0)
    grad_k[...] = jnp.zeros_like(grad_k)
    grad_v[...] = jnp.zeros_like(grad_v)

    def attend_back(i):
        rows = pl.ds(256 * i, 256)
        for head in range(2):
            lo, hi = head * HEAD_DIM, (head + 1) * HEAD_DIM
            low = probs[i % 2, head]
            p = low.astype(WIDE)
            g = grad_att[rows, lo:hi]
            back = dot(g, qkv[:, 2 * PART + lo : 2 * PART + hi], ((1,), (1,)))
            grad_s = (back * (p * (1.0 - p))).astype(LOW)
            grad_q = dot(grad_s, qkv[:, PART + lo : PART + hi]) * head_scale
            grad_proj[rows, lo:hi] = grad_q.astype(LOW)
            grad_v[:, lo:hi] += dot(low, g, ((0,), (0,)))
            grad_k[:, lo:hi] += dot(grad_s, qkv[rows, lo:hi], ((0,), (0,)))

    for i in range(4):
        fetch[i].wait()
        attend_back(i)
        if i < 2:
            fetch.append(load(probs_all.at[:, 256 * i + 512 : 256 * i + 768], probs.at[i]))
        if i == 1:
            step(sums)
        if i == 2:
            step(downs)
        if i == 3:
            step(out_sum)
    grad_proj[:, PART : 2 * PART] = (grad_k[...] * head_scale).astype(LOW)
    grad_proj[:, 2 * PART :] = grad_v[...].astype(LOW)

    def norm_terms(col):
        rows = grad_proj[columns_of(col, 512), :]

        def piece(s, carry):
            weight = wa[s, :, :, 0:PROJ].reshape(256, PROJ)
            terms = dot(rows, weight, ((1,), (1,)))
            part[pl.ds(col * 4, 4), :, columns_of(s)] = terms.reshape(4, ROWS, 256).astype(LOW)
            return carry

        lax.fori_loop(0, 8, piece, 0)

    def product(s, out):
        terms = dot(ones_t[s], grad_proj[...])
        out[:, :, :, 0:PROJ] = terms.reshape(8, 2, 16, PROJ).astype(LOW)
        rows = grads[:, :, columns_of(s)].reshape(8 * ROWS, 256)
        out[:, :, :, PROJ:] = dot(att_t[...], rows).reshape(8, 2, 16, PART).astype(LOW)

    twin = twin_sum(me, mail, stage_a, acc_a, order, product)
    norm_terms(me.b)
    step(grad_sum)
    norm_terms(me.a)
    step(grad_sum)
    step(twin, 3)
    step(grad_sum)
    step(downs)
    step(sums)
    step(twin, 3)
    step(grad_sum)
    step(sums)
    step(twin, 3)

    def proj_sums():
        yield from scatter_hz(me, mail, acc_a, az_over, az_near, h_near)
        own = acc_a.at[:, me.z * 2 + me.h]
        yield from send_seq(me, mail, own, in_own, 0, PROJ)

    rest = proj_sums()
    step(rest)
    run(grad_sum, sums, rest)
    own = acc_a.at[:, me.z * 2 + me.h]
    gain = column(gain_one)
    sum_one = jnp.zeros((16, 1), WIDE)
    run(beside(sums, rest), out_sum, downs)
    units = mlp_ref.shape[2] // 4
    spare = jnp.zeros((16, mlp_ref.shape[2] - UNITS), WIDE)
    gain_mlp = column(gain_two)
    sum_two = jnp.zeros((16, 1), WIDE)
    for slot in range(3):
        whole = None
        for src in range(4):
            if slot == 2:
                piece = down_own[src].astype(WIDE)
            else:
                firsts = [(2 * tile + slot) * 128 for tile in range(UNITS // 128)]
                piece = jnp.concatenate([pair_own[src, :, f : f + 128].astype(WIDE) for f in firsts], axis=1)
            piece = jnp.concatenate([piece, spare], axis=1)
            whole = piece if src == 0 else whole + pltpu.roll(piece, src * units, 1)
        if slot < 2:
            sum_two = sum_two + jnp.sum(whole * mlp_ref[:, slot, :].astype(WIDE), axis=1, keepdims=True)
            whole = whole * gain_mlp
        mlp_grad[:, slot, :] = whole
    run(rest)
    for slot in range(4):
        if slot < 3:
            pieces = [in_own[src, :, slot * PART : slot * PART + PART] for src in range(8)]
        else:
            pieces = [own[k, :, PROJ:] for k in range(8)]
        whole = jnp.concatenate([piece.astype(WIDE) for piece in pieces], axis=1)
        if slot < 3:
            sum_one = sum_one + jnp.sum(whole * attn_ref[:, slot, :].astype(WIDE), axis=1, keepdims=True)
            whole = whole * gain
        attn_grad[:, slot, :] = whole
    gain_grads[:, 0:128] = jnp.broadcast_to(sum_one, (16, 128))
    gain_grads[:, 128:256] = jnp.broadcast_to(sum_two, (16, 128))
    mail.finish()


def back(grad_resid, x, counts, resid, attn_weight, mlp_weight, gain_one, gain_two, down, grads, branch, acc, ones, wa, qkv, probs, att):
    vmem, anywhere = pl.BlockSpec(memory_space=pltpu.VMEM), pl.BlockSpec(memory_space=pl.ANY)
    shape = jax.ShapeDtypeStruct
    count = 9 + 18 + 3 + 6 + 23 + 8 + 13 + 7
    return pl.pallas_call(
        back_kernel,
        out_shape=(
            shape((ROWS, MODEL), LOW), shape((ROWS, MODEL), WIDE), shape(attn_weight.shape, WIDE),
            shape(mlp_weight.shape, WIDE), shape((16, 256), WIDE),
        ),
        in_specs=[vmem] * 2 + [pl.BlockSpec(memory_space=pltpu.SMEM)] + [vmem] * 5 + [anywhere] * 9,
        out_specs=(vmem,) * 5,
        scratch_shapes=[
            pltpu.VMEM((4, 4, 16, UNITS), LOW), pltpu.VMEM((2, 2, 16, UNITS), LOW), pltpu.VMEM((2, 4, 16, UNITS), LOW),
            pltpu.VMEM((4, 16, UNITS), LOW), pltpu.VMEM((4, 16, PAIR), LOW), pltpu.VMEM((8, 16, PROJ), LOW), pltpu.VMEM((8, 8, 16, PAIR), LOW), pltpu.VMEM((2, 2, 2, 16, PAIR), LOW), pltpu.VMEM((2, 2, 4, 16, PAIR), LOW),
            pltpu.VMEM((2, 2, 16, PAIR), LOW), pltpu.VMEM((2, 4, 16, PAIR), LOW), pltpu.VMEM((8, ROWS, MODEL), LOW),
            pltpu.VMEM((4, ROWS, MODEL), LOW), pltpu.VMEM((2, ROWS, MID), LOW), pltpu.VMEM((2, ROWS, MODEL), LOW),
            pltpu.VMEM((8, ROWS, MODEL), LOW),
        ]
        + scatter_bufs()
        + [
            pltpu.VMEM((8, 16, 16, 1024), LOW), pltpu.VMEM((8, 8, 16, 1024), LOW), pltpu.VMEM((2, 2, 4, 16, 1024), LOW),
            pltpu.VMEM((2, 2, 8, 16, 1024), LOW), pltpu.VMEM((8, 16, 1024), LOW),
            pltpu.VMEM((8, 256, 1024), LOW),
            pltpu.VMEM((1024, PROJ), LOW), pltpu.VMEM((2, 2, 256, 1024), LOW), pltpu.VMEM((PART, 1024), LOW),
            pltpu.VMEM((1024, PART), LOW), pltpu.VMEM((1024, PROJ), LOW),
            pltpu.VMEM((1024, PART), WIDE), pltpu.VMEM((1024, PART), WIDE), pltpu.VMEM((2, 8, 2, 16, 1024), LOW),
            pltpu.SemaphoreType.DMA((count,)), pltpu.SemaphoreType.DMA((count,)), pltpu.SemaphoreType.DMA((14,)),
        ],
        compiler_params=pltpu.CompilerParams(collective_id=3, has_side_effects=True, vmem_limit_bytes=62 * 2**20),
        name="back",
    )(grad_resid, x, counts, resid, attn_weight, mlp_weight, gain_one, gain_two, down, grads, branch, acc, ones, wa, qkv, probs, att)
def local(
    tokens, valid_counts, block_owner, norm1_gain, attn_weight, norm2_gain, mlp_weight, cotangent
):
    x, cot = tokens[0], cotangent[0]
    gain_one, gain_two = norm1_gain[None], norm2_gain[None]
    ones, wa, grads, wm, qkv, probs, att, twos, resid = front(
        x, valid_counts, block_owner, cot, attn_weight, mlp_weight, gain_one, gain_two
    )
    acc, branch, branch_grads, grad_resid, down = mlp(resid, cot, valid_counts, twos, grads, wm)
    layer_out, input_grad, attn_grad, mlp_grad, gain_grads = back(
        grad_resid, x, valid_counts, resid, attn_weight, mlp_weight, gain_one, gain_two, down,
        branch_grads, branch, acc, ones, wa, qkv, probs, att,
    )
    return (layer_out[None], input_grad[None], gain_grads[:, 0], attn_grad, gain_grads[:, 128], mlp_grad)


def solution(mesh):
    token_spec = P("dp", "seq", None)
    row_spec = P(("seq", "dp"), None, None)
    gain_spec = P(("seq", "dp"))
    in_specs = (
        token_spec, P("dp", "seq"), P("dp", None), gain_spec, row_spec, gain_spec, row_spec, token_spec
    )
    out_specs = (token_spec, token_spec, gain_spec, row_spec, gain_spec, row_spec)
    return jax.shard_map(local, mesh=mesh, in_specs=in_specs, out_specs=out_specs, check_vma=False)
```
